32 devices in a mesh: rows: 8 (over y, x, core), chan: 4 (over z).
Axes of the slice: x: 2, y: 2, z: 4, core: 2. Of those that a mesh axis runs over, the one named last changes fastest.
Arguments:
- frame_adjoint: bfloat16 [8, 192, 8, 128], P('rows', 'chan'), may hold values from -6 to 6
- frame_slot: int32 [8], replicated, may hold values from 0 to 7, each once
- inputs: bfloat16 [8, 192, 8, 128], P(None, 'chan', 'rows')
- gain: float32 [192], P('chan'), may hold values from 0.1 to 1.9
- weight: bfloat16 [27, 192, 192], P(None, 'chan'), may hold values from -0.078125 to 0.078125
Outputs:
- input_adjoint: bfloat16 [8, 192, 8, 128], P(None, 'chan', 'rows')
- weight_adjoint: float32 [27, 192, 192], P(None, 'chan')
The draws below stay inside these ranges and needn't reach their ends.
Inputs may be any that keep to these rules, and one draw needn't show every extreme that they name: `frame_slot`: each frame appears in exactly one slot.
All inputs are finite; a program needn't handle non-finite values.
Results may differ from the reference program's by a relative error of at most 0.003.
Values may be sent and summed in bfloat16 or wider, within the bound.
No kernel may reach another device: no remote copies, remote signals or barrier semaphores. Data moves between devices by JAX's collectives and lax.ppermute only.
A program may use at most 128 MiB of HBM per device.

```python
import math
import jax
import jax.numpy as jnp
from jax import lax

CHANNELS = 192
TAPS = 27
WIDTH = 128
FRAMES = 8
HEIGHT = 8


def draw_inputs(key, part):
    key = jax.random.fold_in(key, 11)
    first, second, third = jax.random.split(key, 3)
    shape = (FRAMES, CHANNELS, HEIGHT, WIDTH)
    base = jax.random.normal(first, shape, jnp.float32)
    rising = jnp.exp(math.log(3.0) * jnp.arange(CHANNELS, dtype=jnp.float32) / CHANNELS)
    spread = jnp.exp(jax.random.uniform(second, (CHANNELS,), jnp.float32, 0.0, math.log(10.0)))
    pixel = jnp.exp(jax.random.uniform(third, (FRAMES, 1, HEIGHT, WIDTH), jnp.float32, 0.0, math.log(10.0)))
    values = base * (rising * spread)[None, :, None, None] * pixel * 0.3
    return values.astype(jnp.bfloat16)


def block_scale(key, dims, cuts, low, top_value):
    loudness = 1.0
    for dim, shards_of in cuts:
        heights = jax.random.uniform(jax.random.fold_in(jax.random.fold_in(key, 6), dim), (shards_of,), jnp.float32, low / len(cuts), top_value / len(cuts))
        loudness = loudness * jnp.repeat(jnp.exp(heights), dims[dim] // shards_of).reshape((-1,) + (1,) * (len(dims) - 1 - dim))
    return loudness


def gaussian(own_key, extent, scale, most, shards=(), kind=jnp.bfloat16):
    factor_of = block_scale(own_key, extent, shards, -0.22, 0.18) if shards else 1.0
    values = jax.random.normal(own_key, extent, jnp.float32) * scale * factor_of
    return jnp.minimum(jnp.maximum(values, -most), most).astype(kind)


def setup_inputs(seed: int = 0) -> dict:
    key_of = jax.random.split(jax.random.key(seed), 6)
    return {
        "frame_adjoint": gaussian(key_of[0], (FRAMES, CHANNELS, HEIGHT, WIDTH), 1.0, 6.0, ((0, 8), (1, 4))),
        "frame_slot": jax.random.permutation(key_of[1], FRAMES).astype(jnp.int32),
        "inputs": draw_inputs(jax.random.fold_in(key_of[5], 71), 0),
        "gain": jnp.clip(1.0 + 0.18 * jax.random.normal(key_of[3], (CHANNELS,), jnp.float32), 0.1, 1.9),
        "weight": gaussian(key_of[4], (TAPS, CHANNELS, CHANNELS), (TAPS * CHANNELS) ** -0.5, 0.078125, ((1, 4),)),
    }


epsilon = 1e-06

def reference(frame_adjoint, frame_slot, inputs, gain, weight):
    onehot = (frame_slot[None, :] == jnp.arange(FRAMES, dtype=jnp.int32)[:, None]).astype(jnp.float32)
    adjoint = jnp.einsum('tj,jcrw->tcrw', onehot, frame_adjoint.astype(jnp.float32))
    values = inputs.astype(jnp.float32)
    scale = lax.rsqrt(lax.optimization_barrier(jnp.sum(values * values, axis=1)) / CHANNELS + epsilon)[:, None]
    normed = values * scale * gain[None, :, None, None]
    sigma = jax.nn.sigmoid(normed)
    hidden = (normed * sigma).astype(jnp.bfloat16).astype(jnp.float32)
    hidden_pad = jnp.pad(hidden, ((2, 0), (0, 0), (1, 1), (1, 1)))
    adjoint_pad = jnp.pad(adjoint, ((0, 2), (0, 0), (1, 1), (1, 1)))
    kernel = weight.astype(jnp.float32)
    hidden_adjoint = jnp.zeros(values.shape, jnp.float32)
    grad_list = []
    for frame_off in range(3):
        for row_off in range(3):
            for col_off in range(3):
                index = frame_off * 9 + row_off * 3 + col_off
                window = adjoint_pad[2 - frame_off:2 - frame_off + FRAMES, :, 2 - row_off:2 - row_off + HEIGHT, 2 - col_off:2 - col_off + WIDTH]
                hidden_adjoint = hidden_adjoint + jnp.einsum('forw,oc->fcrw', window, kernel[index])
                source = hidden_pad[frame_off:frame_off + FRAMES, :, row_off:row_off + HEIGHT, col_off:col_off + WIDTH]
                grad_list.append(jnp.einsum('forw,fcrw->oc', adjoint, source))
    weight_adjoint = jnp.stack(grad_list) * float(FRAMES * HEIGHT * WIDTH) ** (-0.5)
    normed_adjoint = hidden_adjoint * sigma * (1.0 + normed * (1.0 - sigma)) * gain[None, :, None, None]
    projection = lax.optimization_barrier(jnp.sum(normed_adjoint * values, axis=1))[:, None]
    input_adjoint = scale * normed_adjoint - values * scale * scale * scale * projection / CHANNELS
    return (input_adjoint.astype(jnp.bfloat16), weight_adjoint)
```

```python
import functools

import jax
import jax.numpy as jnp
from jax import lax
from jax.experimental import pallas as pl
from jax.experimental.pallas import tpu as pltpu
from jax.sharding import PartitionSpec as P

CHANNELS = 192
EPSILON = 1e-06
MIB = 1024 * 1024


def round_up(value, unit):
    return -(-value // unit) * unit


def packing(taps_out, ins, count):
    blocks, rest = divmod(ins, 128)
    half = round_up(-(-taps_out // 2), 16) if rest else 0
    return blocks, rest, half, round_up(blocks * taps_out + half, 16 * count)


def vmem():
    return pl.BlockSpec(memory_space=pltpu.VMEM)


def smem():
    return pl.BlockSpec(memory_space=pltpu.SMEM)


def limit(taps_out, pixels):
    return pltpu.CompilerParams(vmem_limit_bytes=10 * MIB + 6 * taps_out * pixels)


def cost(rows, columns, depth):
    return pl.CostEstimate(
        flops=2 * rows * columns * depth,
        bytes_accessed=2 * (rows * depth + columns * depth),
        transcendentals=columns * depth,
    )


def gains(x_refs, start, group):
    found = []
    for ref in x_refs:
        rows = ref[pl.ds(start, 16), :].astype(jnp.float32)
        gain = rows[0:1] + rows[1:2] + rows[2:3]
        found.append(jnp.transpose(jnp.broadcast_to(gain, (128, 128)))[:group])
    return found


def norm(x_refs, t, group):
    values = [ref[pl.ds(t * group, group), :].astype(jnp.float32) for ref in x_refs]
    squares = sum(jnp.sum(value * value, axis=0, keepdims=True) for value in values)
    scale = lax.rsqrt(squares / CHANNELS + EPSILON)
    return scale, [value * scale for value in values]


def prepare_kernel(adjoint_ref, x_ref, gain_ref, strips_ref, payload_ref, lines, gain_rows):
    channels, height, width = adjoint_ref.shape
    frames = x_ref.shape[0]
    group = strips_ref.shape[2]
    lines[...] = adjoint_ref[...].astype(jnp.float32).reshape(channels * height, width)
    nothing = jnp.zeros((group, width), jnp.bfloat16)
    strips_ref[0, 0] = nothing
    strips_ref[height - 1, 2] = nothing
    for r in range(height):
        row = lines[pl.ds(r, channels, stride=height), :]
        if group > channels:
            row = jnp.concatenate(
                [row, jnp.zeros((group - channels, width), jnp.float32)], axis=0
            )
        row = row.astype(jnp.bfloat16)
        for k in range(3):
            if 0 <= r + 1 - k < height:
                strips_ref[r + 1 - k, k] = row
    for t in range(frames):
        values = x_ref[t]
        if group > channels:
            values = jnp.concatenate(
                [
                    values.astype(jnp.float32),
                    jnp.zeros((group - channels, width), jnp.float32),
                ],
                axis=0,
            ).astype(jnp.bfloat16)
        payload_ref[pl.ds(t * group, group), :] = values
    gain = gain_ref[...]
    high = gain.astype(jnp.bfloat16).astype(jnp.float32)
    middle = (gain - high).astype(jnp.bfloat16).astype(jnp.float32)
    gain_rows[...] = jnp.zeros_like(gain_rows)
    gain_rows[pl.ds(0, 1), pl.ds(0, channels)] = high
    gain_rows[pl.ds(1, 1), pl.ds(0, channels)] = middle
    gain_rows[pl.ds(2, 1), pl.ds(0, channels)] = gain - high - middle
    payload_ref[pl.ds(frames * group, 16), :] = gain_rows[...].astype(jnp.bfloat16)


def window_kernel(frames, group, slot_ref, adjoint_ref, windows, place):
    width = adjoint_ref.shape[-1]
    for slot in range(frames):
        place[slot_ref[slot]] = slot

    lane = lax.broadcasted_iota(jnp.int32, (group, width), 1)
    nothing = jnp.zeros((group, width), jnp.bfloat16)
    for a in range(2):
        for inner in range(9):
            for t in range(frames - 2 + a, frames):
                windows[pl.ds((a * 9 + inner) * group, group), pl.ds(t * width, width)] = nothing
    for frame in range(frames):
        slot = place[frame]
        for b in range(3):
            row = adjoint_ref[slot, 2 - b].astype(jnp.float32)
            after = jnp.where(lane == width - 1, 0.0, pltpu.roll(row, width - 1, 1))
            before = jnp.where(lane == 0, 0.0, pltpu.roll(row, 1, 1))
            for c, shifted in enumerate((after, row, before)):
                shifted = shifted.astype(jnp.bfloat16)
                for a in range(3):
                    t = frame + a - 2
                    if t >= 0:
                        windows[
                            pl.ds((a * 9 + b * 3 + c) * group, group), pl.ds(t * width, width)
                        ] = shifted

def grad_kernel(frames, group, factor, at_ref, windows, *refs):
    groups = len(refs) - 2
    x_refs = refs[:groups]
    grad_ref, hidden = refs[groups:]
    ins = groups * group
    width = windows.shape[1] // frames
    gain = gains(x_refs, frames * group, group)
    for t in range(frames):
        scale, scaled = norm(x_refs, t, group)
        for s in range(groups):
            normed = scaled[s] * gain[s]
            value = (normed * jax.nn.sigmoid(normed)).astype(jnp.bfloat16)
            start = pl.multiple_of(lax.rem(at_ref[0] + groups - s, groups) * group, 16)
            hidden[pl.ds(start, group), pl.ds(t * width, width)] = value

    grad = lax.dot_general(
        windows[...], hidden[...], (((1,), (1,)), ((), ())), preferred_element_type=jnp.float32
    )
    grad = grad * factor
    taps_out = grad.shape[0]
    blocks, rest, half, rows = packing(taps_out, ins, 1)
    for block in range(blocks):
        grad_ref[pl.ds(block * taps_out, taps_out), :] = grad[
            :, block * 128 : block * 128 + 128
        ].astype(jnp.bfloat16)
    base = blocks * taps_out
    if rest:
        left = grad[:half, blocks * 128 :]
        right = grad[half:, blocks * 128 :]
        right = jnp.concatenate(
            [right, jnp.zeros((2 * half - taps_out, rest), jnp.float32)], axis=0
        )
        grad_ref[pl.ds(base, half), :] = jnp.concatenate([left, right], axis=1).astype(
            jnp.bfloat16
        )
        base = base + half
    tail = grad_ref.shape[0] - base
    if tail:
        grad_ref[pl.ds(base, tail), :] = jnp.zeros((tail, 128), jnp.bfloat16)


def part_kernel(frames, group, at_ref, weight_ref, windows, *refs):
    groups = (len(refs) - 3) // 2
    x_refs = refs[:groups]
    part_refs = refs[groups : 2 * groups]
    scale_ref, own_share_ref, product = refs[2 * groups :]
    width = scale_ref.shape[-1]
    product[...] = jnp.dot(weight_ref[...], windows[...], preferred_element_type=jnp.float32)
    gain = gains(x_refs, frames * group, group)
    shares = []
    for t in range(frames):
        scale, scaled = norm(x_refs, t, group)
        scale_ref[pl.ds(t, 1), :] = scale
        share = jnp.zeros((1, width), jnp.float32)
        for s in range(groups):
            normed = scaled[s] * gain[s]
            sigma = jax.nn.sigmoid(normed)
            slope = sigma * (1.0 + normed * (1.0 - sigma)) * gain[s]
            start = pl.multiple_of(lax.rem(at_ref[0] + groups - s, groups) * group, 16)
            term = product[pl.ds(start, group), pl.ds(t * width, width)] * slope * scale
            part_refs[s][pl.ds(t * group, group), :] = term.astype(part_refs[s].dtype)
            share = share + jnp.sum(term * scaled[s], axis=0, keepdims=True)
        shares.append(share)
    share = jnp.concatenate(shares, axis=0)
    own_share_ref[...] = share
    high = share.astype(jnp.bfloat16).astype(jnp.float32)
    both = [high, share - high]
    unused = round_up(2 * frames, 16) - 2 * frames
    if unused:
        both.append(jnp.zeros((unused, width), jnp.float32))
    both = jnp.concatenate(both, axis=0).astype(jnp.bfloat16)
    for s in range(1, groups):
        part_refs[s][pl.ds(frames * group, both.shape[0]), :] = both


def finish_kernel(frames, group, packed_ref, x_ref, scale_ref, share_ref, *refs):
    own_ref, others, (out_ref, grad_ref) = refs[0], refs[1:-2], refs[-2:]
    taps_out, ins = grad_ref.shape
    blocks, rest, half, rows = packing(taps_out, ins, 1)
    for block in range(blocks):
        grad_ref[:, pl.ds(block * 128, 128)] = packed_ref[
            pl.ds(block * taps_out, taps_out), :
        ].astype(jnp.float32)
    if rest:
        both = packed_ref[pl.ds(blocks * taps_out, half), :].astype(jnp.float32)
        grad_ref[pl.ds(0, half), pl.ds(blocks * 128, rest)] = both[:, :rest]
        grad_ref[pl.ds(half, taps_out - half), pl.ds(blocks * 128, rest)] = both[
            : taps_out - half, rest:
        ]

    share = share_ref[...]
    for ref in others:
        both = ref[pl.ds(frames * group, round_up(2 * frames, 16)), :].astype(jnp.float32)
        share = share + both[:frames] + both[frames : 2 * frames]
    share = share / CHANNELS
    for t in range(frames):
        term = own_ref[pl.ds(t * group, group), :]
        for ref in others:
            term = term + ref[pl.ds(t * group, group), :].astype(jnp.float32)
        scaled = x_ref[pl.ds(t * group, group), :].astype(jnp.float32) * scale_ref[pl.ds(t, 1), :]
        out_ref[t] = (term - scaled * share[t : t + 1]).astype(jnp.bfloat16)


def shards(frame_adjoint, frame_slot, inputs, gain, weight):
    count = lax.axis_size("rows")
    groups = lax.axis_size("chan")
    frames, channels, _, width = inputs.shape
    group = round_up(channels, 16)
    spare = group - channels
    ins = groups * group

    taps_out = 27 * group
    pixels = frames * width
    strips, payload = pl.pallas_call(
        prepare_kernel,
        out_shape=(
            jax.ShapeDtypeStruct((count, 3, group, width), jnp.bfloat16),
            jax.ShapeDtypeStruct((frames * group + 16, width), jnp.bfloat16),
        ),
        in_specs=[vmem(), vmem(), vmem()],
        out_specs=(vmem(), vmem()),
        scratch_shapes=[
            pltpu.VMEM((channels * count, width), jnp.float32),
            pltpu.VMEM((16, width), jnp.float32),
        ],
        compiler_params=limit(taps_out, pixels),
        name="prepare_kernel",
    )(frame_adjoint[0], inputs[:, :, 0], gain.reshape(1, channels))
    strips = lax.all_to_all(strips, "rows", split_axis=0, concat_axis=0, tiled=True)

    shifts = [[(z, (z + s) % groups) for z in range(groups)] for s in range(groups)]
    everything = [payload] + [lax.ppermute(payload, "chan", shifts[s]) for s in range(1, groups)]
    at = lax.axis_index("chan").astype(jnp.int32).reshape(1)

    kernel = weight.reshape(27, channels, groups, channels)
    kernel = jnp.pad(kernel, ((0, 0), (0, spare), (0, 0), (0, spare)))
    kernel = kernel.reshape(27 * group, ins).T

    packed_rows = packing(taps_out, ins, count)[3]
    factor = float(frames * count * width) ** (-0.5)
    windows = pl.pallas_call(
        functools.partial(window_kernel, frames, group),
        out_shape=jax.ShapeDtypeStruct((taps_out, pixels), jnp.bfloat16),
        in_specs=[smem(), vmem()],
        out_specs=vmem(),
        scratch_shapes=[pltpu.SMEM((frames,), jnp.int32)],
        compiler_params=limit(taps_out, pixels),
        name="window_kernel",
    )(frame_slot, strips)
    packed = pl.pallas_call(
        functools.partial(grad_kernel, frames, group, factor),
        out_shape=jax.ShapeDtypeStruct((packed_rows, 128), jnp.bfloat16),
        in_specs=[smem(), vmem()] + [vmem()] * groups,
        out_specs=vmem(),
        scratch_shapes=[pltpu.VMEM((ins, pixels), jnp.bfloat16)],
        compiler_params=limit(taps_out, pixels),
        cost_estimate=cost(taps_out, ins, pixels),
        name="grad_kernel",
    )(at, windows, *everything)

    pieces = lax.all_to_all(
        packed.reshape(count, packed_rows // count, 128),
        "rows", split_axis=0, concat_axis=0, tiled=True,
    )

    sent = frames * group + round_up(2 * frames, 16)
    *parts, scale, share = pl.pallas_call(
        functools.partial(part_kernel, frames, group),
        out_shape=tuple(
            [jax.ShapeDtypeStruct((frames * group, width), jnp.float32)]
            + [jax.ShapeDtypeStruct((sent, width), jnp.bfloat16)] * (groups - 1)
            + [jax.ShapeDtypeStruct((frames, width), jnp.float32)] * 2
        ),
        in_specs=[smem(), vmem(), vmem()] + [vmem()] * groups,
        out_specs=(vmem(),) * (groups + 2),
        scratch_shapes=[pltpu.VMEM((ins, pixels), jnp.float32)],
        compiler_params=limit(taps_out, pixels),
        cost_estimate=cost(taps_out, ins, pixels),
        name="part_kernel",
    )(at, kernel, windows, *everything)

    arrived = [
        lax.ppermute(parts[s], "chan", shifts[groups - s]) for s in range(1, groups)
    ]
    summed = jnp.sum(pieces.astype(jnp.float32), axis=0).astype(jnp.bfloat16)
    whole = lax.all_gather(summed, "rows", axis=0, tiled=True)
    input_adjoint, grad = pl.pallas_call(
        functools.partial(finish_kernel, frames, group),
        out_shape=(
            jax.ShapeDtypeStruct((frames, group, width), jnp.bfloat16),
            jax.ShapeDtypeStruct((taps_out, ins), jnp.float32),
        ),
        in_specs=[vmem()] * (groups + 4),
        out_specs=(vmem(), vmem()),
        compiler_params=limit(taps_out, pixels),
        name="finish_kernel",
    )(whole, payload, scale, share, parts[0], *arrived)
    grad = grad.reshape(27, group, groups, group)[:, :channels, :, :channels]
    return (
        input_adjoint[:, :channels, None, :],
        grad.reshape(27, channels, groups * channels),
    )


def solution(mesh):
    in_specs = (
        P("rows", "chan", None, None),
        P(),
        P(None, "chan", "rows", None),
        P("chan"),
        P(None, "chan", None),
    )
    out_specs = (P(None, "chan", "rows", None), P(None, "chan", None))
    return jax.shard_map(shards, mesh=mesh, in_specs=in_specs, out_specs=out_specs, check_vma=False)
```

```python
import functools

import jax
import jax.numpy as jnp
from jax import lax
from jax.experimental import pallas as pl
from jax.experimental.pallas import tpu as pltpu
from jax.sharding import PartitionSpec as P

CHANNELS = 192
EPSILON = 1e-06
MIB = 1024 * 1024


def round_up(value, unit):
    return -(-value // unit) * unit


def packing(taps_out, ins, count):
    blocks, rest = divmod(ins, 128)
    half = round_up(-(-taps_out // 2), 16) if rest else 0
    return blocks, rest, half, round_up(blocks * taps_out + half, 16 * count)


def vmem():
    return pl.BlockSpec(memory_space=pltpu.VMEM)


def copied():
    return pl.BlockSpec()


def smem():
    return pl.BlockSpec(memory_space=pltpu.SMEM)


def limit(taps_out, pixels):
    return pltpu.CompilerParams(vmem_limit_bytes=10 * MIB + 6 * taps_out * pixels)


def cost(rows, columns, depth):
    return pl.CostEstimate(
        flops=2 * rows * columns * depth,
        bytes_accessed=2 * (rows * depth + columns * depth),
        transcendentals=columns * depth,
    )


def gains(x_refs, start, group):
    found = []
    for ref in x_refs:
        rows = ref[pl.ds(start, 16), :].astype(jnp.float32)
        gain = rows[0:1] + rows[1:2] + rows[2:3]
        found.append(jnp.transpose(jnp.broadcast_to(gain, (128, 128)))[:group])
    return found


def norm(x_refs, t, group):
    values = [ref[pl.ds(t * group, group), :].astype(jnp.float32) for ref in x_refs]
    squares = sum(jnp.sum(value * value, axis=0, keepdims=True) for value in values)
    scale = lax.rsqrt(squares / CHANNELS + EPSILON)
    return scale, [value * scale for value in values]


def prepare_kernel(adjoint_ref, x_ref, gain_ref, strips_ref, payload_ref, lines, gain_rows):
    channels, height, width = adjoint_ref.shape
    frames = x_ref.shape[0]
    group = strips_ref.shape[2]
    lines[...] = adjoint_ref[...].astype(jnp.float32).reshape(channels * height, width)
    nothing = jnp.zeros((group, width), jnp.bfloat16)
    strips_ref[0, 0] = nothing
    strips_ref[height - 1, 2] = nothing
    for r in range(height):
        row = lines[pl.ds(r, channels, stride=height), :]
        if group > channels:
            row = jnp.concatenate(
                [row, jnp.zeros((group - channels, width), jnp.float32)], axis=0
            )
        row = row.astype(jnp.bfloat16)
        for k in range(3):
            if 0 <= r + 1 - k < height:
                strips_ref[r + 1 - k, k] = row
    for t in range(frames):
        values = x_ref[t]
        if group > channels:
            values = jnp.concatenate(
                [
                    values.astype(jnp.float32),
                    jnp.zeros((group - channels, width), jnp.float32),
                ],
                axis=0,
            ).astype(jnp.bfloat16)
        payload_ref[pl.ds(t * group, group), :] = values
    gain = gain_ref[...]
    high = gain.astype(jnp.bfloat16).astype(jnp.float32)
    middle = (gain - high).astype(jnp.bfloat16).astype(jnp.float32)
    gain_rows[...] = jnp.zeros_like(gain_rows)
    gain_rows[pl.ds(0, 1), pl.ds(0, channels)] = high
    gain_rows[pl.ds(1, 1), pl.ds(0, channels)] = middle
    gain_rows[pl.ds(2, 1), pl.ds(0, channels)] = gain - high - middle
    payload_ref[pl.ds(frames * group, 16), :] = gain_rows[...].astype(jnp.bfloat16)


def window_kernel(frames, group, slot_ref, adjoint_ref, windows, place):
    width = adjoint_ref.shape[-1]
    for slot in range(frames):
        place[slot_ref[slot]] = slot

    lane = lax.broadcasted_iota(jnp.int32, (group, width), 1)
    nothing = jnp.zeros((group, width), jnp.bfloat16)
    for a in range(2):
        for inner in range(9):
            for t in range(frames - 2 + a, frames):
                windows[pl.ds((a * 9 + inner) * group, group), pl.ds(t * width, width)] = nothing
    for frame in range(frames):
        slot = place[frame]
        for b in range(3):
            row = adjoint_ref[slot, 2 - b].astype(jnp.float32)
            after = jnp.where(lane == width - 1, 0.0, pltpu.roll(row, width - 1, 1))
            before = jnp.where(lane == 0, 0.0, pltpu.roll(row, 1, 1))
            for c, shifted in enumerate((after, row, before)):
                shifted = shifted.astype(jnp.bfloat16)
                for a in range(3):
                    t = frame + a - 2
                    if t >= 0:
                        windows[
                            pl.ds((a * 9 + b * 3 + c) * group, group), pl.ds(t * width, width)
                        ] = shifted

def grad_kernel(frames, group, factor, at_ref, windows, *refs):
    groups = len(refs) - 2
    x_refs = refs[:groups]
    grad_ref, hidden = refs[groups:]
    ins = groups * group
    width = windows.shape[1] // frames
    gain = gains(x_refs, frames * group, group)
    for t in range(frames):
        scale, scaled = norm(x_refs, t, group)
        for s in range(groups):
            normed = scaled[s] * gain[s]
            value = (normed * jax.nn.sigmoid(normed)).astype(jnp.bfloat16)
            start = pl.multiple_of(lax.rem(at_ref[0] + groups - s, groups) * group, 16)
            hidden[pl.ds(start, group), pl.ds(t * width, width)] = value

    grad = lax.dot_general(
        windows[...], hidden[...], (((1,), (1,)), ((), ())), preferred_element_type=jnp.float32
    )
    grad = grad * factor
    taps_out = grad.shape[0]
    blocks, rest, half, rows = packing(taps_out, ins, 1)
    for block in range(blocks):
        grad_ref[pl.ds(block * taps_out, taps_out), :] = grad[
            :, block * 128 : block * 128 + 128
        ].astype(jnp.bfloat16)
    base = blocks * taps_out
    if rest:
        left = grad[:half, blocks * 128 :]
        right = grad[half:, blocks * 128 :]
        right = jnp.concatenate(
            [right, jnp.zeros((2 * half - taps_out, rest), jnp.float32)], axis=0
        )
        grad_ref[pl.ds(base, half), :] = jnp.concatenate([left, right], axis=1).astype(
            jnp.bfloat16
        )
        base = base + half
    tail = grad_ref.shape[0] - base
    if tail:
        grad_ref[pl.ds(base, tail), :] = jnp.zeros((tail, 128), jnp.bfloat16)


def part_kernel(frames, group, at_ref, weight_ref, windows, *refs):
    groups = (len(refs) - 3) // 2
    x_refs = refs[:groups]
    part_refs = refs[groups : 2 * groups]
    scale_ref, own_share_ref, product = refs[2 * groups :]
    width = scale_ref.shape[-1]
    product[...] = jnp.dot(weight_ref[...], windows[...], preferred_element_type=jnp.float32)
    gain = gains(x_refs, frames * group, group)
    shares = []
    for t in range(frames):
        scale, scaled = norm(x_refs, t, group)
        scale_ref[pl.ds(t, 1), :] = scale
        share = jnp.zeros((1, width), jnp.float32)
        for s in range(groups):
            normed = scaled[s] * gain[s]
            sigma = jax.nn.sigmoid(normed)
            slope = sigma * (1.0 + normed * (1.0 - sigma)) * gain[s]
            start = pl.multiple_of(lax.rem(at_ref[0] + groups - s, groups) * group, 16)
            term = product[pl.ds(start, group), pl.ds(t * width, width)] * slope * scale
            part_refs[s][pl.ds(t * group, group), :] = term.astype(part_refs[s].dtype)
            share = share + jnp.sum(term * scaled[s], axis=0, keepdims=True)
        shares.append(share)
    share = jnp.concatenate(shares, axis=0)
    own_share_ref[...] = share
    high = share.astype(jnp.bfloat16).astype(jnp.float32)
    both = [high, share - high]
    unused = round_up(2 * frames, 16) - 2 * frames
    if unused:
        both.append(jnp.zeros((unused, width), jnp.float32))
    both = jnp.concatenate(both, axis=0).astype(jnp.bfloat16)
    for s in range(1, groups):
        part_refs[s][pl.ds(frames * group, both.shape[0]), :] = both


def finish_kernel(frames, group, packed_ref, x_ref, scale_ref, share_ref, *refs):
    own_ref, others, (out_ref, grad_ref) = refs[0], refs[1:-2], refs[-2:]
    taps_out, ins = grad_ref.shape
    blocks, rest, half, rows = packing(taps_out, ins, 1)
    for block in range(blocks):
        grad_ref[:, pl.ds(block * 128, 128)] = packed_ref[
            pl.ds(block * taps_out, taps_out), :
        ].astype(jnp.float32)
    if rest:
        both = packed_ref[pl.ds(blocks * taps_out, half), :].astype(jnp.float32)
        grad_ref[pl.ds(0, half), pl.ds(blocks * 128, rest)] = both[:, :rest]
        grad_ref[pl.ds(half, taps_out - half), pl.ds(blocks * 128, rest)] = both[
            : taps_out - half, rest:
        ]

    share = share_ref[...]
    for ref in others:
        both = ref[pl.ds(frames * group, round_up(2 * frames, 16)), :].astype(jnp.float32)
        share = share + both[:frames] + both[frames : 2 * frames]
    share = share / CHANNELS
    for t in range(frames):
        term = own_ref[pl.ds(t * group, group), :]
        for ref in others:
            term = term + ref[pl.ds(t * group, group), :].astype(jnp.float32)
        scaled = x_ref[pl.ds(t * group, group), :].astype(jnp.float32) * scale_ref[pl.ds(t, 1), :]
        out_ref[t] = (term - scaled * share[t : t + 1]).astype(jnp.bfloat16)


def shards(frame_adjoint, frame_slot, inputs, gain, weight):
    count = lax.axis_size("rows")
    groups = lax.axis_size("chan")
    frames, channels, _, width = inputs.shape
    group = round_up(channels, 16)
    spare = group - channels
    ins = groups * group

    taps_out = 27 * group
    pixels = frames * width
    strips, payload = pl.pallas_call(
        prepare_kernel,
        out_shape=(
            jax.ShapeDtypeStruct((count, 3, group, width), jnp.bfloat16),
            jax.ShapeDtypeStruct((frames * group + 16, width), jnp.bfloat16),
        ),
        in_specs=[copied(), copied(), copied()],
        out_specs=(vmem(), vmem()),
        scratch_shapes=[
            pltpu.VMEM((channels * count, width), jnp.float32),
            pltpu.VMEM((16, width), jnp.float32),
        ],
        compiler_params=pltpu.CompilerParams(vmem_limit_bytes=60 * MIB),
        name="prepare_kernel",
    )(frame_adjoint[0], inputs[:, :, 0], gain.reshape(1, channels))
    strips = lax.all_to_all(strips, "rows", split_axis=0, concat_axis=0, tiled=True)

    shifts = [[(z, (z + s) % groups) for z in range(groups)] for s in range(groups)]
    everything = [payload] * groups
    for s in range(1, groups // 2 + 1):
        everything[s] = lax.ppermute(everything[s - 1], "chan", shifts[1])
    for s in range(groups - 1, groups // 2, -1):
        everything[s] = lax.ppermute(everything[(s + 1) % groups], "chan", shifts[groups - 1])
    at = lax.axis_index("chan").astype(jnp.int32).reshape(1)

    kernel = weight.reshape(27, channels, groups, channels)
    kernel = jnp.pad(kernel, ((0, 0), (0, spare), (0, 0), (0, spare)))
    kernel = kernel.reshape(27 * group, ins).T

    packed_rows = packing(taps_out, ins, count)[3]
    factor = float(frames * count * width) ** (-0.5)
    windows = pl.pallas_call(
        functools.partial(window_kernel, frames, group),
        out_shape=jax.ShapeDtypeStruct((taps_out, pixels), jnp.bfloat16),
        in_specs=[smem(), copied()],
        out_specs=vmem(),
        scratch_shapes=[pltpu.SMEM((frames,), jnp.int32)],
        compiler_params=limit(taps_out, pixels),
        name="window_kernel",
    )(frame_slot, strips)
    packed = pl.pallas_call(
        functools.partial(grad_kernel, frames, group, factor),
        out_shape=jax.ShapeDtypeStruct((packed_rows, 128), jnp.bfloat16),
        in_specs=[smem(), vmem()] + [copied()] * groups,
        out_specs=vmem(),
        scratch_shapes=[pltpu.VMEM((ins, pixels), jnp.bfloat16)],
        compiler_params=limit(taps_out, pixels),
        cost_estimate=cost(taps_out, ins, pixels),
        name="grad_kernel",
    )(at, windows, *everything)

    pieces = lax.all_to_all(
        packed.reshape(count, packed_rows // count, 128),
        "rows", split_axis=0, concat_axis=0, tiled=True,
    )

    sent = frames * group + round_up(2 * frames, 16)
    *parts, scale, share = pl.pallas_call(
        functools.partial(part_kernel, frames, group),
        out_shape=tuple(
            [jax.ShapeDtypeStruct((frames * group, width), jnp.float32)]
            + [jax.ShapeDtypeStruct((sent, width), jnp.bfloat16)] * (groups - 1)
            + [jax.ShapeDtypeStruct((frames, width), jnp.float32)] * 2
        ),
        in_specs=[smem(), vmem(), vmem()] + [copied()] * groups,
        out_specs=(vmem(),) * (groups + 2),
        scratch_shapes=[pltpu.VMEM((ins, pixels), jnp.float32)],
        compiler_params=limit(taps_out, pixels),
        cost_estimate=cost(taps_out, ins, pixels),
        name="part_kernel",
    )(at, kernel, windows, *everything)

    arrived = [
        lax.ppermute(parts[s], "chan", shifts[groups - s]) for s in range(1, groups)
    ]
    summed = jnp.sum(pieces.astype(jnp.float32), axis=0).astype(jnp.bfloat16)
    whole = lax.all_gather(summed, "rows", axis=0, tiled=True)
    input_adjoint, grad = pl.pallas_call(
        functools.partial(finish_kernel, frames, group),
        out_shape=(
            jax.ShapeDtypeStruct((frames, group, width), jnp.bfloat16),
            jax.ShapeDtypeStruct((taps_out, ins), jnp.float32),
        ),
        in_specs=[copied()] * (groups + 4),
        out_specs=(vmem(), vmem()),
        compiler_params=limit(taps_out, pixels),
        name="finish_kernel",
    )(whole, payload, scale, share, parts[0], *arrived)
    grad = grad.reshape(27, group, groups, group)[:, :channels, :, :channels]
    return (
        input_adjoint[:, :channels, None, :],
        grad.reshape(27, channels, groups * channels),
    )


def solution(mesh):
    in_specs = (
        P("rows", "chan", None, None),
        P(),
        P(None, "chan", "rows", None),
        P("chan"),
        P(None, "chan", None),
    )
    out_specs = (P(None, "chan", "rows", None), P(None, "chan", None))
    return jax.shard_map(shards, mesh=mesh, in_specs=in_specs, out_specs=out_specs, check_vma=False)
```

```python
import functools

import jax
import jax.numpy as jnp
from jax import lax
from jax.experimental import pallas as pl
from jax.experimental.pallas import tpu as pltpu
from jax.sharding import PartitionSpec as P

CHANNELS = 192
EPSILON = 1e-06
MIB = 1024 * 1024


def round_up(value, unit):
    return -(-value // unit) * unit


def packing(taps_out, ins, count):
    blocks, rest = divmod(ins, 128)
    half = round_up(-(-taps_out // 2), 16) if rest else 0
    return blocks, rest, half, round_up(blocks * taps_out + half, 16 * count)


def vmem():
    return pl.BlockSpec(memory_space=pltpu.VMEM)


def copied():
    return pl.BlockSpec()


def anywhere():
    return pl.BlockSpec(memory_space=pl.ANY)


def smem():
    return pl.BlockSpec(memory_space=pltpu.SMEM)


def limit(taps_out, pixels):
    return pltpu.CompilerParams(vmem_limit_bytes=10 * MIB + 6 * taps_out * pixels)


def cost(rows, columns, depth):
    return pl.CostEstimate(
        flops=2 * rows * columns * depth,
        bytes_accessed=2 * (rows * depth + columns * depth),
        transcendentals=columns * depth,
    )


def gains(x_refs, start, group):
    found = []
    for ref in x_refs:
        rows = ref[pl.ds(start, 16), :].astype(jnp.float32)
        gain = rows[0:1] + rows[1:2] + rows[2:3]
        found.append(jnp.transpose(jnp.broadcast_to(gain, (128, 128)))[:group])
    return found


def norm(x_refs, t, group):
    values = [ref[pl.ds(t * group, group), :].astype(jnp.float32) for ref in x_refs]
    squares = sum(jnp.sum(value * value, axis=0, keepdims=True) for value in values)
    scale = lax.rsqrt(squares / CHANNELS + EPSILON)
    return scale, [value * scale for value in values]


def prepare_kernel(adjoint_ref, x_ref, gain_ref, strips_ref, payload_ref, lines, gain_rows):
    channels, height, width = adjoint_ref.shape
    frames = x_ref.shape[0]
    group = strips_ref.shape[2]
    lines[...] = adjoint_ref[...].astype(jnp.float32).reshape(channels * height, width)
    nothing = jnp.zeros((group, width), jnp.bfloat16)
    strips_ref[0, 0] = nothing
    strips_ref[height - 1, 2] = nothing
    for r in range(height):
        row = lines[pl.ds(r, channels, stride=height), :]
        if group > channels:
            row = jnp.concatenate(
                [row, jnp.zeros((group - channels, width), jnp.float32)], axis=0
            )
        row = row.astype(jnp.bfloat16)
        for k in range(3):
            if 0 <= r + 1 - k < height:
                strips_ref[r + 1 - k, k] = row
    for t in range(frames):
        values = x_ref[t]
        if group > channels:
            values = jnp.concatenate(
                [
                    values.astype(jnp.float32),
                    jnp.zeros((group - channels, width), jnp.float32),
                ],
                axis=0,
            ).astype(jnp.bfloat16)
        payload_ref[pl.ds(t * group, group), :] = values
    gain = gain_ref[...]
    high = gain.astype(jnp.bfloat16).astype(jnp.float32)
    middle = (gain - high).astype(jnp.bfloat16).astype(jnp.float32)
    gain_rows[...] = jnp.zeros_like(gain_rows)
    gain_rows[pl.ds(0, 1), pl.ds(0, channels)] = high
    gain_rows[pl.ds(1, 1), pl.ds(0, channels)] = middle
    gain_rows[pl.ds(2, 1), pl.ds(0, channels)] = gain - high - middle
    payload_ref[pl.ds(frames * group, 16), :] = gain_rows[...].astype(jnp.bfloat16)


def after_kernel(strips_ref, arrived_ref, out_ref):
    pass


def window_kernel(frames, group, slot_ref, adjoint_ref, windows, place):
    width = adjoint_ref.shape[-1]
    for slot in range(frames):
        place[slot_ref[slot]] = slot

    lane = lax.broadcasted_iota(jnp.int32, (group, width), 1)
    nothing = jnp.zeros((group, width), jnp.bfloat16)
    for a in range(2):
        for inner in range(9):
            for t in range(frames - 2 + a, frames):
                windows[pl.ds((a * 9 + inner) * group, group), pl.ds(t * width, width)] = nothing
    for frame in range(frames):
        slot = place[frame]
        for b in range(3):
            row = adjoint_ref[slot, 2 - b].astype(jnp.float32)
            after = jnp.where(lane == width - 1, 0.0, pltpu.roll(row, width - 1, 1))
            before = jnp.where(lane == 0, 0.0, pltpu.roll(row, 1, 1))
            for c, shifted in enumerate((after, row, before)):
                shifted = shifted.astype(jnp.bfloat16)
                for a in range(3):
                    t = frame + a - 2
                    if t >= 0:
                        windows[
                            pl.ds((a * 9 + b * 3 + c) * group, group), pl.ds(t * width, width)
                        ] = shifted

def grad_kernel(frames, group, factor, at_ref, windows, *refs):
    groups = len(refs) - 2
    x_refs = refs[:groups]
    grad_ref, hidden = refs[groups:]
    ins = groups * group
    width = windows.shape[1] // frames
    gain = gains(x_refs, frames * group, group)
    for t in range(frames):
        scale, scaled = norm(x_refs, t, group)
        for s in range(groups):
            normed = scaled[s] * gain[s]
            value = (normed * jax.nn.sigmoid(normed)).astype(jnp.bfloat16)
            start = pl.multiple_of((at_ref[0] ^ s) * group, 16)
            hidden[pl.ds(start, group), pl.ds(t * width, width)] = value

    grad = lax.dot_general(
        windows[...], hidden[...], (((1,), (1,)), ((), ())), preferred_element_type=jnp.float32
    )
    grad = grad * factor
    taps_out = grad.shape[0]
    blocks, rest, half, rows = packing(taps_out, ins, 1)
    for block in range(blocks):
        grad_ref[pl.ds(block * taps_out, taps_out), :] = grad[
            :, block * 128 : block * 128 + 128
        ].astype(jnp.bfloat16)
    base = blocks * taps_out
    if rest:
        left = grad[:half, blocks * 128 :]
        right = grad[half:, blocks * 128 :]
        right = jnp.concatenate(
            [right, jnp.zeros((2 * half - taps_out, rest), jnp.float32)], axis=0
        )
        grad_ref[pl.ds(base, half), :] = jnp.concatenate([left, right], axis=1).astype(
            jnp.bfloat16
        )
        base = base + half
    tail = grad_ref.shape[0] - base
    if tail:
        grad_ref[pl.ds(base, tail), :] = jnp.zeros((tail, 128), jnp.bfloat16)


def part_kernel(frames, group, at_ref, weight_ref, windows, *refs):
    groups = (len(refs) - 1) // 2
    x_refs = refs[:groups]
    part_refs = refs[groups : 2 * groups]
    product = refs[2 * groups]
    width = part_refs[0].shape[-1]
    product[...] = lax.dot_general(
        weight_ref[...], windows[...], (((0,), (0,)), ((), ())), preferred_element_type=jnp.float32
    )
    gain = gains(x_refs, frames * group, group)
    shares = []
    for t in range(frames):
        scale, scaled = norm(x_refs, t, group)
        part_refs[0][pl.ds(frames * group + t, 1), :] = scale
        share = jnp.zeros((1, width), jnp.float32)
        for s in range(groups):
            normed = scaled[s] * gain[s]
            sigma = jax.nn.sigmoid(normed)
            slope = sigma * (1.0 + normed * (1.0 - sigma)) * gain[s]
            start = pl.multiple_of((at_ref[0] ^ s) * group, 16)
            term = product[pl.ds(start, group), pl.ds(t * width, width)] * slope * scale
            part_refs[s][pl.ds(t * group, group), :] = term.astype(part_refs[s].dtype)
            share = share + jnp.sum(term * scaled[s], axis=0, keepdims=True)
        shares.append(share)
    share = jnp.concatenate(shares, axis=0)
    part_refs[0][pl.ds(frames * group + frames, frames), :] = share
    high = share.astype(jnp.bfloat16).astype(jnp.float32)
    both = [high, share - high]
    unused = round_up(2 * frames, 16) - 2 * frames
    if unused:
        both.append(jnp.zeros((unused, width), jnp.float32))
    both = jnp.concatenate(both, axis=0).astype(jnp.bfloat16)
    for s in range(1, groups):
        part_refs[s][pl.ds(frames * group, both.shape[0]), :] = both


def finish_kernel(frames, group, packed_ref, x_ref, *refs):
    own_ref, others, (out_ref, grad_ref) = refs[0], refs[1:-2], refs[-2:]
    taps_out, ins = grad_ref.shape
    blocks, rest, half, rows = packing(taps_out, ins, 1)
    for block in range(blocks):
        grad_ref[:, pl.ds(block * 128, 128)] = packed_ref[
            pl.ds(block * taps_out, taps_out), :
        ].astype(jnp.float32)
    if rest:
        both = packed_ref[pl.ds(blocks * taps_out, half), :].astype(jnp.float32)
        grad_ref[pl.ds(0, half), pl.ds(blocks * 128, rest)] = both[:, :rest]
        grad_ref[pl.ds(half, taps_out - half), pl.ds(blocks * 128, rest)] = both[
            : taps_out - half, rest:
        ]

    share = own_ref[pl.ds(frames * group + frames, frames), :]
    for ref in others:
        both = ref[pl.ds(frames * group, round_up(2 * frames, 16)), :].astype(jnp.float32)
        share = share + both[:frames] + both[frames : 2 * frames]
    share = share / CHANNELS
    for t in range(frames):
        term = own_ref[pl.ds(t * group, group), :]
        for ref in others:
            term = term + ref[pl.ds(t * group, group), :].astype(jnp.float32)
        scale = own_ref[pl.ds(frames * group + t, 1), :]
        scaled = x_ref[pl.ds(t * group, group), :].astype(jnp.float32) * scale
        out_ref[t] = (term - scaled * share[t : t + 1]).astype(jnp.bfloat16)


def shards(frame_adjoint, frame_slot, inputs, gain, weight):
    count = lax.axis_size("rows")
    groups = lax.axis_size("chan")
    frames, channels, _, width = inputs.shape
    group = round_up(channels, 16)
    spare = group - channels
    ins = groups * group

    taps_out = 27 * group
    pixels = frames * width
    strips, payload = pl.pallas_call(
        prepare_kernel,
        out_shape=(
            jax.ShapeDtypeStruct((count, 3, group, width), jnp.bfloat16),
            jax.ShapeDtypeStruct((frames * group + 16, width), jnp.bfloat16),
        ),
        in_specs=[copied(), copied(), copied()],
        out_specs=(vmem(), vmem()),
        scratch_shapes=[
            pltpu.VMEM((channels * count, width), jnp.float32),
            pltpu.VMEM((16, width), jnp.float32),
        ],
        compiler_params=pltpu.CompilerParams(vmem_limit_bytes=60 * MIB),
        name="prepare_kernel",
    )(frame_adjoint[0], inputs[:, :, 0], gain.reshape(1, channels))
    partners = [[(z, z ^ s) for z in range(groups)] for s in range(groups)]
    everything = [payload] + [
        lax.ppermute(payload, "chan", partners[s]) for s in range(1, groups)
    ]
    strips = pl.pallas_call(
        after_kernel,
        out_shape=jax.ShapeDtypeStruct(strips.shape, strips.dtype),
        in_specs=[anywhere(), anywhere()],
        out_specs=anywhere(),
        input_output_aliases={0: 0},
        name="after_kernel",
    )(strips, everything[1])
    strips = lax.all_to_all(strips, "rows", split_axis=0, concat_axis=0, tiled=True)
    at = lax.axis_index("chan").astype(jnp.int32).reshape(1)

    kernel = weight.reshape(27, channels, groups, channels)
    kernel = jnp.pad(kernel, ((0, 0), (0, spare), (0, 0), (0, spare)))
    kernel = kernel.reshape(27 * group, ins)

    packed_rows = packing(taps_out, ins, count)[3]
    factor = float(frames * count * width) ** (-0.5)
    windows = pl.pallas_call(
        functools.partial(window_kernel, frames, group),
        out_shape=jax.ShapeDtypeStruct((taps_out, pixels), jnp.bfloat16),
        in_specs=[smem(), copied()],
        out_specs=vmem(),
        scratch_shapes=[pltpu.SMEM((frames,), jnp.int32)],
        compiler_params=limit(taps_out, pixels),
        name="window_kernel",
    )(frame_slot, strips)
    packed = pl.pallas_call(
        functools.partial(grad_kernel, frames, group, factor),
        out_shape=jax.ShapeDtypeStruct((packed_rows, 128), jnp.bfloat16),
        in_specs=[smem(), vmem()] + [copied()] * groups,
        out_specs=vmem(),
        scratch_shapes=[pltpu.VMEM((ins, pixels), jnp.bfloat16)],
        compiler_params=limit(taps_out, pixels),
        cost_estimate=cost(taps_out, ins, pixels),
        name="grad_kernel",
    )(at, windows, *everything)

    pieces = lax.all_to_all(
        packed.reshape(count, packed_rows // count, 128),
        "rows", split_axis=0, concat_axis=0, tiled=True,
    )

    sent = frames * group + round_up(2 * frames, 16)
    parts = pl.pallas_call(
        functools.partial(part_kernel, frames, group),
        out_shape=tuple(
            [jax.ShapeDtypeStruct((frames * (group + 2), width), jnp.float32)]
            + [jax.ShapeDtypeStruct((sent, width), jnp.bfloat16)] * (groups - 1)
        ),
        in_specs=[smem(), vmem(), vmem()] + [copied()] * groups,
        out_specs=(vmem(),) * groups,
        scratch_shapes=[pltpu.VMEM((ins, pixels), jnp.float32)],
        compiler_params=limit(taps_out, pixels),
        cost_estimate=cost(taps_out, ins, pixels),
        name="part_kernel",
    )(at, kernel, windows, *everything)

    arrived = [lax.ppermute(parts[s], "chan", partners[s]) for s in range(1, groups)]
    summed = jnp.sum(pieces.astype(jnp.float32), axis=0).astype(jnp.bfloat16)
    whole = lax.all_gather(summed, "rows", axis=0, tiled=True)
    input_adjoint, grad = pl.pallas_call(
        functools.partial(finish_kernel, frames, group),
        out_shape=(
            jax.ShapeDtypeStruct((frames, group, width), jnp.bfloat16),
            jax.ShapeDtypeStruct((taps_out, ins), jnp.float32),
        ),
        in_specs=[copied()] * (groups + 2),
        out_specs=(vmem(), vmem()),
        compiler_params=limit(taps_out, pixels),
        name="finish_kernel",
    )(whole, payload, parts[0], *arrived)
    grad = grad.reshape(27, group, groups, group)[:, :channels, :, :channels]
    return (
        input_adjoint[:, :channels, None, :],
        grad.reshape(27, channels, groups * channels),
    )


def solution(mesh):
    in_specs = (
        P("rows", "chan", None, None),
        P(),
        P(None, "chan", "rows", None),
        P("chan"),
        P(None, "chan", None),
    )
    out_specs = (P(None, "chan", "rows", None), P(None, "chan", None))
    return jax.shard_map(shards, mesh=mesh, in_specs=in_specs, out_specs=out_specs, check_vma=False)
```

```python
import functools

import jax
import jax.numpy as jnp
from jax import lax
from jax.experimental import pallas as pl
from jax.experimental.pallas import tpu as pltpu
from jax.sharding import PartitionSpec as P

CHANNELS = 192
EPSILON = 1e-06
MIB = 1024 * 1024


def round_up(value, unit):
    return -(-value // unit) * unit


def packing(taps_out, ins, count):
    blocks, rest = divmod(ins, 128)
    half = round_up(-(-taps_out // 2), 16) if rest else 0
    return blocks, rest, half, round_up(blocks * taps_out + half, 16 * count)


def vmem():
    return pl.BlockSpec(memory_space=pltpu.VMEM)


def copied():
    return pl.BlockSpec()


def anywhere():
    return pl.BlockSpec(memory_space=pl.ANY)


def smem():
    return pl.BlockSpec(memory_space=pltpu.SMEM)


def limit(taps_out, pixels):
    return pltpu.CompilerParams(vmem_limit_bytes=10 * MIB + 6 * taps_out * pixels)


def cost(rows, columns, depth):
    return pl.CostEstimate(
        flops=2 * rows * columns * depth,
        bytes_accessed=2 * (rows * depth + columns * depth),
        transcendentals=columns * depth,
    )


def gains(x_refs, start, group):
    found = []
    for ref in x_refs:
        rows = ref[pl.ds(start, 16), :].astype(jnp.float32)
        gain = rows[0:1] + rows[1:2] + rows[2:3]
        found.append(jnp.transpose(jnp.broadcast_to(gain, (128, 128)))[:group])
    return found


def norm(x_refs, t, group):
    values = [ref[pl.ds(t * group, group), :].astype(jnp.float32) for ref in x_refs]
    squares = sum(jnp.sum(value * value, axis=0, keepdims=True) for value in values)
    scale = lax.rsqrt(squares / CHANNELS + EPSILON)
    return scale, [value * scale for value in values]


def prepare_kernel(adjoint_ref, x_ref, gain_ref, strips_ref, payload_ref, lines, gain_rows):
    channels, height, width = adjoint_ref.shape
    frames = x_ref.shape[0]
    group = strips_ref.shape[2]
    lines[...] = adjoint_ref[...].astype(jnp.float32).reshape(channels * height, width)
    nothing = jnp.zeros((group, width), jnp.bfloat16)
    strips_ref[0, 0] = nothing
    strips_ref[height - 1, 2] = nothing
    for r in range(height):
        row = lines[pl.ds(r, channels, stride=height), :]
        if group > channels:
            row = jnp.concatenate(
                [row, jnp.zeros((group - channels, width), jnp.float32)], axis=0
            )
        row = row.astype(jnp.bfloat16)
        for k in range(3):
            if 0 <= r + 1 - k < height:
                strips_ref[r + 1 - k, k] = row
    for t in range(frames):
        values = x_ref[t]
        if group > channels:
            values = jnp.concatenate(
                [
                    values.astype(jnp.float32),
                    jnp.zeros((group - channels, width), jnp.float32),
                ],
                axis=0,
            ).astype(jnp.bfloat16)
        payload_ref[pl.ds(t * group, group), :] = values
    gain = gain_ref[...]
    high = gain.astype(jnp.bfloat16).astype(jnp.float32)
    middle = (gain - high).astype(jnp.bfloat16).astype(jnp.float32)
    gain_rows[...] = jnp.zeros_like(gain_rows)
    gain_rows[pl.ds(0, 1), pl.ds(0, channels)] = high
    gain_rows[pl.ds(1, 1), pl.ds(0, channels)] = middle
    gain_rows[pl.ds(2, 1), pl.ds(0, channels)] = gain - high - middle
    payload_ref[pl.ds(frames * group, 16), :] = gain_rows[...].astype(jnp.bfloat16)


def hidden_kernel(frames, group, at_ref, *refs):
    x_refs, hidden = refs[:-1], refs[-1]
    groups = len(x_refs)
    width = hidden.shape[1] // frames
    gain = gains(x_refs, frames * group, group)
    for t in range(frames):
        scale, scaled = norm(x_refs, t, group)
        for s in range(groups):
            normed = scaled[s] * gain[s]
            value = (normed * jax.nn.sigmoid(normed)).astype(jnp.bfloat16)
            start = pl.multiple_of((at_ref[0] ^ s) * group, 16)
            hidden[pl.ds(start, group), pl.ds(t * width, width)] = value


def grad_kernel(frames, factor, slot_ref, adjoint_ref, hidden, grad_ref, windows, place):
    group, ins = adjoint_ref.shape[2], hidden.shape[0]
    width = adjoint_ref.shape[-1]
    for slot in range(frames):
        place[slot_ref[slot]] = slot

    lane = lax.broadcasted_iota(jnp.int32, (group, width), 1)
    nothing = jnp.zeros((group, width), jnp.bfloat16)
    for a in range(2):
        for inner in range(9):
            for t in range(frames - 2 + a, frames):
                windows[pl.ds((a * 9 + inner) * group, group), pl.ds(t * width, width)] = nothing
    for frame in range(frames):
        slot = place[frame]
        for b in range(3):
            row = adjoint_ref[slot, 2 - b].astype(jnp.float32)
            after = jnp.where(lane == width - 1, 0.0, pltpu.roll(row, width - 1, 1))
            before = jnp.where(lane == 0, 0.0, pltpu.roll(row, 1, 1))
            for c, shifted in enumerate((after, row, before)):
                shifted = shifted.astype(jnp.bfloat16)
                for a in range(3):
                    t = frame + a - 2
                    if t >= 0:
                        windows[
                            pl.ds((a * 9 + b * 3 + c) * group, group), pl.ds(t * width, width)
                        ] = shifted

    grad = lax.dot_general(
        windows[...], hidden[...], (((1,), (1,)), ((), ())), preferred_element_type=jnp.float32
    )
    grad = grad * factor
    taps_out = grad.shape[0]
    blocks, rest, half, rows = packing(taps_out, ins, 1)
    for block in range(blocks):
        grad_ref[pl.ds(block * taps_out, taps_out), :] = grad[
            :, block * 128 : block * 128 + 128
        ].astype(jnp.bfloat16)
    base = blocks * taps_out
    if rest:
        left = grad[:half, blocks * 128 :]
        right = grad[half:, blocks * 128 :]
        right = jnp.concatenate(
            [right, jnp.zeros((2 * half - taps_out, rest), jnp.float32)], axis=0
        )
        grad_ref[pl.ds(base, half), :] = jnp.concatenate([left, right], axis=1).astype(
            jnp.bfloat16
        )
        base = base + half
    tail = grad_ref.shape[0] - base
    if tail:
        grad_ref[pl.ds(base, tail), :] = jnp.zeros((tail, 128), jnp.bfloat16)


def part_kernel(frames, group, at_ref, weight_ref, windows, *refs):
    groups = (len(refs) - 1) // 2
    x_refs = refs[:groups]
    part_refs = refs[groups : 2 * groups]
    product = refs[2 * groups]
    width = part_refs[0].shape[-1]
    product[...] = lax.dot_general(
        weight_ref[...], windows[...], (((0,), (0,)), ((), ())), preferred_element_type=jnp.float32
    )
    gain = gains(x_refs, frames * group, group)
    shares = []
    for t in range(frames):
        scale, scaled = norm(x_refs, t, group)
        part_refs[0][pl.ds(frames * group + t, 1), :] = scale
        share = jnp.zeros((1, width), jnp.float32)
        for s in range(groups):
            normed = scaled[s] * gain[s]
            sigma = jax.nn.sigmoid(normed)
            slope = sigma * (1.0 + normed * (1.0 - sigma)) * gain[s]
            start = pl.multiple_of((at_ref[0] ^ s) * group, 16)
            term = product[pl.ds(start, group), pl.ds(t * width, width)] * slope * scale
            part_refs[s][pl.ds(t * group, group), :] = term.astype(part_refs[s].dtype)
            share = share + jnp.sum(term * scaled[s], axis=0, keepdims=True)
        shares.append(share)
    share = jnp.concatenate(shares, axis=0)
    part_refs[0][pl.ds(frames * group + frames, frames), :] = share
    high = share.astype(jnp.bfloat16).astype(jnp.float32)
    both = [high, share - high]
    unused = round_up(2 * frames, 16) - 2 * frames
    if unused:
        both.append(jnp.zeros((unused, width), jnp.float32))
    both = jnp.concatenate(both, axis=0).astype(jnp.bfloat16)
    for s in range(1, groups):
        part_refs[s][pl.ds(frames * group, both.shape[0]), :] = both


def finish_kernel(frames, group, packed_ref, x_ref, *refs):
    own_ref, others, (out_ref, grad_ref) = refs[0], refs[1:-2], refs[-2:]
    taps_out, ins = grad_ref.shape
    blocks, rest, half, rows = packing(taps_out, ins, 1)
    for block in range(blocks):
        grad_ref[:, pl.ds(block * 128, 128)] = packed_ref[
            pl.ds(block * taps_out, taps_out), :
        ].astype(jnp.float32)
    if rest:
        both = packed_ref[pl.ds(blocks * taps_out, half), :].astype(jnp.float32)
        grad_ref[pl.ds(0, half), pl.ds(blocks * 128, rest)] = both[:, :rest]
        grad_ref[pl.ds(half, taps_out - half), pl.ds(blocks * 128, rest)] = both[
            : taps_out - half, rest:
        ]

    share = own_ref[pl.ds(frames * group + frames, frames), :]
    for ref in others:
        both = ref[pl.ds(frames * group, round_up(2 * frames, 16)), :].astype(jnp.float32)
        share = share + both[:frames] + both[frames : 2 * frames]
    share = share / CHANNELS
    for t in range(frames):
        term = own_ref[pl.ds(t * group, group), :]
        for ref in others:
            term = term + ref[pl.ds(t * group, group), :].astype(jnp.float32)
        scale = own_ref[pl.ds(frames * group + t, 1), :]
        scaled = x_ref[pl.ds(t * group, group), :].astype(jnp.float32) * scale
        out_ref[t] = (term - scaled * share[t : t + 1]).astype(jnp.bfloat16)


def shards(frame_adjoint, frame_slot, inputs, gain, weight):
    count = lax.axis_size("rows")
    groups = lax.axis_size("chan")
    frames, channels, _, width = inputs.shape
    group = round_up(channels, 16)
    spare = group - channels
    ins = groups * group

    taps_out = 27 * group
    pixels = frames * width
    strips, payload = pl.pallas_call(
        prepare_kernel,
        out_shape=(
            jax.ShapeDtypeStruct((count, 3, group, width), jnp.bfloat16),
            jax.ShapeDtypeStruct((frames * group + 16, width), jnp.bfloat16),
        ),
        in_specs=[copied(), copied(), copied()],
        out_specs=(vmem(), vmem()),
        scratch_shapes=[
            pltpu.VMEM((channels * count, width), jnp.float32),
            pltpu.VMEM((16, width), jnp.float32),
        ],
        compiler_params=pltpu.CompilerParams(vmem_limit_bytes=60 * MIB),
        name="prepare_kernel",
    )(frame_adjoint[0], inputs[:, :, 0], gain.reshape(1, channels))
    partners = [[(z, z ^ s) for z in range(groups)] for s in range(groups)]
    everything = [payload] + [
        lax.ppermute(payload, "chan", partners[s]) for s in range(1, groups)
    ]
    strips = lax.all_to_all(strips, "rows", split_axis=0, concat_axis=0, tiled=True)
    at = lax.axis_index("chan").astype(jnp.int32).reshape(1)

    kernel = weight.reshape(27, channels, groups, channels)
    kernel = jnp.pad(kernel, ((0, 0), (0, spare), (0, 0), (0, spare)))
    kernel = kernel.reshape(27 * group, ins)

    packed_rows = packing(taps_out, ins, count)[3]
    factor = float(frames * count * width) ** (-0.5)
    hidden = pl.pallas_call(
        functools.partial(hidden_kernel, frames, group),
        out_shape=jax.ShapeDtypeStruct((ins, pixels), jnp.bfloat16),
        in_specs=[smem()] + [copied()] * groups,
        out_specs=vmem(),
        compiler_params=limit(taps_out, pixels),
        cost_estimate=pl.CostEstimate(
            flops=16 * ins * pixels, bytes_accessed=32 * ins * pixels, transcendentals=ins * pixels
        ),
        name="hidden_kernel",
    )(at, *everything)
    packed, windows = pl.pallas_call(
        functools.partial(grad_kernel, frames, factor),
        out_shape=(
            jax.ShapeDtypeStruct((packed_rows, 128), jnp.bfloat16),
            jax.ShapeDtypeStruct((taps_out, pixels), jnp.bfloat16),
        ),
        in_specs=[smem(), copied(), vmem()],
        out_specs=(vmem(), vmem()),
        scratch_shapes=[pltpu.SMEM((frames,), jnp.int32)],
        compiler_params=limit(taps_out, pixels),
        cost_estimate=cost(taps_out, ins, pixels),
        name="grad_kernel",
    )(frame_slot, strips, hidden)

    pieces = lax.all_to_all(
        packed.reshape(count, packed_rows // count, 128),
        "rows", split_axis=0, concat_axis=0, tiled=True,
    )

    sent = frames * group + round_up(2 * frames, 16)
    parts = pl.pallas_call(
        functools.partial(part_kernel, frames, group),
        out_shape=tuple(
            [jax.ShapeDtypeStruct((frames * (group + 2), width), jnp.float32)]
            + [jax.ShapeDtypeStruct((sent, width), jnp.bfloat16)] * (groups - 1)
        ),
        in_specs=[smem(), vmem(), vmem()] + [copied()] * groups,
        out_specs=(vmem(),) * groups,
        scratch_shapes=[pltpu.VMEM((ins, pixels), jnp.float32)],
        compiler_params=limit(taps_out, pixels),
        cost_estimate=cost(taps_out, ins, pixels),
        name="part_kernel",
    )(at, kernel, windows, *everything)

    arrived = [lax.ppermute(parts[s], "chan", partners[s]) for s in range(1, groups)]
    summed = jnp.sum(pieces.astype(jnp.float32), axis=0).astype(jnp.bfloat16)
    whole = lax.all_gather(summed, "rows", axis=0, tiled=True)
    input_adjoint, grad = pl.pallas_call(
        functools.partial(finish_kernel, frames, group),
        out_shape=(
            jax.ShapeDtypeStruct((frames, group, width), jnp.bfloat16),
            jax.ShapeDtypeStruct((taps_out, ins), jnp.float32),
        ),
        in_specs=[copied()] * (groups + 2),
        out_specs=(vmem(), vmem()),
        compiler_params=limit(taps_out, pixels),
        name="finish_kernel",
    )(whole, payload, parts[0], *arrived)
    grad = grad.reshape(27, group, groups, group)[:, :channels, :, :channels]
    return (
        input_adjoint[:, :channels, None, :],
        grad.reshape(27, channels, groups * channels),
    )


def solution(mesh):
    in_specs = (
        P("rows", "chan", None, None),
        P(),
        P(None, "chan", "rows", None),
        P("chan"),
        P(None, "chan", None),
    )
    out_specs = (P(None, "chan", "rows", None), P(None, "chan", None))
    return jax.shard_map(shards, mesh=mesh, in_specs=in_specs, out_specs=out_specs, check_vma=False)
```

```python
import functools

import jax
import jax.numpy as jnp
from jax import lax
from jax.experimental import pallas as pl
from jax.experimental.pallas import tpu as pltpu
from jax.sharding import PartitionSpec as P

CHANNELS = 192
EPSILON = 1e-06
MIB = 1024 * 1024


def round_up(value, unit):
    return -(-value // unit) * unit


def packing(taps_out, ins, count):
    blocks, rest = divmod(ins, 128)
    half = round_up(-(-taps_out // 2), 16) if rest else 0
    return blocks, rest, half, round_up(blocks * taps_out + half, 16 * count)


def vmem():
    return pl.BlockSpec(memory_space=pltpu.VMEM)


def copied():
    return pl.BlockSpec()


def smem():
    return pl.BlockSpec(memory_space=pltpu.SMEM)


def limit(taps_out, pixels):
    return pltpu.CompilerParams(vmem_limit_bytes=10 * MIB + 6 * taps_out * pixels)


def cost(rows, columns, depth):
    return pl.CostEstimate(
        flops=2 * rows * columns * depth,
        bytes_accessed=2 * (rows * depth + columns * depth),
        transcendentals=columns * depth,
    )


def gains(x_refs, start, group):
    found = []
    for ref in x_refs:
        rows = ref[pl.ds(start, 16), :].astype(jnp.float32)
        gain = rows[0:1] + rows[1:2] + rows[2:3]
        found.append(jnp.transpose(jnp.broadcast_to(gain, (128, 128)))[:group])
    return found


def norm(x_refs, t, group):
    values = [ref[pl.ds(t * group, group), :].astype(jnp.float32) for ref in x_refs]
    squares = sum(jnp.sum(value * value, axis=0, keepdims=True) for value in values)
    scale = lax.rsqrt(squares / CHANNELS + EPSILON)
    return scale, [value * scale for value in values]


def prepare_kernel(adjoint_ref, x_ref, gain_ref, strips_ref, payload_ref, lines, gain_rows):
    channels, height, width = adjoint_ref.shape
    frames = x_ref.shape[0]
    group = strips_ref.shape[2]
    lines[...] = adjoint_ref[...].astype(jnp.float32).reshape(channels * height, width)
    nothing = jnp.zeros((group, width), jnp.bfloat16)
    strips_ref[0, 0] = nothing
    strips_ref[height - 1, 2] = nothing
    for r in range(height):
        row = lines[pl.ds(r, channels, stride=height), :]
        if group > channels:
            row = jnp.concatenate(
                [row, jnp.zeros((group - channels, width), jnp.float32)], axis=0
            )
        row = row.astype(jnp.bfloat16)
        for k in range(3):
            if 0 <= r + 1 - k < height:
                strips_ref[r + 1 - k, k] = row
    for t in range(frames):
        values = x_ref[t]
        if group > channels:
            values = jnp.concatenate(
                [
                    values.astype(jnp.float32),
                    jnp.zeros((group - channels, width), jnp.float32),
                ],
                axis=0,
            ).astype(jnp.bfloat16)
        payload_ref[pl.ds(t * group, group), :] = values
    gain = gain_ref[...]
    high = gain.astype(jnp.bfloat16).astype(jnp.float32)
    middle = (gain - high).astype(jnp.bfloat16).astype(jnp.float32)
    gain_rows[...] = jnp.zeros_like(gain_rows)
    gain_rows[pl.ds(0, 1), pl.ds(0, channels)] = high
    gain_rows[pl.ds(1, 1), pl.ds(0, channels)] = middle
    gain_rows[pl.ds(2, 1), pl.ds(0, channels)] = gain - high - middle
    payload_ref[pl.ds(frames * group, 16), :] = gain_rows[...].astype(jnp.bfloat16)


def window_kernel(frames, group, slot_ref, adjoint_ref, windows, place):
    width = adjoint_ref.shape[-1]
    for slot in range(frames):
        place[slot_ref[slot]] = slot

    lane = lax.broadcasted_iota(jnp.int32, (group, width), 1)
    nothing = jnp.zeros((group, width), jnp.bfloat16)
    for a in range(2):
        for inner in range(9):
            for t in range(frames - 2 + a, frames):
                windows[pl.ds((a * 9 + inner) * group, group), pl.ds(t * width, width)] = nothing
    for frame in range(frames):
        slot = place[frame]
        for b in range(3):
            row = adjoint_ref[slot, 2 - b].astype(jnp.float32)
            after = jnp.where(lane == width - 1, 0.0, pltpu.roll(row, width - 1, 1))
            before = jnp.where(lane == 0, 0.0, pltpu.roll(row, 1, 1))
            for c, shifted in enumerate((after, row, before)):
                shifted = shifted.astype(jnp.bfloat16)
                for a in range(3):
                    t = frame + a - 2
                    if t >= 0:
                        windows[
                            pl.ds((a * 9 + b * 3 + c) * group, group), pl.ds(t * width, width)
                        ] = shifted

def grad_kernel(frames, group, factor, at_ref, windows, *refs):
    groups = len(refs) - 2
    x_refs = refs[:groups]
    grad_ref, hidden = refs[groups:]
    ins = groups * group
    width = windows.shape[1] // frames
    gain = gains(x_refs, frames * group, group)
    for t in range(frames):
        scale, scaled = norm(x_refs, t, group)
        for s in range(groups):
            normed = scaled[s] * gain[s]
            value = (normed * jax.nn.sigmoid(normed)).astype(jnp.bfloat16)
            start = pl.multiple_of((at_ref[0] ^ s) * group, 16)
            hidden[pl.ds(start, group), pl.ds(t * width, width)] = value

    grad = lax.dot_general(
        windows[...], hidden[...], (((1,), (1,)), ((), ())), preferred_element_type=jnp.float32
    )
    grad = grad * factor
    taps_out = grad.shape[0]
    blocks, rest, half, rows = packing(taps_out, ins, 1)
    for block in range(blocks):
        grad_ref[pl.ds(block * taps_out, taps_out), :] = grad[
            :, block * 128 : block * 128 + 128
        ].astype(jnp.bfloat16)
    base = blocks * taps_out
    if rest:
        left = grad[:half, blocks * 128 :]
        right = grad[half:, blocks * 128 :]
        right = jnp.concatenate(
            [right, jnp.zeros((2 * half - taps_out, rest), jnp.float32)], axis=0
        )
        grad_ref[pl.ds(base, half), :] = jnp.concatenate([left, right], axis=1).astype(
            jnp.bfloat16
        )
        base = base + half
    tail = grad_ref.shape[0] - base
    if tail:
        grad_ref[pl.ds(base, tail), :] = jnp.zeros((tail, 128), jnp.bfloat16)


def part_kernel(frames, group, at_ref, weight_ref, windows, *refs):
    groups = (len(refs) - 1) // 2
    x_refs = refs[:groups]
    part_refs = refs[groups : 2 * groups]
    product = refs[2 * groups]
    width = part_refs[0].shape[-1]
    product[...] = lax.dot_general(
        weight_ref[...], windows[...], (((0,), (0,)), ((), ())), preferred_element_type=jnp.float32
    )
    gain = gains(x_refs, frames * group, group)
    shares = []
    for t in range(frames):
        scale, scaled = norm(x_refs, t, group)
        part_refs[0][pl.ds(frames * group + t, 1), :] = scale
        share = jnp.zeros((1, width), jnp.float32)
        for s in range(groups):
            normed = scaled[s] * gain[s]
            sigma = jax.nn.sigmoid(normed)
            slope = sigma * (1.0 + normed * (1.0 - sigma)) * gain[s]
            start = pl.multiple_of((at_ref[0] ^ s) * group, 16)
            term = product[pl.ds(start, group), pl.ds(t * width, width)] * slope * scale
            part_refs[s][pl.ds(t * group, group), :] = term.astype(part_refs[s].dtype)
            share = share + jnp.sum(term * scaled[s], axis=0, keepdims=True)
        shares.append(share)
    share = jnp.concatenate(shares, axis=0)
    part_refs[0][pl.ds(frames * group + frames, frames), :] = share
    high = share.astype(jnp.bfloat16).astype(jnp.float32)
    both = [high, share - high]
    unused = round_up(2 * frames, 16) - 2 * frames
    if unused:
        both.append(jnp.zeros((unused, width), jnp.float32))
    both = jnp.concatenate(both, axis=0).astype(jnp.bfloat16)
    for s in range(1, groups):
        part_refs[s][pl.ds(frames * group, both.shape[0]), :] = both


def finish_kernel(frames, group, packed_ref, x_ref, *refs):
    own_ref, others, (out_ref, grad_ref) = refs[0], refs[1:-2], refs[-2:]
    taps_out, ins = grad_ref.shape
    blocks, rest, half, rows = packing(taps_out, ins, 1)
    for block in range(blocks):
        grad_ref[:, pl.ds(block * 128, 128)] = packed_ref[
            pl.ds(block * taps_out, taps_out), :
        ].astype(jnp.float32)
    if rest:
        both = packed_ref[pl.ds(blocks * taps_out, half), :].astype(jnp.float32)
        grad_ref[pl.ds(0, half), pl.ds(blocks * 128, rest)] = both[:, :rest]
        grad_ref[pl.ds(half, taps_out - half), pl.ds(blocks * 128, rest)] = both[
            : taps_out - half, rest:
        ]

    share = own_ref[pl.ds(frames * group + frames, frames), :]
    for ref in others:
        both = ref[pl.ds(frames * group, round_up(2 * frames, 16)), :].astype(jnp.float32)
        share = share + both[:frames] + both[frames : 2 * frames]
    share = share / CHANNELS
    for t in range(frames):
        term = own_ref[pl.ds(t * group, group), :]
        for ref in others:
            term = term + ref[pl.ds(t * group, group), :].astype(jnp.float32)
        scale = own_ref[pl.ds(frames * group + t, 1), :]
        scaled = x_ref[pl.ds(t * group, group), :].astype(jnp.float32) * scale
        out_ref[t] = (term - scaled * share[t : t + 1]).astype(jnp.bfloat16)


def shards(frame_adjoint, frame_slot, inputs, gain, weight):
    count = lax.axis_size("rows")
    groups = lax.axis_size("chan")
    frames, channels, _, width = inputs.shape
    group = round_up(channels, 16)
    spare = group - channels
    ins = groups * group

    taps_out = 27 * group
    pixels = frames * width
    strips, payload = pl.pallas_call(
        prepare_kernel,
        out_shape=(
            jax.ShapeDtypeStruct((count, 3, group, width), jnp.bfloat16),
            jax.ShapeDtypeStruct((frames * group + 16, width), jnp.bfloat16),
        ),
        in_specs=[copied(), copied(), copied()],
        out_specs=(vmem(), vmem()),
        scratch_shapes=[
            pltpu.VMEM((channels * count, width), jnp.float32),
            pltpu.VMEM((16, width), jnp.float32),
        ],
        compiler_params=pltpu.CompilerParams(vmem_limit_bytes=60 * MIB),
        name="prepare_kernel",
    )(frame_adjoint[0], inputs[:, :, 0], gain.reshape(1, channels))
    partners = [[(z, z ^ s) for z in range(groups)] for s in range(groups)]
    everything = [payload] * groups
    for s in range(1, groups):
        everything[s] = lax.ppermute(everything[s & (s - 1)], "chan", partners[s & -s])
    strips = lax.all_to_all(strips, "rows", split_axis=0, concat_axis=0, tiled=True)
    at = lax.axis_index("chan").astype(jnp.int32).reshape(1)

    kernel = weight.reshape(27, channels, groups, channels)
    kernel = jnp.pad(kernel, ((0, 0), (0, spare), (0, 0), (0, spare)))
    kernel = kernel.reshape(27 * group, ins)

    packed_rows = packing(taps_out, ins, count)[3]
    factor = float(frames * count * width) ** (-0.5)
    windows = pl.pallas_call(
        functools.partial(window_kernel, frames, group),
        out_shape=jax.ShapeDtypeStruct((taps_out, pixels), jnp.bfloat16),
        in_specs=[smem(), copied()],
        out_specs=vmem(),
        scratch_shapes=[pltpu.SMEM((frames,), jnp.int32)],
        compiler_params=limit(taps_out, pixels),
        name="window_kernel",
    )(frame_slot, strips)
    packed = pl.pallas_call(
        functools.partial(grad_kernel, frames, group, factor),
        out_shape=jax.ShapeDtypeStruct((packed_rows, 128), jnp.bfloat16),
        in_specs=[smem(), vmem()] + [copied()] * groups,
        out_specs=vmem(),
        scratch_shapes=[pltpu.VMEM((ins, pixels), jnp.bfloat16)],
        compiler_params=limit(taps_out, pixels),
        cost_estimate=cost(taps_out, ins, pixels),
        name="grad_kernel",
    )(at, windows, *everything)

    pieces = lax.all_to_all(
        packed.reshape(count, packed_rows // count, 128),
        "rows", split_axis=0, concat_axis=0, tiled=True,
    )

    sent = frames * group + round_up(2 * frames, 16)
    parts = pl.pallas_call(
        functools.partial(part_kernel, frames, group),
        out_shape=tuple(
            [jax.ShapeDtypeStruct((frames * (group + 2), width), jnp.float32)]
            + [jax.ShapeDtypeStruct((sent, width), jnp.bfloat16)] * (groups - 1)
        ),
        in_specs=[smem(), vmem(), vmem()] + [copied()] * groups,
        out_specs=(vmem(),) * groups,
        scratch_shapes=[pltpu.VMEM((ins, pixels), jnp.float32)],
        compiler_params=limit(taps_out, pixels),
        cost_estimate=cost(taps_out, ins, pixels),
        name="part_kernel",
    )(at, kernel, windows, *everything)

    arrived = [lax.ppermute(parts[s], "chan", partners[s]) for s in range(1, groups)]
    summed = jnp.sum(pieces.astype(jnp.float32), axis=0).astype(jnp.bfloat16)
    whole = lax.all_gather(summed, "rows", axis=0, tiled=True)
    input_adjoint, grad = pl.pallas_call(
        functools.partial(finish_kernel, frames, group),
        out_shape=(
            jax.ShapeDtypeStruct((frames, group, width), jnp.bfloat16),
            jax.ShapeDtypeStruct((taps_out, ins), jnp.float32),
        ),
        in_specs=[copied()] * (groups + 2),
        out_specs=(vmem(), vmem()),
        compiler_params=limit(taps_out, pixels),
        name="finish_kernel",
    )(whole, payload, parts[0], *arrived)
    grad = grad.reshape(27, group, groups, group)[:, :channels, :, :channels]
    return (
        input_adjoint[:, :channels, None, :],
        grad.reshape(27, channels, groups * channels),
    )


def solution(mesh):
    in_specs = (
        P("rows", "chan", None, None),
        P(),
        P(None, "chan", "rows", None),
        P("chan"),
        P(None, "chan", None),
    )
    out_specs = (P(None, "chan", "rows", None), P(None, "chan", None))
    return jax.shard_map(shards, mesh=mesh, in_specs=in_specs, out_specs=out_specs, check_vma=False)
```

```python
import functools

import jax
import jax.numpy as jnp
from jax import lax
from jax.experimental import pallas as pl
from jax.experimental.pallas import tpu as pltpu
from jax.sharding import PartitionSpec as P

CHANNELS = 192
EPSILON = 1e-06
MIB = 1024 * 1024


def round_up(value, unit):
    return -(-value // unit) * unit


def packing(taps_out, ins, count):
    blocks, rest = divmod(ins, 128)
    half = round_up(-(-taps_out // 2), 16) if rest else 0
    return blocks, rest, half, round_up(blocks * taps_out + half, 16 * count)


def vmem():
    return pl.BlockSpec(memory_space=pltpu.VMEM)


def copied():
    return pl.BlockSpec()


def anywhere():
    return pl.BlockSpec(memory_space=pl.ANY)


def smem():
    return pl.BlockSpec(memory_space=pltpu.SMEM)


def limit(taps_out, pixels):
    return pltpu.CompilerParams(vmem_limit_bytes=10 * MIB + 6 * taps_out * pixels)


def cost(rows, columns, depth):
    return pl.CostEstimate(
        flops=2 * rows * columns * depth,
        bytes_accessed=2 * (rows * depth + columns * depth),
        transcendentals=columns * depth,
    )


def gains(x_refs, start, group):
    found = []
    for ref in x_refs:
        rows = ref[pl.ds(start, 16), :].astype(jnp.float32)
        gain = rows[0:1] + rows[1:2] + rows[2:3]
        found.append(jnp.transpose(jnp.broadcast_to(gain, (128, 128)))[:group])
    return found


def norm(x_refs, t, group):
    values = [ref[pl.ds(t * group, group), :].astype(jnp.float32) for ref in x_refs]
    squares = sum(jnp.sum(value * value, axis=0, keepdims=True) for value in values)
    scale = lax.rsqrt(squares / CHANNELS + EPSILON)
    return scale, [value * scale for value in values]


def prepare_kernel(adjoint_ref, x_ref, gain_ref, strips_ref, payload_ref, lines, gain_rows):
    channels, height, width = adjoint_ref.shape
    frames = x_ref.shape[0]
    group = strips_ref.shape[2]
    lines[...] = adjoint_ref[...].astype(jnp.float32).reshape(channels * height, width)
    nothing = jnp.zeros((group, width), jnp.bfloat16)
    strips_ref[0, 0] = nothing
    strips_ref[height - 1, 2] = nothing
    for r in range(height):
        row = lines[pl.ds(r, channels, stride=height), :]
        if group > channels:
            row = jnp.concatenate(
                [row, jnp.zeros((group - channels, width), jnp.float32)], axis=0
            )
        row = row.astype(jnp.bfloat16)
        for k in range(3):
            if 0 <= r + 1 - k < height:
                strips_ref[r + 1 - k, k] = row
    for t in range(frames):
        values = x_ref[t]
        if group > channels:
            values = jnp.concatenate(
                [
                    values.astype(jnp.float32),
                    jnp.zeros((group - channels, width), jnp.float32),
                ],
                axis=0,
            ).astype(jnp.bfloat16)
        payload_ref[pl.ds(t * group, group), :] = values
    gain = gain_ref[...]
    high = gain.astype(jnp.bfloat16).astype(jnp.float32)
    middle = (gain - high).astype(jnp.bfloat16).astype(jnp.float32)
    gain_rows[...] = jnp.zeros_like(gain_rows)
    gain_rows[pl.ds(0, 1), pl.ds(0, channels)] = high
    gain_rows[pl.ds(1, 1), pl.ds(0, channels)] = middle
    gain_rows[pl.ds(2, 1), pl.ds(0, channels)] = gain - high - middle
    payload_ref[pl.ds(frames * group, 16), :] = gain_rows[...].astype(jnp.bfloat16)


def hold_kernel(block_ref, out_ref):
    pass


def hold(block):
    return pl.pallas_call(
        hold_kernel,
        out_shape=jax.ShapeDtypeStruct(block.shape, block.dtype),
        in_specs=[anywhere()],
        out_specs=anywhere(),
        input_output_aliases={0: 0},
        cost_estimate=pl.CostEstimate(flops=0, bytes_accessed=128 * MIB, transcendentals=0),
        name="hold_kernel",
    )(block)


def window_kernel(frames, group, slot_ref, adjoint_ref, windows, place):
    width = adjoint_ref.shape[-1]
    for slot in range(frames):
        place[slot_ref[slot]] = slot

    lane = lax.broadcasted_iota(jnp.int32, (group, width), 1)
    nothing = jnp.zeros((group, width), jnp.bfloat16)
    for a in range(2):
        for inner in range(9):
            for t in range(frames - 2 + a, frames):
                windows[pl.ds((a * 9 + inner) * group, group), pl.ds(t * width, width)] = nothing
    for frame in range(frames):
        slot = place[frame]
        for b in range(3):
            row = adjoint_ref[slot, 2 - b].astype(jnp.float32)
            after = jnp.where(lane == width - 1, 0.0, pltpu.roll(row, width - 1, 1))
            before = jnp.where(lane == 0, 0.0, pltpu.roll(row, 1, 1))
            for c, shifted in enumerate((after, row, before)):
                shifted = shifted.astype(jnp.bfloat16)
                for a in range(3):
                    t = frame + a - 2
                    if t >= 0:
                        windows[
                            pl.ds((a * 9 + b * 3 + c) * group, group), pl.ds(t * width, width)
                        ] = shifted

def grad_kernel(frames, group, factor, at_ref, windows, *refs):
    groups = len(refs) - 2
    x_refs = refs[:groups]
    grad_ref, hidden = refs[groups:]
    ins = groups * group
    width = windows.shape[1] // frames
    gain = gains(x_refs, frames * group, group)
    for t in range(frames):
        scale, scaled = norm(x_refs, t, group)
        for s in range(groups):
            normed = scaled[s] * gain[s]
            value = (normed * jax.nn.sigmoid(normed)).astype(jnp.bfloat16)
            start = pl.multiple_of((at_ref[0] ^ s) * group, 16)
            hidden[pl.ds(start, group), pl.ds(t * width, width)] = value

    grad = lax.dot_general(
        windows[...], hidden[...], (((1,), (1,)), ((), ())), preferred_element_type=jnp.float32
    )
    grad = grad * factor
    taps_out = grad.shape[0]
    blocks, rest, half, rows = packing(taps_out, ins, 1)
    for block in range(blocks):
        grad_ref[pl.ds(block * taps_out, taps_out), :] = grad[
            :, block * 128 : block * 128 + 128
        ].astype(jnp.bfloat16)
    base = blocks * taps_out
    if rest:
        left = grad[:half, blocks * 128 :]
        right = grad[half:, blocks * 128 :]
        right = jnp.concatenate(
            [right, jnp.zeros((2 * half - taps_out, rest), jnp.float32)], axis=0
        )
        grad_ref[pl.ds(base, half), :] = jnp.concatenate([left, right], axis=1).astype(
            jnp.bfloat16
        )
        base = base + half
    tail = grad_ref.shape[0] - base
    if tail:
        grad_ref[pl.ds(base, tail), :] = jnp.zeros((tail, 128), jnp.bfloat16)


def part_kernel(frames, group, at_ref, weight_ref, windows, *refs):
    groups = (len(refs) - 1) // 2
    x_refs = refs[:groups]
    part_refs = refs[groups : 2 * groups]
    product = refs[2 * groups]
    width = part_refs[0].shape[-1]
    product[...] = lax.dot_general(
        weight_ref[...], windows[...], (((0,), (0,)), ((), ())), preferred_element_type=jnp.float32
    )
    gain = gains(x_refs, frames * group, group)
    shares = []
    for t in range(frames):
        scale, scaled = norm(x_refs, t, group)
        part_refs[0][pl.ds(frames * group + t, 1), :] = scale
        share = jnp.zeros((1, width), jnp.float32)
        for s in range(groups):
            normed = scaled[s] * gain[s]
            sigma = jax.nn.sigmoid(normed)
            slope = sigma * (1.0 + normed * (1.0 - sigma)) * gain[s]
            start = pl.multiple_of((at_ref[0] ^ s) * group, 16)
            term = product[pl.ds(start, group), pl.ds(t * width, width)] * slope * scale
            part_refs[s][pl.ds(t * group, group), :] = term.astype(part_refs[s].dtype)
            share = share + jnp.sum(term * scaled[s], axis=0, keepdims=True)
        shares.append(share)
    share = jnp.concatenate(shares, axis=0)
    part_refs[0][pl.ds(frames * group + frames, frames), :] = share
    high = share.astype(jnp.bfloat16).astype(jnp.float32)
    both = [high, share - high]
    unused = round_up(2 * frames, 16) - 2 * frames
    if unused:
        both.append(jnp.zeros((unused, width), jnp.float32))
    both = jnp.concatenate(both, axis=0).astype(jnp.bfloat16)
    for s in range(1, groups):
        part_refs[s][pl.ds(frames * group, both.shape[0]), :] = both


def finish_kernel(frames, group, packed_ref, x_ref, *refs):
    own_ref, others, (out_ref, grad_ref) = refs[0], refs[1:-2], refs[-2:]
    taps_out, ins = grad_ref.shape
    blocks, rest, half, rows = packing(taps_out, ins, 1)
    for block in range(blocks):
        grad_ref[:, pl.ds(block * 128, 128)] = packed_ref[
            pl.ds(block * taps_out, taps_out), :
        ].astype(jnp.float32)
    if rest:
        both = packed_ref[pl.ds(blocks * taps_out, half), :].astype(jnp.float32)
        grad_ref[pl.ds(0, half), pl.ds(blocks * 128, rest)] = both[:, :rest]
        grad_ref[pl.ds(half, taps_out - half), pl.ds(blocks * 128, rest)] = both[
            : taps_out - half, rest:
        ]

    share = own_ref[pl.ds(frames * group + frames, frames), :]
    for ref in others:
        both = ref[pl.ds(frames * group, round_up(2 * frames, 16)), :].astype(jnp.float32)
        share = share + both[:frames] + both[frames : 2 * frames]
    share = share / CHANNELS
    for t in range(frames):
        term = own_ref[pl.ds(t * group, group), :]
        for ref in others:
            term = term + ref[pl.ds(t * group, group), :].astype(jnp.float32)
        scale = own_ref[pl.ds(frames * group + t, 1), :]
        scaled = x_ref[pl.ds(t * group, group), :].astype(jnp.float32) * scale
        out_ref[t] = (term - scaled * share[t : t + 1]).astype(jnp.bfloat16)


def shards(frame_adjoint, frame_slot, inputs, gain, weight):
    count = lax.axis_size("rows")
    groups = lax.axis_size("chan")
    frames, channels, _, width = inputs.shape
    group = round_up(channels, 16)
    spare = group - channels
    ins = groups * group

    taps_out = 27 * group
    pixels = frames * width
    strips, payload = pl.pallas_call(
        prepare_kernel,
        out_shape=(
            jax.ShapeDtypeStruct((count, 3, group, width), jnp.bfloat16),
            jax.ShapeDtypeStruct((frames * group + 16, width), jnp.bfloat16),
        ),
        in_specs=[copied(), copied(), copied()],
        out_specs=(vmem(), vmem()),
        scratch_shapes=[
            pltpu.VMEM((channels * count, width), jnp.float32),
            pltpu.VMEM((16, width), jnp.float32),
        ],
        compiler_params=pltpu.CompilerParams(vmem_limit_bytes=60 * MIB),
        name="prepare_kernel",
    )(frame_adjoint[0], inputs[:, :, 0], gain.reshape(1, channels))
    partners = [[(z, z ^ s) for z in range(groups)] for s in range(groups)]
    everything = [payload] * groups
    for s in range(1, groups):
        everything[s] = lax.ppermute(everything[s & (s - 1)], "chan", partners[s & -s])
        if s & (s - 1) == 0 and s > 1:
            everything[s] = hold(everything[s])
    strips = lax.all_to_all(strips, "rows", split_axis=0, concat_axis=0, tiled=True)
    at = lax.axis_index("chan").astype(jnp.int32).reshape(1)

    kernel = weight.reshape(27, channels, groups, channels)
    kernel = jnp.pad(kernel, ((0, 0), (0, spare), (0, 0), (0, spare)))
    kernel = kernel.reshape(27 * group, ins)

    packed_rows = packing(taps_out, ins, count)[3]
    factor = float(frames * count * width) ** (-0.5)
    windows = pl.pallas_call(
        functools.partial(window_kernel, frames, group),
        out_shape=jax.ShapeDtypeStruct((taps_out, pixels), jnp.bfloat16),
        in_specs=[smem(), copied()],
        out_specs=vmem(),
        scratch_shapes=[pltpu.SMEM((frames,), jnp.int32)],
        compiler_params=limit(taps_out, pixels),
        name="window_kernel",
    )(frame_slot, strips)
    packed = pl.pallas_call(
        functools.partial(grad_kernel, frames, group, factor),
        out_shape=jax.ShapeDtypeStruct((packed_rows, 128), jnp.bfloat16),
        in_specs=[smem(), vmem()] + [copied()] * groups,
        out_specs=vmem(),
        scratch_shapes=[pltpu.VMEM((ins, pixels), jnp.bfloat16)],
        compiler_params=limit(taps_out, pixels),
        cost_estimate=cost(taps_out, ins, pixels),
        name="grad_kernel",
    )(at, windows, *everything)

    pieces = lax.all_to_all(
        packed.reshape(count, packed_rows // count, 128),
        "rows", split_axis=0, concat_axis=0, tiled=True,
    )

    sent = frames * group + round_up(2 * frames, 16)
    parts = pl.pallas_call(
        functools.partial(part_kernel, frames, group),
        out_shape=tuple(
            [jax.ShapeDtypeStruct((frames * (group + 2), width), jnp.float32)]
            + [jax.ShapeDtypeStruct((sent, width), jnp.bfloat16)] * (groups - 1)
        ),
        in_specs=[smem(), vmem(), vmem()] + [copied()] * groups,
        out_specs=(vmem(),) * groups,
        scratch_shapes=[pltpu.VMEM((ins, pixels), jnp.float32)],
        compiler_params=limit(taps_out, pixels),
        cost_estimate=cost(taps_out, ins, pixels),
        name="part_kernel",
    )(at, kernel, windows, *everything)

    arrived = [lax.ppermute(parts[s], "chan", partners[s]) for s in range(1, groups)]
    summed = jnp.sum(pieces.astype(jnp.float32), axis=0).astype(jnp.bfloat16)
    whole = lax.all_gather(summed, "rows", axis=0, tiled=True)
    input_adjoint, grad = pl.pallas_call(
        functools.partial(finish_kernel, frames, group),
        out_shape=(
            jax.ShapeDtypeStruct((frames, group, width), jnp.bfloat16),
            jax.ShapeDtypeStruct((taps_out, ins), jnp.float32),
        ),
        in_specs=[copied()] * (groups + 2),
        out_specs=(vmem(), vmem()),
        compiler_params=limit(taps_out, pixels),
        name="finish_kernel",
    )(whole, payload, parts[0], *arrived)
    grad = grad.reshape(27, group, groups, group)[:, :channels, :, :channels]
    return (
        input_adjoint[:, :channels, None, :],
        grad.reshape(27, channels, groups * channels),
    )


def solution(mesh):
    in_specs = (
        P("rows", "chan", None, None),
        P(),
        P(None, "chan", "rows", None),
        P("chan"),
        P(None, "chan", None),
    )
    out_specs = (P(None, "chan", "rows", None), P(None, "chan", None))
    return jax.shard_map(shards, mesh=mesh, in_specs=in_specs, out_specs=out_specs, check_vma=False)
```

```python
import functools

import jax
import jax.numpy as jnp
from jax import lax
from jax.experimental import pallas as pl
from jax.experimental.pallas import tpu as pltpu
from jax.sharding import PartitionSpec as P

CHANNELS = 192
EPSILON = 1e-06
MIB = 1024 * 1024


def round_up(value, unit):
    return -(-value // unit) * unit


def packing(taps_out, ins, count):
    blocks, rest = divmod(ins, 128)
    half = round_up(-(-taps_out // 2), 16) if rest else 0
    return blocks, rest, half, round_up(blocks * taps_out + half, 16 * count)


def vmem():
    return pl.BlockSpec(memory_space=pltpu.VMEM)


def copied():
    return pl.BlockSpec()


def anywhere():
    return pl.BlockSpec(memory_space=pl.ANY)


def smem():
    return pl.BlockSpec(memory_space=pltpu.SMEM)


def limit(taps_out, pixels):
    return pltpu.CompilerParams(vmem_limit_bytes=4 * MIB + 4 * taps_out * pixels)


def cost(rows, columns, depth):
    return pl.CostEstimate(
        flops=2 * rows * columns * depth,
        bytes_accessed=2 * (rows * depth + columns * depth),
        transcendentals=columns * depth,
    )


def gains(x_refs, start, group):
    found = []
    for ref in x_refs:
        rows = ref[pl.ds(start, 16), :].astype(jnp.float32)
        gain = rows[0:1] + rows[1:2] + rows[2:3]
        found.append(jnp.transpose(jnp.broadcast_to(gain, (128, 128)))[:group])
    return found


def norm(x_refs, t, group):
    values = [ref[pl.ds(t * group, group), :].astype(jnp.float32) for ref in x_refs]
    squares = sum(jnp.sum(value * value, axis=0, keepdims=True) for value in values)
    scale = lax.rsqrt(squares / CHANNELS + EPSILON)
    return scale, [value * scale for value in values]


def prepare_kernel(adjoint_ref, x_ref, gain_ref, strips_ref, payload_ref, lines, gain_rows):
    channels, height, width = adjoint_ref.shape
    frames = x_ref.shape[0]
    group = strips_ref.shape[2]
    lines[...] = adjoint_ref[...].astype(jnp.float32).reshape(channels * height, width)
    nothing = jnp.zeros((group, width), jnp.bfloat16)
    strips_ref[0, 0] = nothing
    strips_ref[height - 1, 2] = nothing
    for r in range(height):
        row = lines[pl.ds(r, channels, stride=height), :]
        if group > channels:
            row = jnp.concatenate(
                [row, jnp.zeros((group - channels, width), jnp.float32)], axis=0
            )
        row = row.astype(jnp.bfloat16)
        for k in range(3):
            if 0 <= r + 1 - k < height:
                strips_ref[r + 1 - k, k] = row
    for t in range(frames):
        values = x_ref[t]
        if group > channels:
            values = jnp.concatenate(
                [
                    values.astype(jnp.float32),
                    jnp.zeros((group - channels, width), jnp.float32),
                ],
                axis=0,
            ).astype(jnp.bfloat16)
        payload_ref[pl.ds(t * group, group), :] = values
    gain = gain_ref[...]
    high = gain.astype(jnp.bfloat16).astype(jnp.float32)
    middle = (gain - high).astype(jnp.bfloat16).astype(jnp.float32)
    gain_rows[...] = jnp.zeros_like(gain_rows)
    gain_rows[pl.ds(0, 1), pl.ds(0, channels)] = high
    gain_rows[pl.ds(1, 1), pl.ds(0, channels)] = middle
    gain_rows[pl.ds(2, 1), pl.ds(0, channels)] = gain - high - middle
    payload_ref[pl.ds(frames * group, 16), :] = gain_rows[...].astype(jnp.bfloat16)


def window_kernel(frames, group, slot_ref, adjoint_ref, windows, place):
    width = adjoint_ref.shape[-1]
    for slot in range(frames):
        place[slot_ref[slot]] = slot

    lane = lax.broadcasted_iota(jnp.int32, (group, width), 1)
    nothing = jnp.zeros((group, width), jnp.bfloat16)
    for a in range(2):
        for inner in range(9):
            for t in range(frames - 2 + a, frames):
                windows[pl.ds((a * 9 + inner) * group, group), pl.ds(t * width, width)] = nothing
    for frame in range(frames):
        slot = place[frame]
        for b in range(3):
            row = adjoint_ref[slot, 2 - b].astype(jnp.float32)
            after = jnp.where(lane == width - 1, 0.0, pltpu.roll(row, width - 1, 1))
            before = jnp.where(lane == 0, 0.0, pltpu.roll(row, 1, 1))
            for c, shifted in enumerate((after, row, before)):
                shifted = shifted.astype(jnp.bfloat16)
                for a in range(3):
                    t = frame + a - 2
                    if t >= 0:
                        windows[
                            pl.ds((a * 9 + b * 3 + c) * group, group), pl.ds(t * width, width)
                        ] = shifted

def grad_kernel(frames, group, factor, at_ref, windows, *refs):
    groups = len(refs) - 2
    x_refs = refs[:groups]
    grad_ref, hidden = refs[groups:]
    ins = groups * group
    width = windows.shape[1] // frames
    gain = gains(x_refs, frames * group, group)
    for t in range(frames):
        scale, scaled = norm(x_refs, t, group)
        for s in range(groups):
            normed = scaled[s] * gain[s]
            value = (normed * jax.nn.sigmoid(normed)).astype(jnp.bfloat16)
            start = pl.multiple_of((at_ref[0] ^ s) * group, 16)
            hidden[pl.ds(start, group), pl.ds(t * width, width)] = value

    grad = lax.dot_general(
        windows[...], hidden[...], (((1,), (1,)), ((), ())), preferred_element_type=jnp.float32
    )
    grad = grad * factor
    taps_out = grad.shape[0]
    blocks, rest, half, rows = packing(taps_out, ins, 1)
    for block in range(blocks):
        grad_ref[pl.ds(block * taps_out, taps_out), :] = grad[
            :, block * 128 : block * 128 + 128
        ].astype(jnp.bfloat16)
    base = blocks * taps_out
    if rest:
        left = grad[:half, blocks * 128 :]
        right = grad[half:, blocks * 128 :]
        right = jnp.concatenate(
            [right, jnp.zeros((2 * half - taps_out, rest), jnp.float32)], axis=0
        )
        grad_ref[pl.ds(base, half), :] = jnp.concatenate([left, right], axis=1).astype(
            jnp.bfloat16
        )
        base = base + half
    tail = grad_ref.shape[0] - base
    if tail:
        grad_ref[pl.ds(base, tail), :] = jnp.zeros((tail, 128), jnp.bfloat16)


def part_kernel(frames, group, at_ref, weight_ref, windows, *refs):
    groups = (len(refs) - 1) // 2
    x_refs = refs[:groups]
    part_refs = refs[groups : 2 * groups]
    product = refs[2 * groups]
    width = part_refs[0].shape[-1]
    product[...] = lax.dot_general(
        weight_ref[...], windows[...], (((0,), (0,)), ((), ())), preferred_element_type=jnp.float32
    )
    gain = gains(x_refs, frames * group, group)
    shares = []
    for t in range(frames):
        scale, scaled = norm(x_refs, t, group)
        part_refs[0][pl.ds(frames * group + t, 1), :] = scale
        share = jnp.zeros((1, width), jnp.float32)
        for s in range(groups):
            normed = scaled[s] * gain[s]
            sigma = jax.nn.sigmoid(normed)
            slope = sigma * (1.0 + normed * (1.0 - sigma)) * gain[s]
            start = pl.multiple_of((at_ref[0] ^ s) * group, 16)
            term = product[pl.ds(start, group), pl.ds(t * width, width)] * slope * scale
            part_refs[s][pl.ds(t * group, group), :] = term.astype(part_refs[s].dtype)
            share = share + jnp.sum(term * scaled[s], axis=0, keepdims=True)
        shares.append(share)
    share = jnp.concatenate(shares, axis=0)
    part_refs[0][pl.ds(frames * group + frames, frames), :] = share
    high = share.astype(jnp.bfloat16).astype(jnp.float32)
    both = [high, share - high]
    unused = round_up(2 * frames, 16) - 2 * frames
    if unused:
        both.append(jnp.zeros((unused, width), jnp.float32))
    both = jnp.concatenate(both, axis=0).astype(jnp.bfloat16)
    for s in range(1, groups):
        part_refs[s][pl.ds(frames * group, both.shape[0]), :] = both


def finish_kernel(frames, group, packed_ref, x_ref, *refs):
    own_ref, others = refs[0], refs[1:-5]
    out_hbm, grad_hbm, out_ref, grad_ref, done = refs[-5:]
    taps_out, ins = grad_ref.shape
    blocks, rest, half, rows = packing(taps_out, ins, 1)

    share = own_ref[pl.ds(frames * group + frames, frames), :]
    for ref in others:
        both = ref[pl.ds(frames * group, round_up(2 * frames, 16)), :].astype(jnp.float32)
        share = share + both[:frames] + both[frames : 2 * frames]
    share = share / CHANNELS
    for t in range(frames):
        term = own_ref[pl.ds(t * group, group), :]
        for ref in others:
            term = term + ref[pl.ds(t * group, group), :].astype(jnp.float32)
        scale = own_ref[pl.ds(frames * group + t, 1), :]
        scaled = x_ref[pl.ds(t * group, group), :].astype(jnp.float32) * scale
        out_ref[t] = (term - scaled * share[t : t + 1]).astype(jnp.bfloat16)
    copies = [pltpu.make_async_copy(out_ref, out_hbm, done.at[0])]
    copies[0].start()

    part = taps_out // 3
    for p in range(3):
        first = p * part
        for block in range(blocks):
            grad_ref[pl.ds(first, part), pl.ds(block * 128, 128)] = packed_ref[
                pl.ds(block * taps_out + first, part), :
            ].astype(jnp.float32)
        if rest:
            for begin, end, low in ((0, half, 0), (half, taps_out, rest)):
                begin, end = max(begin, first), min(end, first + part)
                if begin < end:
                    shift = half if low else 0
                    grad_ref[pl.ds(begin, end - begin), pl.ds(blocks * 128, rest)] = packed_ref[
                        pl.ds(blocks * taps_out + begin - shift, end - begin), :
                    ].astype(jnp.float32)[:, low : low + rest]
        copies.append(
            pltpu.make_async_copy(
                grad_ref.at[pl.ds(first, part)], grad_hbm.at[pl.ds(first, part)], done.at[p + 1]
            )
        )
        copies[-1].start()
    for copy in copies:
        copy.wait()


def shards(frame_adjoint, frame_slot, inputs, gain, weight):
    count = lax.axis_size("rows")
    groups = lax.axis_size("chan")
    frames, channels, _, width = inputs.shape
    group = round_up(channels, 16)
    spare = group - channels
    ins = groups * group

    taps_out = 27 * group
    pixels = frames * width
    strips, payload = pl.pallas_call(
        prepare_kernel,
        out_shape=(
            jax.ShapeDtypeStruct((count, 3, group, width), jnp.bfloat16),
            jax.ShapeDtypeStruct((frames * group + 16, width), jnp.bfloat16),
        ),
        in_specs=[copied(), copied(), copied()],
        out_specs=(vmem(), vmem()),
        scratch_shapes=[
            pltpu.VMEM((channels * count, width), jnp.float32),
            pltpu.VMEM((16, width), jnp.float32),
        ],
        compiler_params=pltpu.CompilerParams(vmem_limit_bytes=60 * MIB),
        name="prepare_kernel",
    )(frame_adjoint[0], inputs[:, :, 0], gain.reshape(1, channels))
    partners = [[(z, z ^ s) for z in range(groups)] for s in range(groups)]
    everything = [payload] * groups
    for s in range(1, groups):
        everything[s] = lax.ppermute(everything[s & (s - 1)], "chan", partners[s & -s])
    strips = lax.all_to_all(strips, "rows", split_axis=0, concat_axis=0, tiled=True)
    at = lax.axis_index("chan").astype(jnp.int32).reshape(1)

    kernel = weight.reshape(27, channels, groups, channels)
    kernel = jnp.pad(kernel, ((0, 0), (0, spare), (0, 0), (0, spare)))
    kernel = kernel.reshape(27 * group, ins)

    packed_rows = packing(taps_out, ins, count)[3]
    factor = float(frames * count * width) ** (-0.5)
    windows = pl.pallas_call(
        functools.partial(window_kernel, frames, group),
        out_shape=jax.ShapeDtypeStruct((taps_out, pixels), jnp.bfloat16),
        in_specs=[smem(), copied()],
        out_specs=vmem(),
        scratch_shapes=[pltpu.SMEM((frames,), jnp.int32)],
        compiler_params=limit(taps_out, pixels),
        name="window_kernel",
    )(frame_slot, strips)
    packed = pl.pallas_call(
        functools.partial(grad_kernel, frames, group, factor),
        out_shape=jax.ShapeDtypeStruct((packed_rows, 128), jnp.bfloat16),
        in_specs=[smem(), vmem()] + [copied()] * groups,
        out_specs=vmem(),
        scratch_shapes=[pltpu.VMEM((ins, pixels), jnp.bfloat16)],
        compiler_params=limit(taps_out, pixels),
        cost_estimate=cost(taps_out, ins, pixels),
        name="grad_kernel",
    )(at, windows, *everything)

    pieces = lax.all_to_all(
        packed.reshape(count, packed_rows // count, 128),
        "rows", split_axis=0, concat_axis=0, tiled=True,
    )

    sent = frames * group + round_up(2 * frames, 16)
    parts = pl.pallas_call(
        functools.partial(part_kernel, frames, group),
        out_shape=tuple(
            [jax.ShapeDtypeStruct((frames * (group + 2), width), jnp.float32)]
            + [jax.ShapeDtypeStruct((sent, width), jnp.bfloat16)] * (groups - 1)
        ),
        in_specs=[smem(), vmem(), vmem()] + [copied()] * groups,
        out_specs=(vmem(),) * groups,
        scratch_shapes=[pltpu.VMEM((ins, pixels), jnp.float32)],
        compiler_params=limit(taps_out, pixels),
        cost_estimate=cost(taps_out, ins, pixels),
        name="part_kernel",
    )(at, kernel, windows, *everything)

    arrived = [lax.ppermute(parts[s], "chan", partners[s]) for s in range(1, groups)]
    summed = jnp.sum(pieces.astype(jnp.float32), axis=0).astype(jnp.bfloat16)
    whole = lax.all_gather(summed, "rows", axis=0, tiled=True)
    input_adjoint, grad = pl.pallas_call(
        functools.partial(finish_kernel, frames, group),
        out_shape=(
            jax.ShapeDtypeStruct((frames, group, width), jnp.bfloat16),
            jax.ShapeDtypeStruct((taps_out, ins), jnp.float32),
        ),
        in_specs=[vmem()] * (groups + 2),
        out_specs=(anywhere(), anywhere()),
        scratch_shapes=[
            pltpu.VMEM((frames, group, width), jnp.bfloat16),
            pltpu.VMEM((taps_out, ins), jnp.float32),
            pltpu.SemaphoreType.DMA((4,)),
        ],
        compiler_params=limit(taps_out, pixels),
        name="finish_kernel",
    )(whole, payload, parts[0], *arrived)
    grad = grad.reshape(27, group, groups, group)[:, :channels, :, :channels]
    return (
        input_adjoint[:, :channels, None, :],
        grad.reshape(27, channels, groups * channels),
    )


def solution(mesh):
    in_specs = (
        P("rows", "chan", None, None),
        P(),
        P(None, "chan", "rows", None),
        P("chan"),
        P(None, "chan", None),
    )
    out_specs = (P(None, "chan", "rows", None), P(None, "chan", None))
    return jax.shard_map(shards, mesh=mesh, in_specs=in_specs, out_specs=out_specs, check_vma=False)
```

```python
import functools

import jax
import jax.numpy as jnp
from jax import lax
from jax.experimental import pallas as pl
from jax.experimental.pallas import tpu as pltpu
from jax.sharding import PartitionSpec as P

CHANNELS = 192
EPSILON = 1e-06
MIB = 1024 * 1024


def round_up(value, unit):
    return -(-value // unit) * unit


def packing(taps_out, ins, count):
    blocks, rest = divmod(ins, 128)
    half = round_up(-(-taps_out // 2), 16) if rest else 0
    return blocks, rest, half, round_up(blocks * taps_out + half, 16 * count)


def vmem():
    return pl.BlockSpec(memory_space=pltpu.VMEM)


def copied():
    return pl.BlockSpec()


def anywhere():
    return pl.BlockSpec(memory_space=pl.ANY)


def smem():
    return pl.BlockSpec(memory_space=pltpu.SMEM)


def limit(taps_out, pixels):
    return pltpu.CompilerParams(vmem_limit_bytes=10 * MIB + 6 * taps_out * pixels)


def cost(rows, columns, depth):
    return pl.CostEstimate(
        flops=2 * rows * columns * depth,
        bytes_accessed=2 * (rows * depth + columns * depth),
        transcendentals=columns * depth,
    )


def gains(x_refs, start, group):
    found = []
    for ref in x_refs:
        rows = ref[pl.ds(start, 16), :].astype(jnp.float32)
        gain = rows[0:1] + rows[1:2] + rows[2:3]
        found.append(jnp.transpose(jnp.broadcast_to(gain, (128, 128)))[:group])
    return found


def norm(x_refs, t, group):
    values = [ref[pl.ds(t * group, group), :].astype(jnp.float32) for ref in x_refs]
    squares = sum(jnp.sum(value * value, axis=0, keepdims=True) for value in values)
    scale = lax.rsqrt(squares / CHANNELS + EPSILON)
    return scale, [value * scale for value in values]


def prepare_kernel(
    frames, adjoint_hbm, x_hbm, gain_hbm, strips_hbm, payload_hbm,
    held, lines, values, gain, gain_rows, strips, payload, moved,
):
    channels, height, width = held.shape
    group = strips.shape[2]
    last = frames * group
    direct = group == channels
    arriving = [
        pltpu.make_async_copy(adjoint_hbm, held, moved.at[0]),
        pltpu.make_async_copy(
            x_hbm, payload.at[pl.ds(0, last)] if direct else values, moved.at[1]
        ),
        pltpu.make_async_copy(gain_hbm, gain, moved.at[2]),
    ]
    for copy in arriving:
        copy.start()

    arriving[0].wait()
    lines[...] = held[...].astype(jnp.float32).reshape(channels * height, width)
    nothing = jnp.zeros((group, width), jnp.bfloat16)
    strips[0, 0] = nothing
    strips[height - 1, 2] = nothing
    for r in range(height):
        row = lines[pl.ds(r, channels, stride=height), :]
        if not direct:
            row = jnp.concatenate(
                [row, jnp.zeros((group - channels, width), jnp.float32)], axis=0
            )
        row = row.astype(jnp.bfloat16)
        for k in range(3):
            if 0 <= r + 1 - k < height:
                strips[r + 1 - k, k] = row
    leaving = [pltpu.make_async_copy(strips, strips_hbm, moved.at[3])]
    leaving[0].start()

    arriving[1].wait()
    arriving[2].wait()
    if not direct:
        for t in range(frames):
            payload[pl.ds(t * group, group), :] = jnp.concatenate(
                [
                    values[t].astype(jnp.float32),
                    jnp.zeros((group - channels, width), jnp.float32),
                ],
                axis=0,
            ).astype(jnp.bfloat16)
    high = gain[...].astype(jnp.bfloat16).astype(jnp.float32)
    middle = (gain[...] - high).astype(jnp.bfloat16).astype(jnp.float32)
    gain_rows[...] = jnp.zeros_like(gain_rows)
    gain_rows[pl.ds(0, 1), pl.ds(0, channels)] = high
    gain_rows[pl.ds(1, 1), pl.ds(0, channels)] = middle
    gain_rows[pl.ds(2, 1), pl.ds(0, channels)] = gain[...] - high - middle
    payload[pl.ds(last, 16), :] = gain_rows[...].astype(jnp.bfloat16)
    leaving.append(pltpu.make_async_copy(payload, payload_hbm, moved.at[4]))
    leaving[1].start()
    for copy in leaving:
        copy.wait()


def window_kernel(frames, group, slot_ref, adjoint_ref, windows, place):
    width = adjoint_ref.shape[-1]
    for slot in range(frames):
        place[slot_ref[slot]] = slot

    lane = lax.broadcasted_iota(jnp.int32, (group, width), 1)
    nothing = jnp.zeros((group, width), jnp.bfloat16)
    for a in range(2):
        for inner in range(9):
            for t in range(frames - 2 + a, frames):
                windows[pl.ds((a * 9 + inner) * group, group), pl.ds(t * width, width)] = nothing
    for frame in range(frames):
        slot = place[frame]
        for b in range(3):
            row = adjoint_ref[slot, 2 - b].astype(jnp.float32)
            after = jnp.where(lane == width - 1, 0.0, pltpu.roll(row, width - 1, 1))
            before = jnp.where(lane == 0, 0.0, pltpu.roll(row, 1, 1))
            for c, shifted in enumerate((after, row, before)):
                shifted = shifted.astype(jnp.bfloat16)
                for a in range(3):
                    t = frame + a - 2
                    if t >= 0:
                        windows[
                            pl.ds((a * 9 + b * 3 + c) * group, group), pl.ds(t * width, width)
                        ] = shifted

def grad_kernel(frames, group, factor, at_ref, windows, *refs):
    groups = len(refs) - 2
    x_refs = refs[:groups]
    grad_ref, hidden = refs[groups:]
    ins = groups * group
    width = windows.shape[1] // frames
    gain = gains(x_refs, frames * group, group)
    for t in range(frames):
        scale, scaled = norm(x_refs, t, group)
        for s in range(groups):
            normed = scaled[s] * gain[s]
            value = (normed * jax.nn.sigmoid(normed)).astype(jnp.bfloat16)
            start = pl.multiple_of((at_ref[0] ^ s) * group, 16)
            hidden[pl.ds(start, group), pl.ds(t * width, width)] = value

    grad = lax.dot_general(
        windows[...], hidden[...], (((1,), (1,)), ((), ())), preferred_element_type=jnp.float32
    )
    grad = grad * factor
    taps_out = grad.shape[0]
    blocks, rest, half, rows = packing(taps_out, ins, 1)
    for block in range(blocks):
        grad_ref[pl.ds(block * taps_out, taps_out), :] = grad[
            :, block * 128 : block * 128 + 128
        ].astype(jnp.bfloat16)
    base = blocks * taps_out
    if rest:
        left = grad[:half, blocks * 128 :]
        right = grad[half:, blocks * 128 :]
        right = jnp.concatenate(
            [right, jnp.zeros((2 * half - taps_out, rest), jnp.float32)], axis=0
        )
        grad_ref[pl.ds(base, half), :] = jnp.concatenate([left, right], axis=1).astype(
            jnp.bfloat16
        )
        base = base + half
    tail = grad_ref.shape[0] - base
    if tail:
        grad_ref[pl.ds(base, tail), :] = jnp.zeros((tail, 128), jnp.bfloat16)


def part_kernel(frames, group, at_ref, weight_ref, windows, *refs):
    groups = (len(refs) - 1) // 2
    x_refs = refs[:groups]
    part_refs = refs[groups : 2 * groups]
    product = refs[2 * groups]
    width = part_refs[0].shape[-1]
    product[...] = lax.dot_general(
        weight_ref[...], windows[...], (((0,), (0,)), ((), ())), preferred_element_type=jnp.float32
    )
    gain = gains(x_refs, frames * group, group)
    shares = []
    for t in range(frames):
        scale, scaled = norm(x_refs, t, group)
        part_refs[0][pl.ds(frames * group + t, 1), :] = scale
        share = jnp.zeros((1, width), jnp.float32)
        for s in range(groups):
            normed = scaled[s] * gain[s]
            sigma = jax.nn.sigmoid(normed)
            slope = sigma * (1.0 + normed * (1.0 - sigma)) * gain[s]
            start = pl.multiple_of((at_ref[0] ^ s) * group, 16)
            term = product[pl.ds(start, group), pl.ds(t * width, width)] * slope * scale
            part_refs[s][pl.ds(t * group, group), :] = term.astype(part_refs[s].dtype)
            share = share + jnp.sum(term * scaled[s], axis=0, keepdims=True)
        shares.append(share)
    share = jnp.concatenate(shares, axis=0)
    part_refs[0][pl.ds(frames * group + frames, frames), :] = share
    high = share.astype(jnp.bfloat16).astype(jnp.float32)
    both = [high, share - high]
    unused = round_up(2 * frames, 16) - 2 * frames
    if unused:
        both.append(jnp.zeros((unused, width), jnp.float32))
    both = jnp.concatenate(both, axis=0).astype(jnp.bfloat16)
    for s in range(1, groups):
        part_refs[s][pl.ds(frames * group, both.shape[0]), :] = both


def finish_kernel(frames, group, packed_ref, x_ref, *refs):
    own_ref, others, (out_ref, grad_ref) = refs[0], refs[1:-2], refs[-2:]
    taps_out, ins = grad_ref.shape
    blocks, rest, half, rows = packing(taps_out, ins, 1)
    for block in range(blocks):
        grad_ref[:, pl.ds(block * 128, 128)] = packed_ref[
            pl.ds(block * taps_out, taps_out), :
        ].astype(jnp.float32)
    if rest:
        both = packed_ref[pl.ds(blocks * taps_out, half), :].astype(jnp.float32)
        grad_ref[pl.ds(0, half), pl.ds(blocks * 128, rest)] = both[:, :rest]
        grad_ref[pl.ds(half, taps_out - half), pl.ds(blocks * 128, rest)] = both[
            : taps_out - half, rest:
        ]

    share = own_ref[pl.ds(frames * group + frames, frames), :]
    for ref in others:
        both = ref[pl.ds(frames * group, round_up(2 * frames, 16)), :].astype(jnp.float32)
        share = share + both[:frames] + both[frames : 2 * frames]
    share = share / CHANNELS
    for t in range(frames):
        term = own_ref[pl.ds(t * group, group), :]
        for ref in others:
            term = term + ref[pl.ds(t * group, group), :].astype(jnp.float32)
        scale = own_ref[pl.ds(frames * group + t, 1), :]
        scaled = x_ref[pl.ds(t * group, group), :].astype(jnp.float32) * scale
        out_ref[t] = (term - scaled * share[t : t + 1]).astype(jnp.bfloat16)


def shards(frame_adjoint, frame_slot, inputs, gain, weight):
    count = lax.axis_size("rows")
    groups = lax.axis_size("chan")
    frames, channels, _, width = inputs.shape
    group = round_up(channels, 16)
    spare = group - channels
    ins = groups * group

    taps_out = 27 * group
    pixels = frames * width
    sent = inputs[:, :, 0] if spare else inputs.reshape(frames * channels, width)
    strips, payload = pl.pallas_call(
        functools.partial(prepare_kernel, frames),
        out_shape=(
            jax.ShapeDtypeStruct((count, 3, group, width), jnp.bfloat16),
            jax.ShapeDtypeStruct((frames * group + 16, width), jnp.bfloat16),
        ),
        in_specs=[anywhere(), anywhere(), anywhere()],
        out_specs=(anywhere(), anywhere()),
        scratch_shapes=[
            pltpu.VMEM((channels, count, width), jnp.bfloat16),
            pltpu.VMEM((channels * count, width), jnp.float32),
            pltpu.VMEM(sent.shape if spare else (16, width), jnp.bfloat16),
            pltpu.VMEM((1, channels), jnp.float32),
            pltpu.VMEM((16, width), jnp.float32),
            pltpu.VMEM((count, 3, group, width), jnp.bfloat16),
            pltpu.VMEM((frames * group + 16, width), jnp.bfloat16),
            pltpu.SemaphoreType.DMA((5,)),
        ],
        compiler_params=pltpu.CompilerParams(vmem_limit_bytes=60 * MIB),
        name="prepare_kernel",
    )(frame_adjoint[0], sent, gain.reshape(1, channels))

    partners = [[(z, z ^ s) for z in range(groups)] for s in range(groups)]
    everything = [payload] * groups
    for s in range(1, groups):
        everything[s] = lax.ppermute(everything[s & (s - 1)], "chan", partners[s & -s])
    gate = min(2, groups - 1)
    strips, everything[gate] = lax.optimization_barrier((strips, everything[gate]))
    strips = lax.all_to_all(strips, "rows", split_axis=0, concat_axis=0, tiled=True)
    at = lax.axis_index("chan").astype(jnp.int32).reshape(1)

    kernel = weight.reshape(27, channels, groups, channels)
    kernel = jnp.pad(kernel, ((0, 0), (0, spare), (0, 0), (0, spare)))
    kernel = kernel.reshape(27 * group, ins)

    packed_rows = packing(taps_out, ins, count)[3]
    factor = float(frames * count * width) ** (-0.5)
    windows = pl.pallas_call(
        functools.partial(window_kernel, frames, group),
        out_shape=jax.ShapeDtypeStruct((taps_out, pixels), jnp.bfloat16),
        in_specs=[smem(), copied()],
        out_specs=vmem(),
        scratch_shapes=[pltpu.SMEM((frames,), jnp.int32)],
        compiler_params=limit(taps_out, pixels),
        name="window_kernel",
    )(frame_slot, strips)
    packed = pl.pallas_call(
        functools.partial(grad_kernel, frames, group, factor),
        out_shape=jax.ShapeDtypeStruct((packed_rows, 128), jnp.bfloat16),
        in_specs=[smem(), vmem()] + [copied()] * groups,
        out_specs=vmem(),
        scratch_shapes=[pltpu.VMEM((ins, pixels), jnp.bfloat16)],
        compiler_params=limit(taps_out, pixels),
        cost_estimate=cost(taps_out, ins, pixels),
        name="grad_kernel",
    )(at, windows, *everything)

    pieces = lax.all_to_all(
        packed.reshape(count, packed_rows // count, 128),
        "rows", split_axis=0, concat_axis=0, tiled=True,
    )

    part_rows = frames * group + round_up(2 * frames, 16)
    parts = pl.pallas_call(
        functools.partial(part_kernel, frames, group),
        out_shape=tuple(
            [jax.ShapeDtypeStruct((frames * (group + 2), width), jnp.float32)]
            + [jax.ShapeDtypeStruct((part_rows, width), jnp.bfloat16)] * (groups - 1)
        ),
        in_specs=[smem(), vmem(), vmem()] + [copied()] * groups,
        out_specs=(vmem(),) * groups,
        scratch_shapes=[pltpu.VMEM((ins, pixels), jnp.float32)],
        compiler_params=limit(taps_out, pixels),
        cost_estimate=cost(taps_out, ins, pixels),
        name="part_kernel",
    )(at, kernel, windows, *everything)

    arrived = [lax.ppermute(parts[s], "chan", partners[s]) for s in range(1, groups)]
    summed = jnp.sum(pieces.astype(jnp.float32), axis=0).astype(jnp.bfloat16)
    whole = lax.all_gather(summed, "rows", axis=0, tiled=True)
    input_adjoint, grad = pl.pallas_call(
        functools.partial(finish_kernel, frames, group),
        out_shape=(
            jax.ShapeDtypeStruct((frames, group, width), jnp.bfloat16),
            jax.ShapeDtypeStruct((taps_out, ins), jnp.float32),
        ),
        in_specs=[copied()] * (groups + 2),
        out_specs=(vmem(), vmem()),
        compiler_params=limit(taps_out, pixels),
        name="finish_kernel",
    )(whole, payload, parts[0], *arrived)
    grad = grad.reshape(27, group, groups, group)[:, :channels, :, :channels]
    return (
        input_adjoint[:, :channels, None, :],
        grad.reshape(27, channels, groups * channels),
    )


def solution(mesh):
    in_specs = (
        P("rows", "chan", None, None),
        P(),
        P(None, "chan", "rows", None),
        P("chan"),
        P(None, "chan", None),
    )
    out_specs = (P(None, "chan", "rows", None), P(None, "chan", None))
    return jax.shard_map(shards, mesh=mesh, in_specs=in_specs, out_specs=out_specs, check_vma=False)
```

```python
import functools

import jax
import jax.numpy as jnp
from jax import lax
from jax.experimental import pallas as pl
from jax.experimental.pallas import tpu as pltpu
from jax.sharding import PartitionSpec as P

CHANNELS = 192
EPSILON = 1e-06
MIB = 1024 * 1024


def round_up(value, unit):
    return -(-value // unit) * unit


def packing(taps_out, ins, count):
    blocks, rest = divmod(ins, 128)
    half = round_up(-(-taps_out // 2), 16) if rest else 0
    return blocks, rest, half, round_up(blocks * taps_out + half, 16 * count)


def vmem():
    return pl.BlockSpec(memory_space=pltpu.VMEM)


def copied():
    return pl.BlockSpec()


def smem():
    return pl.BlockSpec(memory_space=pltpu.SMEM)


def limit(taps_out, pixels):
    return pltpu.CompilerParams(vmem_limit_bytes=10 * MIB + 6 * taps_out * pixels)


def cost(rows, columns, depth):
    return pl.CostEstimate(
        flops=2 * rows * columns * depth,
        bytes_accessed=2 * (rows * depth + columns * depth),
        transcendentals=columns * depth,
    )


def gains(x_refs, start, group):
    found = []
    for ref in x_refs:
        rows = ref[pl.ds(start, 16), :].astype(jnp.float32)
        gain = rows[0:1] + rows[1:2] + rows[2:3]
        found.append(jnp.transpose(jnp.broadcast_to(gain, (128, 128)))[:group])
    return found


def norm(x_refs, t, group):
    values = [ref[pl.ds(t * group, group), :].astype(jnp.float32) for ref in x_refs]
    squares = sum(jnp.sum(value * value, axis=0, keepdims=True) for value in values)
    scale = lax.rsqrt(squares / CHANNELS + EPSILON)
    return scale, [value * scale for value in values]


def prepare_kernel(adjoint_ref, x_ref, gain_ref, strips_ref, payload_ref, lines, gain_rows):
    channels, height, width = adjoint_ref.shape
    frames = x_ref.shape[0]
    group = strips_ref.shape[2]
    lines[...] = adjoint_ref[...].astype(jnp.float32).reshape(channels * height, width)
    nothing = jnp.zeros((group, width), jnp.bfloat16)
    strips_ref[0, 0] = nothing
    strips_ref[height - 1, 2] = nothing
    for r in range(height):
        row = lines[pl.ds(r, channels, stride=height), :]
        if group > channels:
            row = jnp.concatenate(
                [row, jnp.zeros((group - channels, width), jnp.float32)], axis=0
            )
        row = row.astype(jnp.bfloat16)
        for k in range(3):
            if 0 <= r + 1 - k < height:
                strips_ref[r + 1 - k, k] = row
    for t in range(frames):
        values = x_ref[t]
        if group > channels:
            values = jnp.concatenate(
                [
                    values.astype(jnp.float32),
                    jnp.zeros((group - channels, width), jnp.float32),
                ],
                axis=0,
            ).astype(jnp.bfloat16)
        payload_ref[pl.ds(t * group, group), :] = values
    gain = gain_ref[...]
    high = gain.astype(jnp.bfloat16).astype(jnp.float32)
    middle = (gain - high).astype(jnp.bfloat16).astype(jnp.float32)
    gain_rows[...] = jnp.zeros_like(gain_rows)
    gain_rows[pl.ds(0, 1), pl.ds(0, channels)] = high
    gain_rows[pl.ds(1, 1), pl.ds(0, channels)] = middle
    gain_rows[pl.ds(2, 1), pl.ds(0, channels)] = gain - high - middle
    payload_ref[pl.ds(frames * group, 16), :] = gain_rows[...].astype(jnp.bfloat16)


def window_kernel(frames, group, slot_ref, adjoint_ref, windows, place):
    width = adjoint_ref.shape[-1]
    for slot in range(frames):
        place[slot_ref[slot]] = slot

    lane = lax.broadcasted_iota(jnp.int32, (group, width), 1)
    nothing = jnp.zeros((group, width), jnp.bfloat16)
    for a in range(2):
        for inner in range(9):
            for t in range(frames - 2 + a, frames):
                windows[pl.ds((a * 9 + inner) * group, group), pl.ds(t * width, width)] = nothing
    for frame in range(frames):
        slot = place[frame]
        for b in range(3):
            row = adjoint_ref[slot, 2 - b].astype(jnp.float32)
            after = jnp.where(lane == width - 1, 0.0, pltpu.roll(row, width - 1, 1))
            before = jnp.where(lane == 0, 0.0, pltpu.roll(row, 1, 1))
            for c, shifted in enumerate((after, row, before)):
                shifted = shifted.astype(jnp.bfloat16)
                for a in range(3):
                    t = frame + a - 2
                    if t >= 0:
                        windows[
                            pl.ds((a * 9 + b * 3 + c) * group, group), pl.ds(t * width, width)
                        ] = shifted

def grad_kernel(frames, group, factor, at_ref, windows, *refs):
    groups = len(refs) - 2
    x_refs = refs[:groups]
    grad_ref, hidden = refs[groups:]
    ins = groups * group
    width = windows.shape[1] // frames
    gain = gains(x_refs, frames * group, group)
    for t in range(frames):
        scale, scaled = norm(x_refs, t, group)
        for s in range(groups):
            normed = scaled[s] * gain[s]
            value = (normed * jax.nn.sigmoid(normed)).astype(jnp.bfloat16)
            start = pl.multiple_of((at_ref[0] ^ s) * group, 16)
            hidden[pl.ds(start, group), pl.ds(t * width, width)] = value

    grad = lax.dot_general(
        windows[...], hidden[...], (((1,), (1,)), ((), ())), preferred_element_type=jnp.float32
    )
    grad = grad * factor
    taps_out = grad.shape[0]
    blocks, rest, half, rows = packing(taps_out, ins, 1)
    for block in range(blocks):
        grad_ref[pl.ds(block * taps_out, taps_out), :] = grad[
            :, block * 128 : block * 128 + 128
        ].astype(jnp.bfloat16)
    base = blocks * taps_out
    if rest:
        left = grad[:half, blocks * 128 :]
        right = grad[half:, blocks * 128 :]
        right = jnp.concatenate(
            [right, jnp.zeros((2 * half - taps_out, rest), jnp.float32)], axis=0
        )
        grad_ref[pl.ds(base, half), :] = jnp.concatenate([left, right], axis=1).astype(
            jnp.bfloat16
        )
        base = base + half
    tail = grad_ref.shape[0] - base
    if tail:
        grad_ref[pl.ds(base, tail), :] = jnp.zeros((tail, 128), jnp.bfloat16)


def part_kernel(frames, group, at_ref, weight_ref, windows, *refs):
    groups = (len(refs) - 1) // 2
    x_refs = refs[:groups]
    part_refs = refs[groups : 2 * groups]
    product = refs[2 * groups]
    width = part_refs[0].shape[-1]
    product[...] = lax.dot_general(
        weight_ref[...], windows[...], (((0,), (0,)), ((), ())), preferred_element_type=jnp.float32
    )
    gain = gains(x_refs, frames * group, group)
    shares = []
    for t in range(frames):
        scale, scaled = norm(x_refs, t, group)
        part_refs[0][pl.ds(frames * group + t, 1), :] = scale
        share = jnp.zeros((1, width), jnp.float32)
        for s in range(groups):
            normed = scaled[s] * gain[s]
            sigma = jax.nn.sigmoid(normed)
            slope = sigma * (1.0 + normed * (1.0 - sigma)) * gain[s]
            start = pl.multiple_of((at_ref[0] ^ s) * group, 16)
            term = product[pl.ds(start, group), pl.ds(t * width, width)] * slope * scale
            part_refs[s][pl.ds(t * group, group), :] = term.astype(part_refs[s].dtype)
            share = share + jnp.sum(term * scaled[s], axis=0, keepdims=True)
        shares.append(share)
    share = jnp.concatenate(shares, axis=0)
    part_refs[0][pl.ds(frames * group + frames, frames), :] = share
    high = share.astype(jnp.bfloat16).astype(jnp.float32)
    both = [high, share - high]
    unused = round_up(2 * frames, 16) - 2 * frames
    if unused:
        both.append(jnp.zeros((unused, width), jnp.float32))
    both = jnp.concatenate(both, axis=0).astype(jnp.bfloat16)
    for s in range(1, groups):
        part_refs[s][pl.ds(frames * group, both.shape[0]), :] = both


def finish_kernel(frames, group, packed_ref, x_ref, *refs):
    own_ref, others, (out_ref, grad_ref) = refs[0], refs[1:-2], refs[-2:]
    taps_out, ins = grad_ref.shape
    blocks, rest, half, rows = packing(taps_out, ins, 1)
    for block in range(blocks):
        grad_ref[:, pl.ds(block * 128, 128)] = packed_ref[
            pl.ds(block * taps_out, taps_out), :
        ].astype(jnp.float32)
    if rest:
        both = packed_ref[pl.ds(blocks * taps_out, half), :].astype(jnp.float32)
        grad_ref[pl.ds(0, half), pl.ds(blocks * 128, rest)] = both[:, :rest]
        grad_ref[pl.ds(half, taps_out - half), pl.ds(blocks * 128, rest)] = both[
            : taps_out - half, rest:
        ]

    share = own_ref[pl.ds(frames * group + frames, frames), :]
    for ref in others:
        both = ref[pl.ds(frames * group, round_up(2 * frames, 16)), :].astype(jnp.float32)
        share = share + both[:frames] + both[frames : 2 * frames]
    share = share / CHANNELS
    for t in range(frames):
        term = own_ref[pl.ds(t * group, group), :]
        for ref in others:
            term = term + ref[pl.ds(t * group, group), :].astype(jnp.float32)
        scale = own_ref[pl.ds(frames * group + t, 1), :]
        scaled = x_ref[pl.ds(t * group, group), :].astype(jnp.float32) * scale
        out_ref[t] = (term - scaled * share[t : t + 1]).astype(jnp.bfloat16)


def shards(frame_adjoint, frame_slot, inputs, gain, weight):
    count = lax.axis_size("rows")
    groups = lax.axis_size("chan")
    frames, channels, _, width = inputs.shape
    group = round_up(channels, 16)
    spare = group - channels
    ins = groups * group

    taps_out = 27 * group
    pixels = frames * width
    strips, payload = pl.pallas_call(
        prepare_kernel,
        out_shape=(
            jax.ShapeDtypeStruct((count, 3, group, width), jnp.bfloat16),
            jax.ShapeDtypeStruct((frames * group + 16, width), jnp.bfloat16),
        ),
        in_specs=[copied(), copied(), copied()],
        out_specs=(vmem(), vmem()),
        scratch_shapes=[
            pltpu.VMEM((channels * count, width), jnp.float32),
            pltpu.VMEM((16, width), jnp.float32),
        ],
        compiler_params=pltpu.CompilerParams(vmem_limit_bytes=60 * MIB),
        name="prepare_kernel",
    )(frame_adjoint[0], inputs[:, :, 0], gain.reshape(1, channels))
    partners = [[(z, z ^ s) for z in range(groups)] for s in range(groups)]
    everything = [payload] + [
        lax.ppermute(payload, "chan", partners[s]) for s in range(1, groups)
    ]
    strips = lax.cond(
        lax.axis_index("rows") < count,
        lambda rows: lax.all_to_all(rows, "rows", split_axis=0, concat_axis=0, tiled=True),
        lambda rows: rows,
        strips,
    )
    at = lax.axis_index("chan").astype(jnp.int32).reshape(1)

    kernel = weight.reshape(27, channels, groups, channels)
    kernel = jnp.pad(kernel, ((0, 0), (0, spare), (0, 0), (0, spare)))
    kernel = kernel.reshape(27 * group, ins)

    packed_rows = packing(taps_out, ins, count)[3]
    factor = float(frames * count * width) ** (-0.5)
    windows = pl.pallas_call(
        functools.partial(window_kernel, frames, group),
        out_shape=jax.ShapeDtypeStruct((taps_out, pixels), jnp.bfloat16),
        in_specs=[smem(), copied()],
        out_specs=vmem(),
        scratch_shapes=[pltpu.SMEM((frames,), jnp.int32)],
        compiler_params=limit(taps_out, pixels),
        name="window_kernel",
    )(frame_slot, strips)
    packed = pl.pallas_call(
        functools.partial(grad_kernel, frames, group, factor),
        out_shape=jax.ShapeDtypeStruct((packed_rows, 128), jnp.bfloat16),
        in_specs=[smem(), vmem()] + [copied()] * groups,
        out_specs=vmem(),
        scratch_shapes=[pltpu.VMEM((ins, pixels), jnp.bfloat16)],
        compiler_params=limit(taps_out, pixels),
        cost_estimate=cost(taps_out, ins, pixels),
        name="grad_kernel",
    )(at, windows, *everything)

    pieces = lax.all_to_all(
        packed.reshape(count, packed_rows // count, 128),
        "rows", split_axis=0, concat_axis=0, tiled=True,
    )

    sent = frames * group + round_up(2 * frames, 16)
    parts = pl.pallas_call(
        functools.partial(part_kernel, frames, group),
        out_shape=tuple(
            [jax.ShapeDtypeStruct((frames * (group + 2), width), jnp.float32)]
            + [jax.ShapeDtypeStruct((sent, width), jnp.bfloat16)] * (groups - 1)
        ),
        in_specs=[smem(), vmem(), vmem()] + [copied()] * groups,
        out_specs=(vmem(),) * groups,
        scratch_shapes=[pltpu.VMEM((ins, pixels), jnp.float32)],
        compiler_params=limit(taps_out, pixels),
        cost_estimate=cost(taps_out, ins, pixels),
        name="part_kernel",
    )(at, kernel, windows, *everything)

    arrived = [lax.ppermute(parts[s], "chan", partners[s]) for s in range(1, groups)]
    summed = jnp.sum(pieces.astype(jnp.float32), axis=0).astype(jnp.bfloat16)
    whole = lax.all_gather(summed, "rows", axis=0, tiled=True)
    input_adjoint, grad = pl.pallas_call(
        functools.partial(finish_kernel, frames, group),
        out_shape=(
            jax.ShapeDtypeStruct((frames, group, width), jnp.bfloat16),
            jax.ShapeDtypeStruct((taps_out, ins), jnp.float32),
        ),
        in_specs=[copied()] * (groups + 2),
        out_specs=(vmem(), vmem()),
        compiler_params=limit(taps_out, pixels),
        name="finish_kernel",
    )(whole, payload, parts[0], *arrived)
    grad = grad.reshape(27, group, groups, group)[:, :channels, :, :channels]
    return (
        input_adjoint[:, :channels, None, :],
        grad.reshape(27, channels, groups * channels),
    )


def solution(mesh):
    in_specs = (
        P("rows", "chan", None, None),
        P(),
        P(None, "chan", "rows", None),
        P("chan"),
        P(None, "chan", None),
    )
    out_specs = (P(None, "chan", "rows", None), P(None, "chan", None))
    return jax.shard_map(shards, mesh=mesh, in_specs=in_specs, out_specs=out_specs, check_vma=False)
```

```python
import functools

import jax
import jax.numpy as jnp
from jax import lax
from jax.experimental import pallas as pl
from jax.experimental.pallas import tpu as pltpu
from jax.sharding import PartitionSpec as P

CHANNELS = 192
EPSILON = 1e-06
MIB = 1024 * 1024


def round_up(value, unit):
    return -(-value // unit) * unit


def packing(taps_out, ins, count):
    blocks, rest = divmod(ins, 128)
    half = round_up(-(-taps_out // 2), 16) if rest else 0
    return blocks, rest, half, round_up(blocks * taps_out + half, 16 * count)


def vmem():
    return pl.BlockSpec(memory_space=pltpu.VMEM)


def copied():
    return pl.BlockSpec()


def smem():
    return pl.BlockSpec(memory_space=pltpu.SMEM)


def limit(taps_out, pixels):
    return pltpu.CompilerParams(vmem_limit_bytes=10 * MIB + 6 * taps_out * pixels)


def cost(rows, columns, depth):
    return pl.CostEstimate(
        flops=2 * rows * columns * depth,
        bytes_accessed=2 * (rows * depth + columns * depth),
        transcendentals=columns * depth,
    )


def grouped(x_refs, pieces):
    found, start = [], 0
    for count in pieces:
        found.append(x_refs[start : start + count])
        start += count
    return found


def frame_of(refs, t, frames, group):
    share = frames // len(refs)
    return refs[t // share][pl.ds(t % share * group, group), :].astype(jnp.float32)


def gains(x_groups, frames, group):
    found = []
    for refs in x_groups:
        rows = refs[0][pl.ds(frames // len(refs) * group, 16), :].astype(jnp.float32)
        gain = rows[0:1] + rows[1:2] + rows[2:3]
        found.append(jnp.transpose(jnp.broadcast_to(gain, (128, 128)))[:group])
    return found


def norm(x_groups, t, frames, group):
    values = [frame_of(refs, t, frames, group) for refs in x_groups]
    squares = sum(jnp.sum(value * value, axis=0, keepdims=True) for value in values)
    scale = lax.rsqrt(squares / CHANNELS + EPSILON)
    return scale, [value * scale for value in values]


def prepare_kernel(
    adjoint_ref, x_ref, gain_ref, strips_ref, payload_ref, first_ref, second_ref, lines, gain_rows
):
    channels, height, width = adjoint_ref.shape
    frames = x_ref.shape[0]
    group = strips_ref.shape[2]
    lines[...] = adjoint_ref[...].astype(jnp.float32).reshape(channels * height, width)
    nothing = jnp.zeros((group, width), jnp.bfloat16)
    strips_ref[0, 0] = nothing
    strips_ref[height - 1, 2] = nothing
    for r in range(height):
        row = lines[pl.ds(r, channels, stride=height), :]
        if group > channels:
            row = jnp.concatenate(
                [row, jnp.zeros((group - channels, width), jnp.float32)], axis=0
            )
        row = row.astype(jnp.bfloat16)
        for k in range(3):
            if 0 <= r + 1 - k < height:
                strips_ref[r + 1 - k, k] = row
    for t in range(frames):
        values = x_ref[t]
        if group > channels:
            values = jnp.concatenate(
                [
                    values.astype(jnp.float32),
                    jnp.zeros((group - channels, width), jnp.float32),
                ],
                axis=0,
            ).astype(jnp.bfloat16)
        payload_ref[pl.ds(t * group, group), :] = values
        half_ref = first_ref if t < frames // 2 else second_ref
        half_ref[pl.ds(t % (frames // 2) * group, group), :] = values
    gain = gain_ref[...]
    high = gain.astype(jnp.bfloat16).astype(jnp.float32)
    middle = (gain - high).astype(jnp.bfloat16).astype(jnp.float32)
    gain_rows[...] = jnp.zeros_like(gain_rows)
    gain_rows[pl.ds(0, 1), pl.ds(0, channels)] = high
    gain_rows[pl.ds(1, 1), pl.ds(0, channels)] = middle
    gain_rows[pl.ds(2, 1), pl.ds(0, channels)] = gain - high - middle
    for ref, start in ((payload_ref, frames * group), (first_ref, frames // 2 * group)):
        ref[pl.ds(start, 16), :] = gain_rows[...].astype(jnp.bfloat16)


def window_kernel(frames, group, slot_ref, adjoint_ref, windows, place):
    width = adjoint_ref.shape[-1]
    for slot in range(frames):
        place[slot_ref[slot]] = slot

    lane = lax.broadcasted_iota(jnp.int32, (group, width), 1)
    nothing = jnp.zeros((group, width), jnp.bfloat16)
    for a in range(2):
        for inner in range(9):
            for t in range(frames - 2 + a, frames):
                windows[pl.ds((a * 9 + inner) * group, group), pl.ds(t * width, width)] = nothing
    for frame in range(frames):
        slot = place[frame]
        for b in range(3):
            row = adjoint_ref[slot, 2 - b].astype(jnp.float32)
            after = jnp.where(lane == width - 1, 0.0, pltpu.roll(row, width - 1, 1))
            before = jnp.where(lane == 0, 0.0, pltpu.roll(row, 1, 1))
            for c, shifted in enumerate((after, row, before)):
                shifted = shifted.astype(jnp.bfloat16)
                for a in range(3):
                    t = frame + a - 2
                    if t >= 0:
                        windows[
                            pl.ds((a * 9 + b * 3 + c) * group, group), pl.ds(t * width, width)
                        ] = shifted

def grad_kernel(frames, group, pieces, factor, at_ref, windows, *refs):
    groups = len(pieces)
    x_groups = grouped(refs, pieces)
    grad_ref, hidden = refs[sum(pieces) :]
    ins = groups * group
    width = windows.shape[1] // frames
    gain = gains(x_groups, frames, group)
    for t in range(frames):
        scale, scaled = norm(x_groups, t, frames, group)
        for s in range(groups):
            normed = scaled[s] * gain[s]
            value = (normed * jax.nn.sigmoid(normed)).astype(jnp.bfloat16)
            start = pl.multiple_of((at_ref[0] ^ s) * group, 16)
            hidden[pl.ds(start, group), pl.ds(t * width, width)] = value

    grad = lax.dot_general(
        windows[...], hidden[...], (((1,), (1,)), ((), ())), preferred_element_type=jnp.float32
    )
    grad = grad * factor
    taps_out = grad.shape[0]
    blocks, rest, half, rows = packing(taps_out, ins, 1)
    for block in range(blocks):
        grad_ref[pl.ds(block * taps_out, taps_out), :] = grad[
            :, block * 128 : block * 128 + 128
        ].astype(jnp.bfloat16)
    base = blocks * taps_out
    if rest:
        left = grad[:half, blocks * 128 :]
        right = grad[half:, blocks * 128 :]
        right = jnp.concatenate(
            [right, jnp.zeros((2 * half - taps_out, rest), jnp.float32)], axis=0
        )
        grad_ref[pl.ds(base, half), :] = jnp.concatenate([left, right], axis=1).astype(
            jnp.bfloat16
        )
        base = base + half
    tail = grad_ref.shape[0] - base
    if tail:
        grad_ref[pl.ds(base, tail), :] = jnp.zeros((tail, 128), jnp.bfloat16)


def part_kernel(frames, group, pieces, at_ref, weight_ref, windows, *refs):
    groups, given = len(pieces), sum(pieces)
    x_groups = grouped(refs, pieces)
    part_refs = refs[given : given + groups]
    product = refs[given + groups]
    width = part_refs[0].shape[-1]
    product[...] = lax.dot_general(
        weight_ref[...], windows[...], (((0,), (0,)), ((), ())), preferred_element_type=jnp.float32
    )
    gain = gains(x_groups, frames, group)
    shares = []
    for t in range(frames):
        scale, scaled = norm(x_groups, t, frames, group)
        part_refs[0][pl.ds(frames * group + t, 1), :] = scale
        share = jnp.zeros((1, width), jnp.float32)
        for s in range(groups):
            normed = scaled[s] * gain[s]
            sigma = jax.nn.sigmoid(normed)
            slope = sigma * (1.0 + normed * (1.0 - sigma)) * gain[s]
            start = pl.multiple_of((at_ref[0] ^ s) * group, 16)
            term = product[pl.ds(start, group), pl.ds(t * width, width)] * slope * scale
            part_refs[s][pl.ds(t * group, group), :] = term.astype(part_refs[s].dtype)
            share = share + jnp.sum(term * scaled[s], axis=0, keepdims=True)
        shares.append(share)
    share = jnp.concatenate(shares, axis=0)
    part_refs[0][pl.ds(frames * group + frames, frames), :] = share
    high = share.astype(jnp.bfloat16).astype(jnp.float32)
    both = [high, share - high]
    unused = round_up(2 * frames, 16) - 2 * frames
    if unused:
        both.append(jnp.zeros((unused, width), jnp.float32))
    both = jnp.concatenate(both, axis=0).astype(jnp.bfloat16)
    for s in range(1, groups):
        part_refs[s][pl.ds(frames * group, both.shape[0]), :] = both


def finish_kernel(frames, group, packed_ref, x_ref, *refs):
    own_ref, others, (out_ref, grad_ref) = refs[0], refs[1:-2], refs[-2:]
    taps_out, ins = grad_ref.shape
    blocks, rest, half, rows = packing(taps_out, ins, 1)
    for block in range(blocks):
        grad_ref[:, pl.ds(block * 128, 128)] = packed_ref[
            pl.ds(block * taps_out, taps_out), :
        ].astype(jnp.float32)
    if rest:
        both = packed_ref[pl.ds(blocks * taps_out, half), :].astype(jnp.float32)
        grad_ref[pl.ds(0, half), pl.ds(blocks * 128, rest)] = both[:, :rest]
        grad_ref[pl.ds(half, taps_out - half), pl.ds(blocks * 128, rest)] = both[
            : taps_out - half, rest:
        ]

    share = own_ref[pl.ds(frames * group + frames, frames), :]
    for ref in others:
        both = ref[pl.ds(frames * group, round_up(2 * frames, 16)), :].astype(jnp.float32)
        share = share + both[:frames] + both[frames : 2 * frames]
    share = share / CHANNELS
    for t in range(frames):
        term = own_ref[pl.ds(t * group, group), :]
        for ref in others:
            term = term + ref[pl.ds(t * group, group), :].astype(jnp.float32)
        scale = own_ref[pl.ds(frames * group + t, 1), :]
        scaled = x_ref[pl.ds(t * group, group), :].astype(jnp.float32) * scale
        out_ref[t] = (term - scaled * share[t : t + 1]).astype(jnp.bfloat16)


def shards(frame_adjoint, frame_slot, inputs, gain, weight):
    count = lax.axis_size("rows")
    groups = lax.axis_size("chan")
    frames, channels, _, width = inputs.shape
    group = round_up(channels, 16)
    spare = group - channels
    ins = groups * group

    taps_out = 27 * group
    pixels = frames * width
    half = frames // 2 * group
    strips, payload, *halves = pl.pallas_call(
        prepare_kernel,
        out_shape=(
            jax.ShapeDtypeStruct((count, 3, group, width), jnp.bfloat16),
            jax.ShapeDtypeStruct((frames * group + 16, width), jnp.bfloat16),
            jax.ShapeDtypeStruct((half + 16, width), jnp.bfloat16),
            jax.ShapeDtypeStruct((half, width), jnp.bfloat16),
        ),
        in_specs=[copied(), copied(), copied()],
        out_specs=(vmem(),) * 4,
        scratch_shapes=[
            pltpu.VMEM((channels * count, width), jnp.float32),
            pltpu.VMEM((16, width), jnp.float32),
        ],
        compiler_params=pltpu.CompilerParams(vmem_limit_bytes=60 * MIB),
        name="prepare_kernel",
    )(frame_adjoint[0], inputs[:, :, 0], gain.reshape(1, channels))
    partners = [[(z, z ^ s) for z in range(groups)] for s in range(groups)]
    everything = [[payload], [lax.ppermute(payload, "chan", partners[1])]]
    for s in range(2, groups):
        source = everything[s & (s - 1)] if s & (s - 1) else halves
        everything.append([lax.ppermute(part, "chan", partners[s & -s]) for part in source])
    pieces_of = tuple(len(parts) for parts in everything)
    blocks = [part for parts in everything for part in parts]
    strips = lax.all_to_all(strips, "rows", split_axis=0, concat_axis=0, tiled=True)
    at = lax.axis_index("chan").astype(jnp.int32).reshape(1)

    kernel = weight.reshape(27, channels, groups, channels)
    kernel = jnp.pad(kernel, ((0, 0), (0, spare), (0, 0), (0, spare)))
    kernel = kernel.reshape(27 * group, ins)

    packed_rows = packing(taps_out, ins, count)[3]
    factor = float(frames * count * width) ** (-0.5)
    windows = pl.pallas_call(
        functools.partial(window_kernel, frames, group),
        out_shape=jax.ShapeDtypeStruct((taps_out, pixels), jnp.bfloat16),
        in_specs=[smem(), copied()],
        out_specs=vmem(),
        scratch_shapes=[pltpu.SMEM((frames,), jnp.int32)],
        compiler_params=limit(taps_out, pixels),
        name="window_kernel",
    )(frame_slot, strips)
    packed = pl.pallas_call(
        functools.partial(grad_kernel, frames, group, pieces_of, factor),
        out_shape=jax.ShapeDtypeStruct((packed_rows, 128), jnp.bfloat16),
        in_specs=[smem(), vmem()] + [copied()] * len(blocks),
        out_specs=vmem(),
        scratch_shapes=[pltpu.VMEM((ins, pixels), jnp.bfloat16)],
        compiler_params=limit(taps_out, pixels),
        cost_estimate=cost(taps_out, ins, pixels),
        name="grad_kernel",
    )(at, windows, *blocks)

    pieces = lax.all_to_all(
        packed.reshape(count, packed_rows // count, 128),
        "rows", split_axis=0, concat_axis=0, tiled=True,
    )

    sent = frames * group + round_up(2 * frames, 16)
    parts = pl.pallas_call(
        functools.partial(part_kernel, frames, group, pieces_of),
        out_shape=tuple(
            [jax.ShapeDtypeStruct((frames * (group + 2), width), jnp.float32)]
            + [jax.ShapeDtypeStruct((sent, width), jnp.bfloat16)] * (groups - 1)
        ),
        in_specs=[smem(), vmem(), vmem()] + [copied()] * len(blocks),
        out_specs=(vmem(),) * groups,
        scratch_shapes=[pltpu.VMEM((ins, pixels), jnp.float32)],
        compiler_params=limit(taps_out, pixels),
        cost_estimate=cost(taps_out, ins, pixels),
        name="part_kernel",
    )(at, kernel, windows, *blocks)

    arrived = [lax.ppermute(parts[s], "chan", partners[s]) for s in range(1, groups)]
    summed = jnp.sum(pieces.astype(jnp.float32), axis=0).astype(jnp.bfloat16)
    whole = lax.all_gather(summed, "rows", axis=0, tiled=True)
    input_adjoint, grad = pl.pallas_call(
        functools.partial(finish_kernel, frames, group),
        out_shape=(
            jax.ShapeDtypeStruct((frames, group, width), jnp.bfloat16),
            jax.ShapeDtypeStruct((taps_out, ins), jnp.float32),
        ),
        in_specs=[copied()] * (groups + 2),
        out_specs=(vmem(), vmem()),
        compiler_params=limit(taps_out, pixels),
        name="finish_kernel",
    )(whole, payload, parts[0], *arrived)
    grad = grad.reshape(27, group, groups, group)[:, :channels, :, :channels]
    return (
        input_adjoint[:, :channels, None, :],
        grad.reshape(27, channels, groups * channels),
    )


def solution(mesh):
    in_specs = (
        P("rows", "chan", None, None),
        P(),
        P(None, "chan", "rows", None),
        P("chan"),
        P(None, "chan", None),
    )
    out_specs = (P(None, "chan", "rows", None), P(None, "chan", None))
    return jax.shard_map(shards, mesh=mesh, in_specs=in_specs, out_specs=out_specs, check_vma=False)
```

```python
import functools

import jax
import jax.numpy as jnp
from jax import lax
from jax.experimental import pallas as pl
from jax.experimental.pallas import tpu as pltpu
from jax.sharding import PartitionSpec as P

CHANNELS = 192
EPSILON = 1e-06
MIB = 1024 * 1024


def round_up(value, unit):
    return -(-value // unit) * unit


def packing(taps_out, ins, count):
    blocks, rest = divmod(ins, 128)
    half = round_up(-(-taps_out // 2), 16) if rest else 0
    return blocks, rest, half, round_up(blocks * taps_out + half, 16 * count)


def vmem():
    return pl.BlockSpec(memory_space=pltpu.VMEM)


def copied():
    return pl.BlockSpec()


def anywhere():
    return pl.BlockSpec(memory_space=pl.ANY)


def smem():
    return pl.BlockSpec(memory_space=pltpu.SMEM)


def limit(taps_out, pixels):
    return pltpu.CompilerParams(vmem_limit_bytes=10 * MIB + 6 * taps_out * pixels)


def cost(rows, columns, depth):
    return pl.CostEstimate(
        flops=2 * rows * columns * depth,
        bytes_accessed=2 * (rows * depth + columns * depth),
        transcendentals=columns * depth,
    )


def gains(x_refs, start, group):
    found = []
    for ref in x_refs:
        rows = ref[pl.ds(start, 16), :].astype(jnp.float32)
        gain = rows[0:1] + rows[1:2] + rows[2:3]
        found.append(jnp.transpose(jnp.broadcast_to(gain, (128, 128)))[:group])
    return found


def norm(x_refs, t, group):
    values = [ref[pl.ds(t * group, group), :].astype(jnp.float32) for ref in x_refs]
    squares = sum(jnp.sum(value * value, axis=0, keepdims=True) for value in values)
    scale = lax.rsqrt(squares / CHANNELS + EPSILON)
    return scale, [value * scale for value in values]


def prepare_kernel(adjoint_ref, x_ref, gain_ref, strips_ref, payload_ref, lines, gain_rows):
    channels, height, width = adjoint_ref.shape
    frames = x_ref.shape[0]
    group = strips_ref.shape[2]
    lines[...] = adjoint_ref[...].astype(jnp.float32).reshape(channels * height, width)
    nothing = jnp.zeros((group, width), jnp.bfloat16)
    strips_ref[0, 0] = nothing
    strips_ref[height - 1, 2] = nothing
    for r in range(height):
        row = lines[pl.ds(r, channels, stride=height), :]
        if group > channels:
            row = jnp.concatenate(
                [row, jnp.zeros((group - channels, width), jnp.float32)], axis=0
            )
        row = row.astype(jnp.bfloat16)
        for k in range(3):
            if 0 <= r + 1 - k < height:
                strips_ref[r + 1 - k, k] = row
    for t in range(frames):
        values = x_ref[t]
        if group > channels:
            values = jnp.concatenate(
                [
                    values.astype(jnp.float32),
                    jnp.zeros((group - channels, width), jnp.float32),
                ],
                axis=0,
            ).astype(jnp.bfloat16)
        payload_ref[pl.ds(t * group, group), :] = values
    gain = gain_ref[...]
    high = gain.astype(jnp.bfloat16).astype(jnp.float32)
    middle = (gain - high).astype(jnp.bfloat16).astype(jnp.float32)
    gain_rows[...] = jnp.zeros_like(gain_rows)
    gain_rows[pl.ds(0, 1), pl.ds(0, channels)] = high
    gain_rows[pl.ds(1, 1), pl.ds(0, channels)] = middle
    gain_rows[pl.ds(2, 1), pl.ds(0, channels)] = gain - high - middle
    payload_ref[pl.ds(frames * group, 16), :] = gain_rows[...].astype(jnp.bfloat16)


def grad_kernel(frames, group, factor, at_ref, adjoint_ref, slot_hbm, *refs):
    groups = (len(refs) - 6) // 2
    x_hbm = refs[:groups]
    grad_ref, windows, place, hidden, slots, moved = refs[groups : groups + 6]
    x_refs = refs[groups + 6 :]
    ins = groups * group
    width = adjoint_ref.shape[-1]
    arriving = [
        pltpu.make_async_copy(source, target, moved.at[k])
        for k, (source, target) in enumerate(zip((slot_hbm, *x_hbm), (slots, *x_refs)))
    ]
    for copy in arriving:
        copy.start()
    for copy in arriving:
        copy.wait()

    gain = gains(x_refs, frames * group, group)
    for t in range(frames):
        scale, scaled = norm(x_refs, t, group)
        for s in range(groups):
            normed = scaled[s] * gain[s]
            value = (normed * jax.nn.sigmoid(normed)).astype(jnp.bfloat16)
            start = pl.multiple_of((at_ref[0] ^ s) * group, 16)
            hidden[pl.ds(start, group), pl.ds(t * width, width)] = value

    for slot in range(frames):
        place[slots[slot]] = slot

    lane = lax.broadcasted_iota(jnp.int32, (group, width), 1)
    nothing = jnp.zeros((group, width), jnp.bfloat16)
    for a in range(2):
        for inner in range(9):
            for t in range(frames - 2 + a, frames):
                windows[pl.ds((a * 9 + inner) * group, group), pl.ds(t * width, width)] = nothing
    for frame in range(frames):
        slot = place[frame]
        for b in range(3):
            row = adjoint_ref[slot, 2 - b].astype(jnp.float32)
            after = jnp.where(lane == width - 1, 0.0, pltpu.roll(row, width - 1, 1))
            before = jnp.where(lane == 0, 0.0, pltpu.roll(row, 1, 1))
            for c, shifted in enumerate((after, row, before)):
                shifted = shifted.astype(jnp.bfloat16)
                for a in range(3):
                    t = frame + a - 2
                    if t >= 0:
                        windows[
                            pl.ds((a * 9 + b * 3 + c) * group, group), pl.ds(t * width, width)
                        ] = shifted

    grad = lax.dot_general(
        windows[...], hidden[...], (((1,), (1,)), ((), ())), preferred_element_type=jnp.float32
    )
    grad = grad * factor
    taps_out = grad.shape[0]
    blocks, rest, half, rows = packing(taps_out, ins, 1)
    for block in range(blocks):
        grad_ref[pl.ds(block * taps_out, taps_out), :] = grad[
            :, block * 128 : block * 128 + 128
        ].astype(jnp.bfloat16)
    base = blocks * taps_out
    if rest:
        left = grad[:half, blocks * 128 :]
        right = grad[half:, blocks * 128 :]
        right = jnp.concatenate(
            [right, jnp.zeros((2 * half - taps_out, rest), jnp.float32)], axis=0
        )
        grad_ref[pl.ds(base, half), :] = jnp.concatenate([left, right], axis=1).astype(
            jnp.bfloat16
        )
        base = base + half
    tail = grad_ref.shape[0] - base
    if tail:
        grad_ref[pl.ds(base, tail), :] = jnp.zeros((tail, 128), jnp.bfloat16)


def part_kernel(frames, group, at_ref, weight_ref, windows, *refs):
    groups = (len(refs) - 1) // 2
    x_refs = refs[:groups]
    part_refs = refs[groups : 2 * groups]
    product = refs[2 * groups]
    width = part_refs[0].shape[-1]
    product[...] = lax.dot_general(
        weight_ref[...], windows[...], (((0,), (0,)), ((), ())), preferred_element_type=jnp.float32
    )
    gain = gains(x_refs, frames * group, group)
    shares = []
    for t in range(frames):
        scale, scaled = norm(x_refs, t, group)
        part_refs[0][pl.ds(frames * group + t, 1), :] = scale
        share = jnp.zeros((1, width), jnp.float32)
        for s in range(groups):
            normed = scaled[s] * gain[s]
            sigma = jax.nn.sigmoid(normed)
            slope = sigma * (1.0 + normed * (1.0 - sigma)) * gain[s]
            start = pl.multiple_of((at_ref[0] ^ s) * group, 16)
            term = product[pl.ds(start, group), pl.ds(t * width, width)] * slope * scale
            part_refs[s][pl.ds(t * group, group), :] = term.astype(part_refs[s].dtype)
            share = share + jnp.sum(term * scaled[s], axis=0, keepdims=True)
        shares.append(share)
    share = jnp.concatenate(shares, axis=0)
    part_refs[0][pl.ds(frames * group + frames, frames), :] = share
    high = share.astype(jnp.bfloat16).astype(jnp.float32)
    both = [high, share - high]
    unused = round_up(2 * frames, 16) - 2 * frames
    if unused:
        both.append(jnp.zeros((unused, width), jnp.float32))
    both = jnp.concatenate(both, axis=0).astype(jnp.bfloat16)
    for s in range(1, groups):
        part_refs[s][pl.ds(frames * group, both.shape[0]), :] = both


def finish_kernel(frames, group, packed_ref, x_ref, *refs):
    own_hbm, others, (out_ref, grad_ref, own_ref, moved) = refs[0], refs[1:-4], refs[-4:]
    own_copy = pltpu.make_async_copy(own_hbm, own_ref, moved)
    own_copy.start()
    taps_out, ins = grad_ref.shape
    blocks, rest, half, rows = packing(taps_out, ins, 1)
    for block in range(blocks):
        grad_ref[:, pl.ds(block * 128, 128)] = packed_ref[
            pl.ds(block * taps_out, taps_out), :
        ].astype(jnp.float32)
    if rest:
        both = packed_ref[pl.ds(blocks * taps_out, half), :].astype(jnp.float32)
        grad_ref[pl.ds(0, half), pl.ds(blocks * 128, rest)] = both[:, :rest]
        grad_ref[pl.ds(half, taps_out - half), pl.ds(blocks * 128, rest)] = both[
            : taps_out - half, rest:
        ]

    own_copy.wait()
    share = own_ref[pl.ds(frames * group + frames, frames), :]
    for ref in others:
        both = ref[pl.ds(frames * group, round_up(2 * frames, 16)), :].astype(jnp.float32)
        share = share + both[:frames] + both[frames : 2 * frames]
    share = share / CHANNELS
    for t in range(frames):
        term = own_ref[pl.ds(t * group, group), :]
        for ref in others:
            term = term + ref[pl.ds(t * group, group), :].astype(jnp.float32)
        scale = own_ref[pl.ds(frames * group + t, 1), :]
        scaled = x_ref[pl.ds(t * group, group), :].astype(jnp.float32) * scale
        out_ref[t] = (term - scaled * share[t : t + 1]).astype(jnp.bfloat16)


def shards(frame_adjoint, frame_slot, inputs, gain, weight):
    count = lax.axis_size("rows")
    groups = lax.axis_size("chan")
    frames, channels, _, width = inputs.shape
    group = round_up(channels, 16)
    spare = group - channels
    ins = groups * group

    taps_out = 27 * group
    pixels = frames * width
    strips, payload = pl.pallas_call(
        prepare_kernel,
        out_shape=(
            jax.ShapeDtypeStruct((count, 3, group, width), jnp.bfloat16),
            jax.ShapeDtypeStruct((frames * group + 16, width), jnp.bfloat16),
        ),
        in_specs=[copied(), copied(), copied()],
        out_specs=(vmem(), vmem()),
        scratch_shapes=[
            pltpu.VMEM((channels * count, width), jnp.float32),
            pltpu.VMEM((16, width), jnp.float32),
        ],
        compiler_params=pltpu.CompilerParams(vmem_limit_bytes=60 * MIB),
        name="prepare_kernel",
    )(frame_adjoint[0], inputs[:, :, 0], gain.reshape(1, channels))
    partners = [[(z, z ^ s) for z in range(groups)] for s in range(groups)]
    everything = [payload] + [
        lax.ppermute(payload, "chan", partners[s]) for s in range(1, groups)
    ]
    strips = lax.cond(
        lax.axis_index("rows") < count,
        lambda rows: lax.all_to_all(rows, "rows", split_axis=0, concat_axis=0, tiled=True),
        lambda rows: rows,
        strips,
    )
    at = lax.axis_index("chan").astype(jnp.int32).reshape(1)

    kernel = weight.reshape(27, channels, groups, channels)
    kernel = jnp.pad(kernel, ((0, 0), (0, spare), (0, 0), (0, spare)))
    kernel = kernel.reshape(27 * group, ins)

    packed_rows = packing(taps_out, ins, count)[3]
    factor = float(frames * count * width) ** (-0.5)
    packed, windows = pl.pallas_call(
        functools.partial(grad_kernel, frames, group, factor),
        out_shape=(
            jax.ShapeDtypeStruct((packed_rows, 128), jnp.bfloat16),
            jax.ShapeDtypeStruct((taps_out, pixels), jnp.bfloat16),
        ),
        in_specs=[smem(), vmem()] + [anywhere()] * (groups + 1),
        out_specs=(vmem(), vmem()),
        scratch_shapes=[
            pltpu.SMEM((frames,), jnp.int32),
            pltpu.VMEM((ins, pixels), jnp.bfloat16),
            pltpu.SMEM((frames,), jnp.int32),
            pltpu.SemaphoreType.DMA((groups + 1,)),
        ]
        + [pltpu.VMEM(payload.shape, jnp.bfloat16)] * groups,
        compiler_params=limit(taps_out, pixels),
        cost_estimate=cost(taps_out, ins, pixels),
        name="grad_kernel",
    )(at, strips, frame_slot, *everything)

    pieces = lax.all_to_all(
        packed.reshape(count, packed_rows // count, 128),
        "rows", split_axis=0, concat_axis=0, tiled=True,
    )

    sent = frames * group + round_up(2 * frames, 16)
    parts = pl.pallas_call(
        functools.partial(part_kernel, frames, group),
        out_shape=tuple(
            [jax.ShapeDtypeStruct((frames * (group + 2), width), jnp.float32)]
            + [jax.ShapeDtypeStruct((sent, width), jnp.bfloat16)] * (groups - 1)
        ),
        in_specs=[smem(), vmem(), vmem()] + [copied()] * groups,
        out_specs=(vmem(),) * groups,
        scratch_shapes=[pltpu.VMEM((ins, pixels), jnp.float32)],
        compiler_params=limit(taps_out, pixels),
        cost_estimate=cost(taps_out, ins, pixels),
        name="part_kernel",
    )(at, kernel, windows, *everything)

    arrived = [lax.ppermute(parts[s], "chan", partners[s]) for s in range(1, groups)]
    summed = jnp.sum(pieces.astype(jnp.float32), axis=0).astype(jnp.bfloat16)
    whole = lax.all_gather(summed, "rows", axis=0, tiled=True)
    input_adjoint, grad = pl.pallas_call(
        functools.partial(finish_kernel, frames, group),
        out_shape=(
            jax.ShapeDtypeStruct((frames, group, width), jnp.bfloat16),
            jax.ShapeDtypeStruct((taps_out, ins), jnp.float32),
        ),
        in_specs=[copied(), copied(), anywhere()] + [copied()] * (groups - 1),
        out_specs=(vmem(), vmem()),
        scratch_shapes=[
            pltpu.VMEM((frames * (group + 2), width), jnp.float32),
            pltpu.SemaphoreType.DMA,
        ],
        compiler_params=limit(taps_out, pixels),
        name="finish_kernel",
    )(whole, payload, parts[0], *arrived)
    grad = grad.reshape(27, group, groups, group)[:, :channels, :, :channels]
    return (
        input_adjoint[:, :channels, None, :],
        grad.reshape(27, channels, groups * channels),
    )


def solution(mesh):
    in_specs = (
        P("rows", "chan", None, None),
        P(),
        P(None, "chan", "rows", None),
        P("chan"),
        P(None, "chan", None),
    )
    out_specs = (P(None, "chan", "rows", None), P(None, "chan", None))
    return jax.shard_map(shards, mesh=mesh, in_specs=in_specs, out_specs=out_specs, check_vma=False)
```

```python
import functools

import jax
import jax.numpy as jnp
from jax import lax
from jax.experimental import pallas as pl
from jax.experimental.pallas import tpu as pltpu
from jax.sharding import PartitionSpec as P

CHANNELS = 192
EPSILON = 1e-06
MIB = 1024 * 1024


def round_up(value, unit):
    return -(-value // unit) * unit


def packing(taps_out, ins, count):
    blocks, rest = divmod(ins, 128)
    half = round_up(-(-taps_out // 2), 16) if rest else 0
    return blocks, rest, half, round_up(blocks * taps_out + half, 16 * count)


def vmem():
    return pl.BlockSpec(memory_space=pltpu.VMEM)


def copied():
    return pl.BlockSpec()


def smem():
    return pl.BlockSpec(memory_space=pltpu.SMEM)


def limit(taps_out, pixels):
    return pltpu.CompilerParams(vmem_limit_bytes=10 * MIB + 6 * taps_out * pixels)


def cost(rows, columns, depth):
    return pl.CostEstimate(
        flops=2 * rows * columns * depth,
        bytes_accessed=2 * (rows * depth + columns * depth),
        transcendentals=columns * depth,
    )


def gains(x_refs, start, group):
    found = []
    for ref in x_refs:
        rows = ref[pl.ds(start, 16), :].astype(jnp.float32)
        gain = rows[0:1] + rows[1:2] + rows[2:3]
        found.append(jnp.transpose(jnp.broadcast_to(gain, (128, 128)))[:group])
    return found


def norm(x_refs, t, group):
    values = [ref[pl.ds(t * group, group), :].astype(jnp.float32) for ref in x_refs]
    squares = sum(jnp.sum(value * value, axis=0, keepdims=True) for value in values)
    scale = lax.rsqrt(squares / CHANNELS + EPSILON)
    return scale, [value * scale for value in values]


def prepare_kernel(adjoint_ref, x_ref, gain_ref, strips_ref, payload_ref, lines, gain_rows):
    channels, height, width = adjoint_ref.shape
    frames = x_ref.shape[0]
    group = strips_ref.shape[2]
    lines[...] = adjoint_ref[...].astype(jnp.float32).reshape(channels * height, width)
    nothing = jnp.zeros((group, width), jnp.bfloat16)
    strips_ref[0, 0] = nothing
    strips_ref[height - 1, 2] = nothing
    for r in range(height):
        row = lines[pl.ds(r, channels, stride=height), :]
        if group > channels:
            row = jnp.concatenate(
                [row, jnp.zeros((group - channels, width), jnp.float32)], axis=0
            )
        row = row.astype(jnp.bfloat16)
        for k in range(3):
            if 0 <= r + 1 - k < height:
                strips_ref[r + 1 - k, k] = row
    for t in range(frames):
        values = x_ref[t]
        if group > channels:
            values = jnp.concatenate(
                [
                    values.astype(jnp.float32),
                    jnp.zeros((group - channels, width), jnp.float32),
                ],
                axis=0,
            ).astype(jnp.bfloat16)
        payload_ref[pl.ds(t * group, group), :] = values
    gain = gain_ref[...]
    high = gain.astype(jnp.bfloat16).astype(jnp.float32)
    middle = (gain - high).astype(jnp.bfloat16).astype(jnp.float32)
    gain_rows[...] = jnp.zeros_like(gain_rows)
    gain_rows[pl.ds(0, 1), pl.ds(0, channels)] = high
    gain_rows[pl.ds(1, 1), pl.ds(0, channels)] = middle
    gain_rows[pl.ds(2, 1), pl.ds(0, channels)] = gain - high - middle
    payload_ref[pl.ds(frames * group, 16), :] = gain_rows[...].astype(jnp.bfloat16)


def build_windows(frames, group, slot_ref, adjoint_ref, windows, place):
    width = adjoint_ref.shape[-1]
    for slot in range(frames):
        place[slot_ref[slot]] = slot

    lane = lax.broadcasted_iota(jnp.int32, (group, width), 1)
    nothing = jnp.zeros((group, width), jnp.bfloat16)
    for a in range(2):
        for inner in range(9):
            for t in range(frames - 2 + a, frames):
                windows[pl.ds((a * 9 + inner) * group, group), pl.ds(t * width, width)] = nothing
    for frame in range(frames):
        slot = place[frame]
        for b in range(3):
            row = adjoint_ref[slot, 2 - b].astype(jnp.float32)
            after = jnp.where(lane == width - 1, 0.0, pltpu.roll(row, width - 1, 1))
            before = jnp.where(lane == 0, 0.0, pltpu.roll(row, 1, 1))
            for c, shifted in enumerate((after, row, before)):
                shifted = shifted.astype(jnp.bfloat16)
                for a in range(3):
                    t = frame + a - 2
                    if t >= 0:
                        windows[
                            pl.ds((a * 9 + b * 3 + c) * group, group), pl.ds(t * width, width)
                        ] = shifted


def grad_kernel(frames, group, factor, at_ref, slot_ref, adjoint_ref, *refs):
    groups = len(refs) - 4
    x_refs = refs[:groups]
    grad_ref, place, windows, hidden = refs[groups:]
    ins = groups * group
    width = adjoint_ref.shape[-1]
    build_windows(frames, group, slot_ref, adjoint_ref, windows, place)
    gain = gains(x_refs, frames * group, group)
    for t in range(frames):
        scale, scaled = norm(x_refs, t, group)
        for s in range(groups):
            normed = scaled[s] * gain[s]
            value = (normed * jax.nn.sigmoid(normed)).astype(jnp.bfloat16)
            start = pl.multiple_of((at_ref[0] ^ s) * group, 16)
            hidden[pl.ds(start, group), pl.ds(t * width, width)] = value

    grad = lax.dot_general(
        windows[...], hidden[...], (((1,), (1,)), ((), ())), preferred_element_type=jnp.float32
    )
    grad = grad * factor
    taps_out = grad.shape[0]
    blocks, rest, half, rows = packing(taps_out, ins, 1)
    for block in range(blocks):
        grad_ref[pl.ds(block * taps_out, taps_out), :] = grad[
            :, block * 128 : block * 128 + 128
        ].astype(jnp.bfloat16)
    base = blocks * taps_out
    if rest:
        left = grad[:half, blocks * 128 :]
        right = grad[half:, blocks * 128 :]
        right = jnp.concatenate(
            [right, jnp.zeros((2 * half - taps_out, rest), jnp.float32)], axis=0
        )
        grad_ref[pl.ds(base, half), :] = jnp.concatenate([left, right], axis=1).astype(
            jnp.bfloat16
        )
        base = base + half
    tail = grad_ref.shape[0] - base
    if tail:
        grad_ref[pl.ds(base, tail), :] = jnp.zeros((tail, 128), jnp.bfloat16)


def part_kernel(frames, group, at_ref, slot_ref, adjoint_ref, weight_ref, *refs):
    groups = (len(refs) - 3) // 2
    x_refs = refs[:groups]
    part_refs = refs[groups : 2 * groups]
    place, windows, product = refs[2 * groups :]
    build_windows(frames, group, slot_ref, adjoint_ref, windows, place)
    width = part_refs[0].shape[-1]
    product[...] = lax.dot_general(
        weight_ref[...], windows[...], (((0,), (0,)), ((), ())), preferred_element_type=jnp.float32
    )
    gain = gains(x_refs, frames * group, group)
    shares = []
    for t in range(frames):
        scale, scaled = norm(x_refs, t, group)
        part_refs[0][pl.ds(frames * group + t, 1), :] = scale
        share = jnp.zeros((1, width), jnp.float32)
        for s in range(groups):
            normed = scaled[s] * gain[s]
            sigma = jax.nn.sigmoid(normed)
            slope = sigma * (1.0 + normed * (1.0 - sigma)) * gain[s]
            start = pl.multiple_of((at_ref[0] ^ s) * group, 16)
            term = product[pl.ds(start, group), pl.ds(t * width, width)] * slope * scale
            part_refs[s][pl.ds(t * group, group), :] = term.astype(part_refs[s].dtype)
            share = share + jnp.sum(term * scaled[s], axis=0, keepdims=True)
        shares.append(share)
    share = jnp.concatenate(shares, axis=0)
    part_refs[0][pl.ds(frames * group + frames, frames), :] = share
    high = share.astype(jnp.bfloat16).astype(jnp.float32)
    both = [high, share - high]
    unused = round_up(2 * frames, 16) - 2 * frames
    if unused:
        both.append(jnp.zeros((unused, width), jnp.float32))
    both = jnp.concatenate(both, axis=0).astype(jnp.bfloat16)
    for s in range(1, groups):
        part_refs[s][pl.ds(frames * group, both.shape[0]), :] = both


def finish_kernel(frames, group, packed_ref, x_ref, *refs):
    own_ref, others, (out_ref, grad_ref) = refs[0], refs[1:-2], refs[-2:]
    taps_out, ins = grad_ref.shape
    blocks, rest, half, rows = packing(taps_out, ins, 1)
    for block in range(blocks):
        grad_ref[:, pl.ds(block * 128, 128)] = packed_ref[
            pl.ds(block * taps_out, taps_out), :
        ].astype(jnp.float32)
    if rest:
        both = packed_ref[pl.ds(blocks * taps_out, half), :].astype(jnp.float32)
        grad_ref[pl.ds(0, half), pl.ds(blocks * 128, rest)] = both[:, :rest]
        grad_ref[pl.ds(half, taps_out - half), pl.ds(blocks * 128, rest)] = both[
            : taps_out - half, rest:
        ]

    share = own_ref[pl.ds(frames * group + frames, frames), :]
    for ref in others:
        both = ref[pl.ds(frames * group, round_up(2 * frames, 16)), :].astype(jnp.float32)
        share = share + both[:frames] + both[frames : 2 * frames]
    share = share / CHANNELS
    for t in range(frames):
        term = own_ref[pl.ds(t * group, group), :]
        for ref in others:
            term = term + ref[pl.ds(t * group, group), :].astype(jnp.float32)
        scale = own_ref[pl.ds(frames * group + t, 1), :]
        scaled = x_ref[pl.ds(t * group, group), :].astype(jnp.float32) * scale
        out_ref[t] = (term - scaled * share[t : t + 1]).astype(jnp.bfloat16)


def shards(frame_adjoint, frame_slot, inputs, gain, weight):
    count = lax.axis_size("rows")
    groups = lax.axis_size("chan")
    frames, channels, _, width = inputs.shape
    group = round_up(channels, 16)
    spare = group - channels
    ins = groups * group

    taps_out = 27 * group
    pixels = frames * width
    strips, payload = pl.pallas_call(
        prepare_kernel,
        out_shape=(
            jax.ShapeDtypeStruct((count, 3, group, width), jnp.bfloat16),
            jax.ShapeDtypeStruct((frames * group + 16, width), jnp.bfloat16),
        ),
        in_specs=[copied(), copied(), copied()],
        out_specs=(vmem(), vmem()),
        scratch_shapes=[
            pltpu.VMEM((channels * count, width), jnp.float32),
            pltpu.VMEM((16, width), jnp.float32),
        ],
        compiler_params=pltpu.CompilerParams(vmem_limit_bytes=60 * MIB),
        name="prepare_kernel",
    )(frame_adjoint[0], inputs[:, :, 0], gain.reshape(1, channels))
    partners = [[(z, z ^ s) for z in range(groups)] for s in range(groups)]
    everything = [payload] + [
        lax.ppermute(payload, "chan", partners[s]) for s in range(1, groups)
    ]
    strips = lax.cond(
        lax.axis_index("rows") < count,
        lambda rows: lax.all_to_all(rows, "rows", split_axis=0, concat_axis=0, tiled=True),
        lambda rows: rows,
        strips,
    )
    at = lax.axis_index("chan").astype(jnp.int32).reshape(1)

    kernel = weight.reshape(27, channels, groups, channels)
    kernel = jnp.pad(kernel, ((0, 0), (0, spare), (0, 0), (0, spare)))
    kernel = kernel.reshape(27 * group, ins)

    packed_rows = packing(taps_out, ins, count)[3]
    factor = float(frames * count * width) ** (-0.5)
    packed = pl.pallas_call(
        functools.partial(grad_kernel, frames, group, factor),
        out_shape=jax.ShapeDtypeStruct((packed_rows, 128), jnp.bfloat16),
        in_specs=[smem(), smem(), copied()] + [copied()] * groups,
        out_specs=vmem(),
        scratch_shapes=[
            pltpu.SMEM((frames,), jnp.int32),
            pltpu.VMEM((taps_out, pixels), jnp.bfloat16),
            pltpu.VMEM((ins, pixels), jnp.bfloat16),
        ],
        compiler_params=limit(taps_out, pixels),
        cost_estimate=cost(taps_out, ins, pixels),
        name="grad_kernel",
    )(at, frame_slot, strips, *everything)

    pieces = lax.all_to_all(
        packed.reshape(count, packed_rows // count, 128),
        "rows", split_axis=0, concat_axis=0, tiled=True,
    )

    sent = frames * group + round_up(2 * frames, 16)
    parts = pl.pallas_call(
        functools.partial(part_kernel, frames, group),
        out_shape=tuple(
            [jax.ShapeDtypeStruct((frames * (group + 2), width), jnp.float32)]
            + [jax.ShapeDtypeStruct((sent, width), jnp.bfloat16)] * (groups - 1)
        ),
        in_specs=[smem(), smem(), copied(), copied()] + [copied()] * groups,
        out_specs=(vmem(),) * groups,
        scratch_shapes=[
            pltpu.SMEM((frames,), jnp.int32),
            pltpu.VMEM((taps_out, pixels), jnp.bfloat16),
            pltpu.VMEM((ins, pixels), jnp.float32),
        ],
        compiler_params=limit(taps_out, pixels),
        cost_estimate=cost(taps_out, ins, pixels),
        name="part_kernel",
    )(at, frame_slot, strips, kernel, *everything)

    arrived = [lax.ppermute(parts[s], "chan", partners[s]) for s in range(1, groups)]
    summed = jnp.sum(pieces.astype(jnp.float32), axis=0).astype(jnp.bfloat16)
    whole = lax.all_gather(summed, "rows", axis=0, tiled=True)
    input_adjoint, grad = pl.pallas_call(
        functools.partial(finish_kernel, frames, group),
        out_shape=(
            jax.ShapeDtypeStruct((frames, group, width), jnp.bfloat16),
            jax.ShapeDtypeStruct((taps_out, ins), jnp.float32),
        ),
        in_specs=[copied()] * (groups + 2),
        out_specs=(vmem(), vmem()),
        compiler_params=limit(taps_out, pixels),
        name="finish_kernel",
    )(whole, payload, parts[0], *arrived)
    grad = grad.reshape(27, group, groups, group)[:, :channels, :, :channels]
    return (
        input_adjoint[:, :channels, None, :],
        grad.reshape(27, channels, groups * channels),
    )


def solution(mesh):
    in_specs = (
        P("rows", "chan", None, None),
        P(),
        P(None, "chan", "rows", None),
        P("chan"),
        P(None, "chan", None),
    )
    out_specs = (P(None, "chan", "rows", None), P(None, "chan", None))
    return jax.shard_map(shards, mesh=mesh, in_specs=in_specs, out_specs=out_specs, check_vma=False)
```

```python
import functools

import jax
import jax.numpy as jnp
from jax import lax
from jax.experimental import pallas as pl
from jax.experimental.pallas import tpu as pltpu
from jax.sharding import PartitionSpec as P

CHANNELS = 192
EPSILON = 1e-06
MIB = 1024 * 1024


def round_up(value, unit):
    return -(-value // unit) * unit


def packing(taps_out, ins, count):
    blocks, rest = divmod(ins, 128)
    half = round_up(-(-taps_out // 2), 16) if rest else 0
    return blocks, rest, half, round_up(blocks * taps_out + half, 16 * count)


def vmem():
    return pl.BlockSpec(memory_space=pltpu.VMEM)


def copied():
    return pl.BlockSpec()


def smem():
    return pl.BlockSpec(memory_space=pltpu.SMEM)


def limit(taps_out, pixels):
    return pltpu.CompilerParams(vmem_limit_bytes=10 * MIB + 6 * taps_out * pixels)


def cost(rows, columns, depth):
    return pl.CostEstimate(
        flops=2 * rows * columns * depth,
        bytes_accessed=2 * (rows * depth + columns * depth),
        transcendentals=columns * depth,
    )


def gains(gain_ref, line, x_refs, start, group):
    line[...] = jnp.zeros_like(line)
    line[pl.ds(0, 1), pl.ds(0, gain_ref.shape[1])] = gain_ref[...]
    found = [jnp.transpose(jnp.broadcast_to(line[pl.ds(0, 1), :], (128, 128)))[:group]]
    for ref in x_refs[1:]:
        rows = ref[pl.ds(start, 16), :].astype(jnp.float32)
        gain = rows[0:1] + rows[1:2] + rows[2:3]
        found.append(jnp.transpose(jnp.broadcast_to(gain, (128, 128)))[:group])
    return found


def norm(x_refs, t, group):
    values = [ref[pl.ds(t * group, group), :].astype(jnp.float32) for ref in x_refs]
    squares = sum(jnp.sum(value * value, axis=0, keepdims=True) for value in values)
    scale = lax.rsqrt(squares / CHANNELS + EPSILON)
    return scale, [value * scale for value in values]


def prepare_kernel(adjoint_ref, x_ref, gain_ref, strips_ref, payload_ref, lines, gain_rows):
    channels, height, width = adjoint_ref.shape
    frames = x_ref.shape[0]
    group = strips_ref.shape[2]
    lines[...] = adjoint_ref[...].astype(jnp.float32).reshape(channels * height, width)
    nothing = jnp.zeros((group, width), jnp.bfloat16)
    strips_ref[0, 0] = nothing
    strips_ref[height - 1, 2] = nothing
    for r in range(height):
        row = lines[pl.ds(r, channels, stride=height), :]
        if group > channels:
            row = jnp.concatenate(
                [row, jnp.zeros((group - channels, width), jnp.float32)], axis=0
            )
        row = row.astype(jnp.bfloat16)
        for k in range(3):
            if 0 <= r + 1 - k < height:
                strips_ref[r + 1 - k, k] = row
    for t in range(frames):
        values = x_ref[t]
        if group > channels:
            values = jnp.concatenate(
                [
                    values.astype(jnp.float32),
                    jnp.zeros((group - channels, width), jnp.float32),
                ],
                axis=0,
            ).astype(jnp.bfloat16)
        payload_ref[pl.ds(t * group, group), :] = values
    gain = gain_ref[...]
    high = gain.astype(jnp.bfloat16).astype(jnp.float32)
    middle = (gain - high).astype(jnp.bfloat16).astype(jnp.float32)
    gain_rows[...] = jnp.zeros_like(gain_rows)
    gain_rows[pl.ds(0, 1), pl.ds(0, channels)] = high
    gain_rows[pl.ds(1, 1), pl.ds(0, channels)] = middle
    gain_rows[pl.ds(2, 1), pl.ds(0, channels)] = gain - high - middle
    payload_ref[pl.ds(frames * group, 16), :] = gain_rows[...].astype(jnp.bfloat16)


def build_windows(frames, group, slot_ref, adjoint_ref, windows, place):
    width = adjoint_ref.shape[-1]
    for slot in range(frames):
        place[slot_ref[slot]] = slot

    lane = lax.broadcasted_iota(jnp.int32, (group, width), 1)
    nothing = jnp.zeros((group, width), jnp.bfloat16)
    for a in range(2):
        for inner in range(9):
            for t in range(frames - 2 + a, frames):
                windows[pl.ds((a * 9 + inner) * group, group), pl.ds(t * width, width)] = nothing
    for frame in range(frames):
        slot = place[frame]
        for b in range(3):
            row = adjoint_ref[slot, 2 - b].astype(jnp.float32)
            after = jnp.where(lane == width - 1, 0.0, pltpu.roll(row, width - 1, 1))
            before = jnp.where(lane == 0, 0.0, pltpu.roll(row, 1, 1))
            for c, shifted in enumerate((after, row, before)):
                shifted = shifted.astype(jnp.bfloat16)
                for a in range(3):
                    t = frame + a - 2
                    if t >= 0:
                        windows[
                            pl.ds((a * 9 + b * 3 + c) * group, group), pl.ds(t * width, width)
                        ] = shifted


def grad_kernel(frames, group, factor, at_ref, slot_ref, gain_ref, adjoint_ref, *refs):
    groups = len(refs) - 5
    x_refs = refs[:groups]
    grad_ref, place, line, windows, hidden = refs[groups:]
    ins = groups * group
    width = adjoint_ref.shape[-1]
    build_windows(frames, group, slot_ref, adjoint_ref, windows, place)
    gain = gains(gain_ref, line, x_refs, frames * group, group)
    for t in range(frames):
        scale, scaled = norm(x_refs, t, group)
        for s in range(groups):
            normed = scaled[s] * gain[s]
            value = (normed * jax.nn.sigmoid(normed)).astype(jnp.bfloat16)
            start = pl.multiple_of((at_ref[0] ^ s) * group, 16)
            hidden[pl.ds(start, group), pl.ds(t * width, width)] = value

    grad = lax.dot_general(
        windows[...], hidden[...], (((1,), (1,)), ((), ())), preferred_element_type=jnp.float32
    )
    grad = grad * factor
    taps_out = grad.shape[0]
    blocks, rest, half, rows = packing(taps_out, ins, 1)
    for block in range(blocks):
        grad_ref[pl.ds(block * taps_out, taps_out), :] = grad[
            :, block * 128 : block * 128 + 128
        ].astype(jnp.bfloat16)
    base = blocks * taps_out
    if rest:
        left = grad[:half, blocks * 128 :]
        right = grad[half:, blocks * 128 :]
        right = jnp.concatenate(
            [right, jnp.zeros((2 * half - taps_out, rest), jnp.float32)], axis=0
        )
        grad_ref[pl.ds(base, half), :] = jnp.concatenate([left, right], axis=1).astype(
            jnp.bfloat16
        )
        base = base + half
    tail = grad_ref.shape[0] - base
    if tail:
        grad_ref[pl.ds(base, tail), :] = jnp.zeros((tail, 128), jnp.bfloat16)


def part_kernel(frames, group, at_ref, slot_ref, gain_ref, adjoint_ref, weight_ref, *refs):
    groups = (len(refs) - 4) // 2
    x_refs = refs[:groups]
    part_refs = refs[groups : 2 * groups]
    place, line, windows, product = refs[2 * groups :]
    build_windows(frames, group, slot_ref, adjoint_ref, windows, place)
    width = part_refs[0].shape[-1]
    product[...] = lax.dot_general(
        weight_ref[...], windows[...], (((0,), (0,)), ((), ())), preferred_element_type=jnp.float32
    )
    gain = gains(gain_ref, line, x_refs, frames * group, group)
    shares = []
    for t in range(frames):
        scale, scaled = norm(x_refs, t, group)
        part_refs[0][pl.ds(frames * group + t, 1), :] = scale
        share = jnp.zeros((1, width), jnp.float32)
        for s in range(groups):
            normed = scaled[s] * gain[s]
            sigma = jax.nn.sigmoid(normed)
            slope = sigma * (1.0 + normed * (1.0 - sigma)) * gain[s]
            start = pl.multiple_of((at_ref[0] ^ s) * group, 16)
            term = product[pl.ds(start, group), pl.ds(t * width, width)] * slope * scale
            part_refs[s][pl.ds(t * group, group), :] = term.astype(part_refs[s].dtype)
            share = share + jnp.sum(term * scaled[s], axis=0, keepdims=True)
        shares.append(share)
    share = jnp.concatenate(shares, axis=0)
    part_refs[0][pl.ds(frames * group + frames, frames), :] = share
    high = share.astype(jnp.bfloat16).astype(jnp.float32)
    both = [high, share - high]
    unused = round_up(2 * frames, 16) - 2 * frames
    if unused:
        both.append(jnp.zeros((unused, width), jnp.float32))
    both = jnp.concatenate(both, axis=0).astype(jnp.bfloat16)
    for s in range(1, groups):
        part_refs[s][pl.ds(frames * group, both.shape[0]), :] = both


def finish_kernel(frames, group, packed_ref, x_ref, *refs):
    own_ref, others, (out_ref, grad_ref) = refs[0], refs[1:-2], refs[-2:]
    taps_out, ins = grad_ref.shape
    blocks, rest, half, rows = packing(taps_out, ins, 1)
    for block in range(blocks):
        grad_ref[:, pl.ds(block * 128, 128)] = packed_ref[
            pl.ds(block * taps_out, taps_out), :
        ].astype(jnp.float32)
    if rest:
        both = packed_ref[pl.ds(blocks * taps_out, half), :].astype(jnp.float32)
        grad_ref[pl.ds(0, half), pl.ds(blocks * 128, rest)] = both[:, :rest]
        grad_ref[pl.ds(half, taps_out - half), pl.ds(blocks * 128, rest)] = both[
            : taps_out - half, rest:
        ]

    share = own_ref[pl.ds(frames * group + frames, frames), :]
    for ref in others:
        both = ref[pl.ds(frames * group, round_up(2 * frames, 16)), :].astype(jnp.float32)
        share = share + both[:frames] + both[frames : 2 * frames]
    share = share / CHANNELS
    for t in range(frames):
        term = own_ref[pl.ds(t * group, group), :]
        for ref in others:
            term = term + ref[pl.ds(t * group, group), :].astype(jnp.float32)
        scale = own_ref[pl.ds(frames * group + t, 1), :]
        scaled = x_ref[pl.ds(t * group, group), :].astype(jnp.float32) * scale
        out_ref[t] = (term - scaled * share[t : t + 1]).astype(jnp.bfloat16)


def shards(frame_adjoint, frame_slot, inputs, gain, weight):
    count = lax.axis_size("rows")
    groups = lax.axis_size("chan")
    frames, channels, _, width = inputs.shape
    group = round_up(channels, 16)
    spare = group - channels
    ins = groups * group

    taps_out = 27 * group
    pixels = frames * width
    strips, payload = pl.pallas_call(
        prepare_kernel,
        out_shape=(
            jax.ShapeDtypeStruct((count, 3, group, width), jnp.bfloat16),
            jax.ShapeDtypeStruct((frames * group + 16, width), jnp.bfloat16),
        ),
        in_specs=[copied(), copied(), copied()],
        out_specs=(vmem(), vmem()),
        scratch_shapes=[
            pltpu.VMEM((channels * count, width), jnp.float32),
            pltpu.VMEM((16, width), jnp.float32),
        ],
        compiler_params=pltpu.CompilerParams(vmem_limit_bytes=60 * MIB),
        name="prepare_kernel",
    )(frame_adjoint[0], inputs[:, :, 0], gain.reshape(1, channels))
    partners = [[(z, z ^ s) for z in range(groups)] for s in range(groups)]
    own = jnp.pad(inputs[:, :, 0], ((0, 0), (0, spare), (0, 0))).reshape(frames * group, width)
    gain_line = gain.reshape(1, channels)
    everything = [own] + [
        lax.ppermute(payload, "chan", partners[s]) for s in range(1, groups)
    ]
    strips = lax.cond(
        lax.axis_index("rows") < count,
        lambda rows: lax.all_to_all(rows, "rows", split_axis=0, concat_axis=0, tiled=True),
        lambda rows: rows,
        strips,
    )
    at = lax.axis_index("chan").astype(jnp.int32).reshape(1)

    kernel = weight.reshape(27, channels, groups, channels)
    kernel = jnp.pad(kernel, ((0, 0), (0, spare), (0, 0), (0, spare)))
    kernel = kernel.reshape(27 * group, ins)

    packed_rows = packing(taps_out, ins, count)[3]
    factor = float(frames * count * width) ** (-0.5)
    packed = pl.pallas_call(
        functools.partial(grad_kernel, frames, group, factor),
        out_shape=jax.ShapeDtypeStruct((packed_rows, 128), jnp.bfloat16),
        in_specs=[smem(), smem()] + [copied()] * (groups + 2),
        out_specs=vmem(),
        scratch_shapes=[
            pltpu.SMEM((frames,), jnp.int32),
            pltpu.VMEM((8, 128), jnp.float32),
            pltpu.VMEM((taps_out, pixels), jnp.bfloat16),
            pltpu.VMEM((ins, pixels), jnp.bfloat16),
        ],
        compiler_params=limit(taps_out, pixels),
        cost_estimate=cost(taps_out, ins, pixels),
        name="grad_kernel",
    )(at, frame_slot, gain_line, strips, *everything)

    pieces = lax.all_to_all(
        packed.reshape(count, packed_rows // count, 128),
        "rows", split_axis=0, concat_axis=0, tiled=True,
    )

    sent = frames * group + round_up(2 * frames, 16)
    parts = pl.pallas_call(
        functools.partial(part_kernel, frames, group),
        out_shape=tuple(
            [jax.ShapeDtypeStruct((frames * (group + 2), width), jnp.float32)]
            + [jax.ShapeDtypeStruct((sent, width), jnp.bfloat16)] * (groups - 1)
        ),
        in_specs=[smem(), smem()] + [copied()] * (groups + 3),
        out_specs=(vmem(),) * groups,
        scratch_shapes=[
            pltpu.SMEM((frames,), jnp.int32),
            pltpu.VMEM((8, 128), jnp.float32),
            pltpu.VMEM((taps_out, pixels), jnp.bfloat16),
            pltpu.VMEM((ins, pixels), jnp.float32),
        ],
        compiler_params=limit(taps_out, pixels),
        cost_estimate=cost(taps_out, ins, pixels),
        name="part_kernel",
    )(at, frame_slot, gain_line, strips, kernel, *everything)

    arrived = [lax.ppermute(parts[s], "chan", partners[s]) for s in range(1, groups)]
    summed = jnp.sum(pieces.astype(jnp.float32), axis=0).astype(jnp.bfloat16)
    whole = lax.all_gather(summed, "rows", axis=0, tiled=True)
    input_adjoint, grad = pl.pallas_call(
        functools.partial(finish_kernel, frames, group),
        out_shape=(
            jax.ShapeDtypeStruct((frames, group, width), jnp.bfloat16),
            jax.ShapeDtypeStruct((taps_out, ins), jnp.float32),
        ),
        in_specs=[copied()] * (groups + 2),
        out_specs=(vmem(), vmem()),
        compiler_params=limit(taps_out, pixels),
        name="finish_kernel",
    )(whole, own, parts[0], *arrived)
    grad = grad.reshape(27, group, groups, group)[:, :channels, :, :channels]
    return (
        input_adjoint[:, :channels, None, :],
        grad.reshape(27, channels, groups * channels),
    )


def solution(mesh):
    in_specs = (
        P("rows", "chan", None, None),
        P(),
        P(None, "chan", "rows", None),
        P("chan"),
        P(None, "chan", None),
    )
    out_specs = (P(None, "chan", "rows", None), P(None, "chan", None))
    return jax.shard_map(shards, mesh=mesh, in_specs=in_specs, out_specs=out_specs, check_vma=False)
```

```python
import functools

import jax
import jax.numpy as jnp
from jax import lax
from jax.experimental import pallas as pl
from jax.experimental.pallas import tpu as pltpu
from jax.sharding import PartitionSpec as P

CHANNELS = 192
EPSILON = 1e-06
MIB = 1024 * 1024


def round_up(value, unit):
    return -(-value // unit) * unit


def packing(taps_out, ins, count):
    blocks, rest = divmod(ins, 128)
    half = round_up(-(-taps_out // 2), 16) if rest else 0
    return blocks, rest, half, round_up(blocks * taps_out + half, 16 * count)


def vmem():
    return pl.BlockSpec(memory_space=pltpu.VMEM)


def copied():
    return pl.BlockSpec()


def smem():
    return pl.BlockSpec(memory_space=pltpu.SMEM)


def limit(taps_out, pixels):
    return pltpu.CompilerParams(vmem_limit_bytes=10 * MIB + 6 * taps_out * pixels)


def cost(rows, columns, depth):
    return pl.CostEstimate(
        flops=2 * rows * columns * depth,
        bytes_accessed=2 * (rows * depth + columns * depth),
        transcendentals=columns * depth,
    )


def gains(gain_ref, line, x_refs, start, group):
    line[...] = jnp.zeros_like(line)
    line[pl.ds(0, 1), pl.ds(0, gain_ref.shape[1])] = gain_ref[...]
    found = [jnp.transpose(jnp.broadcast_to(line[pl.ds(0, 1), :], (128, 128)))[:group]]
    for ref in x_refs[1:]:
        rows = ref[pl.ds(start, 16), :].astype(jnp.float32)
        gain = rows[0:1] + rows[1:2] + rows[2:3]
        found.append(jnp.transpose(jnp.broadcast_to(gain, (128, 128)))[:group])
    return found


def norm(x_refs, t, group):
    values = [ref[pl.ds(t * group, group), :].astype(jnp.float32) for ref in x_refs]
    squares = sum(jnp.sum(value * value, axis=0, keepdims=True) for value in values)
    scale = lax.rsqrt(squares / CHANNELS + EPSILON)
    return scale, [value * scale for value in values]


def prepare_kernel(adjoint_ref, x_ref, gain_ref, strips_ref, payload_ref, lines, gain_rows):
    channels, height, width = adjoint_ref.shape
    frames = x_ref.shape[0]
    group = strips_ref.shape[2]
    lines[...] = adjoint_ref[...].astype(jnp.float32).reshape(channels * height, width)
    nothing = jnp.zeros((group, width), jnp.bfloat16)
    strips_ref[0, 0] = nothing
    strips_ref[height - 1, 2] = nothing
    for r in range(height):
        row = lines[pl.ds(r, channels, stride=height), :]
        if group > channels:
            row = jnp.concatenate(
                [row, jnp.zeros((group - channels, width), jnp.float32)], axis=0
            )
        row = row.astype(jnp.bfloat16)
        for k in range(3):
            if 0 <= r + 1 - k < height:
                strips_ref[r + 1 - k, k] = row
    for t in range(frames):
        values = x_ref[t]
        if group > channels:
            values = jnp.concatenate(
                [
                    values.astype(jnp.float32),
                    jnp.zeros((group - channels, width), jnp.float32),
                ],
                axis=0,
            ).astype(jnp.bfloat16)
        payload_ref[pl.ds(t * group, group), :] = values
    gain = gain_ref[...]
    high = gain.astype(jnp.bfloat16).astype(jnp.float32)
    middle = (gain - high).astype(jnp.bfloat16).astype(jnp.float32)
    gain_rows[...] = jnp.zeros_like(gain_rows)
    gain_rows[pl.ds(0, 1), pl.ds(0, channels)] = high
    gain_rows[pl.ds(1, 1), pl.ds(0, channels)] = middle
    gain_rows[pl.ds(2, 1), pl.ds(0, channels)] = gain - high - middle
    payload_ref[pl.ds(frames * group, 16), :] = gain_rows[...].astype(jnp.bfloat16)


def build_windows(frames, group, slot_ref, adjoint_ref, windows, place):
    width = adjoint_ref.shape[-1]
    for slot in range(frames):
        place[slot_ref[slot]] = slot

    lane = lax.broadcasted_iota(jnp.int32, (group, width), 1)
    nothing = jnp.zeros((group, width), jnp.bfloat16)
    for a in range(2):
        for inner in range(9):
            for t in range(frames - 2 + a, frames):
                windows[pl.ds((a * 9 + inner) * group, group), pl.ds(t * width, width)] = nothing
    for frame in range(frames):
        slot = place[frame]
        for b in range(3):
            row = adjoint_ref[slot, 2 - b].astype(jnp.float32)
            after = jnp.where(lane == width - 1, 0.0, pltpu.roll(row, width - 1, 1))
            before = jnp.where(lane == 0, 0.0, pltpu.roll(row, 1, 1))
            for c, shifted in enumerate((after, row, before)):
                shifted = shifted.astype(jnp.bfloat16)
                for a in range(3):
                    t = frame + a - 2
                    if t >= 0:
                        windows[
                            pl.ds((a * 9 + b * 3 + c) * group, group), pl.ds(t * width, width)
                        ] = shifted


def grad_kernel(frames, group, factor, at_ref, slot_ref, gain_ref, adjoint_ref, *refs):
    groups = len(refs) - 5
    x_refs = refs[:groups]
    grad_ref, place, line, windows, hidden = refs[groups:]
    ins = groups * group
    width = adjoint_ref.shape[-1]
    gain = gains(gain_ref, line, x_refs, frames * group, group)
    for t in range(frames):
        scale, scaled = norm(x_refs, t, group)
        for s in range(groups):
            normed = scaled[s] * gain[s]
            value = (normed * jax.nn.sigmoid(normed)).astype(jnp.bfloat16)
            start = pl.multiple_of((at_ref[0] ^ s) * group, 16)
            hidden[pl.ds(start, group), pl.ds(t * width, width)] = value

    build_windows(frames, group, slot_ref, adjoint_ref, windows, place)
    grad = lax.dot_general(
        windows[...], hidden[...], (((1,), (1,)), ((), ())), preferred_element_type=jnp.float32
    )
    grad = grad * factor
    taps_out = grad.shape[0]
    blocks, rest, half, rows = packing(taps_out, ins, 1)
    for block in range(blocks):
        grad_ref[pl.ds(block * taps_out, taps_out), :] = grad[
            :, block * 128 : block * 128 + 128
        ].astype(jnp.bfloat16)
    base = blocks * taps_out
    if rest:
        left = grad[:half, blocks * 128 :]
        right = grad[half:, blocks * 128 :]
        right = jnp.concatenate(
            [right, jnp.zeros((2 * half - taps_out, rest), jnp.float32)], axis=0
        )
        grad_ref[pl.ds(base, half), :] = jnp.concatenate([left, right], axis=1).astype(
            jnp.bfloat16
        )
        base = base + half
    tail = grad_ref.shape[0] - base
    if tail:
        grad_ref[pl.ds(base, tail), :] = jnp.zeros((tail, 128), jnp.bfloat16)


def part_kernel(frames, group, at_ref, slot_ref, gain_ref, adjoint_ref, weight_ref, *refs):
    groups = (len(refs) - 4) // 2
    x_refs = refs[:groups]
    part_refs = refs[groups : 2 * groups]
    place, line, windows, product = refs[2 * groups :]
    build_windows(frames, group, slot_ref, adjoint_ref, windows, place)
    width = part_refs[0].shape[-1]
    product[...] = lax.dot_general(
        weight_ref[...], windows[...], (((0,), (0,)), ((), ())), preferred_element_type=jnp.float32
    )
    gain = gains(gain_ref, line, x_refs, frames * group, group)
    shares = []
    for t in range(frames):
        scale, scaled = norm(x_refs, t, group)
        part_refs[0][pl.ds(frames * group + t, 1), :] = scale
        share = jnp.zeros((1, width), jnp.float32)
        for s in range(groups):
            normed = scaled[s] * gain[s]
            sigma = jax.nn.sigmoid(normed)
            slope = sigma * (1.0 + normed * (1.0 - sigma)) * gain[s]
            start = pl.multiple_of((at_ref[0] ^ s) * group, 16)
            term = product[pl.ds(start, group), pl.ds(t * width, width)] * slope * scale
            part_refs[s][pl.ds(t * group, group), :] = term.astype(part_refs[s].dtype)
            share = share + jnp.sum(term * scaled[s], axis=0, keepdims=True)
        shares.append(share)
    share = jnp.concatenate(shares, axis=0)
    part_refs[0][pl.ds(frames * group + frames, frames), :] = share
    high = share.astype(jnp.bfloat16).astype(jnp.float32)
    both = [high, share - high]
    unused = round_up(2 * frames, 16) - 2 * frames
    if unused:
        both.append(jnp.zeros((unused, width), jnp.float32))
    both = jnp.concatenate(both, axis=0).astype(jnp.bfloat16)
    for s in range(1, groups):
        part_refs[s][pl.ds(frames * group, both.shape[0]), :] = both


def finish_kernel(frames, group, packed_ref, x_ref, *refs):
    own_ref, others, (out_ref, grad_ref) = refs[0], refs[1:-2], refs[-2:]
    taps_out, ins = grad_ref.shape
    blocks, rest, half, rows = packing(taps_out, ins, 1)
    for block in range(blocks):
        grad_ref[:, pl.ds(block * 128, 128)] = packed_ref[
            pl.ds(block * taps_out, taps_out), :
        ].astype(jnp.float32)
    if rest:
        both = packed_ref[pl.ds(blocks * taps_out, half), :].astype(jnp.float32)
        grad_ref[pl.ds(0, half), pl.ds(blocks * 128, rest)] = both[:, :rest]
        grad_ref[pl.ds(half, taps_out - half), pl.ds(blocks * 128, rest)] = both[
            : taps_out - half, rest:
        ]

    share = own_ref[pl.ds(frames * group + frames, frames), :]
    for ref in others:
        both = ref[pl.ds(frames * group, round_up(2 * frames, 16)), :].astype(jnp.float32)
        share = share + both[:frames] + both[frames : 2 * frames]
    share = share / CHANNELS
    for t in range(frames):
        term = own_ref[pl.ds(t * group, group), :]
        for ref in others:
            term = term + ref[pl.ds(t * group, group), :].astype(jnp.float32)
        scale = own_ref[pl.ds(frames * group + t, 1), :]
        scaled = x_ref[pl.ds(t * group, group), :].astype(jnp.float32) * scale
        out_ref[t] = (term - scaled * share[t : t + 1]).astype(jnp.bfloat16)


def shards(frame_adjoint, frame_slot, inputs, gain, weight):
    count = lax.axis_size("rows")
    groups = lax.axis_size("chan")
    frames, channels, _, width = inputs.shape
    group = round_up(channels, 16)
    spare = group - channels
    ins = groups * group

    taps_out = 27 * group
    pixels = frames * width
    strips, payload = pl.pallas_call(
        prepare_kernel,
        out_shape=(
            jax.ShapeDtypeStruct((count, 3, group, width), jnp.bfloat16),
            jax.ShapeDtypeStruct((frames * group + 16, width), jnp.bfloat16),
        ),
        in_specs=[copied(), copied(), copied()],
        out_specs=(vmem(), vmem()),
        scratch_shapes=[
            pltpu.VMEM((channels * count, width), jnp.float32),
            pltpu.VMEM((16, width), jnp.float32),
        ],
        compiler_params=pltpu.CompilerParams(vmem_limit_bytes=60 * MIB),
        name="prepare_kernel",
    )(frame_adjoint[0], inputs[:, :, 0], gain.reshape(1, channels))
    partners = [[(z, z ^ s) for z in range(groups)] for s in range(groups)]
    own = jnp.pad(inputs[:, :, 0], ((0, 0), (0, spare), (0, 0))).reshape(frames * group, width)
    gain_line = gain.reshape(1, channels)
    everything = [own] + [
        lax.ppermute(payload, "chan", partners[s]) for s in range(1, groups)
    ]
    strips = lax.cond(
        lax.axis_index("rows") < count,
        lambda rows: lax.all_to_all(rows, "rows", split_axis=0, concat_axis=0, tiled=True),
        lambda rows: rows,
        strips,
    )
    at = lax.axis_index("chan").astype(jnp.int32).reshape(1)

    kernel = weight.reshape(27, channels, groups, channels)
    kernel = jnp.pad(kernel, ((0, 0), (0, spare), (0, 0), (0, spare)))
    kernel = kernel.reshape(27 * group, ins)

    packed_rows = packing(taps_out, ins, count)[3]
    factor = float(frames * count * width) ** (-0.5)
    packed = pl.pallas_call(
        functools.partial(grad_kernel, frames, group, factor),
        out_shape=jax.ShapeDtypeStruct((packed_rows, 128), jnp.bfloat16),
        in_specs=[smem(), smem()] + [copied()] * (groups + 2),
        out_specs=vmem(),
        scratch_shapes=[
            pltpu.SMEM((frames,), jnp.int32),
            pltpu.VMEM((8, 128), jnp.float32),
            pltpu.VMEM((taps_out, pixels), jnp.bfloat16),
            pltpu.VMEM((ins, pixels), jnp.bfloat16),
        ],
        compiler_params=limit(taps_out, pixels),
        cost_estimate=cost(taps_out, ins, pixels),
        name="grad_kernel",
    )(at, frame_slot, gain_line, strips, *everything)

    pieces = lax.all_to_all(
        packed.reshape(count, packed_rows // count, 128),
        "rows", split_axis=0, concat_axis=0, tiled=True,
    )

    sent = frames * group + round_up(2 * frames, 16)
    parts = pl.pallas_call(
        functools.partial(part_kernel, frames, group),
        out_shape=tuple(
            [jax.ShapeDtypeStruct((frames * (group + 2), width), jnp.float32)]
            + [jax.ShapeDtypeStruct((sent, width), jnp.bfloat16)] * (groups - 1)
        ),
        in_specs=[smem(), smem()] + [copied()] * (groups + 3),
        out_specs=(vmem(),) * groups,
        scratch_shapes=[
            pltpu.SMEM((frames,), jnp.int32),
            pltpu.VMEM((8, 128), jnp.float32),
            pltpu.VMEM((taps_out, pixels), jnp.bfloat16),
            pltpu.VMEM((ins, pixels), jnp.float32),
        ],
        compiler_params=limit(taps_out, pixels),
        cost_estimate=cost(taps_out, ins, pixels),
        name="part_kernel",
    )(at, frame_slot, gain_line, strips, kernel, *everything)

    arrived = [lax.ppermute(parts[s], "chan", partners[s]) for s in range(1, groups)]
    summed = jnp.sum(pieces.astype(jnp.float32), axis=0).astype(jnp.bfloat16)
    whole = lax.all_gather(summed, "rows", axis=0, tiled=True)
    input_adjoint, grad = pl.pallas_call(
        functools.partial(finish_kernel, frames, group),
        out_shape=(
            jax.ShapeDtypeStruct((frames, group, width), jnp.bfloat16),
            jax.ShapeDtypeStruct((taps_out, ins), jnp.float32),
        ),
        in_specs=[copied()] * (groups + 2),
        out_specs=(vmem(), vmem()),
        compiler_params=limit(taps_out, pixels),
        name="finish_kernel",
    )(whole, own, parts[0], *arrived)
    grad = grad.reshape(27, group, groups, group)[:, :channels, :, :channels]
    return (
        input_adjoint[:, :channels, None, :],
        grad.reshape(27, channels, groups * channels),
    )


def solution(mesh):
    in_specs = (
        P("rows", "chan", None, None),
        P(),
        P(None, "chan", "rows", None),
        P("chan"),
        P(None, "chan", None),
    )
    out_specs = (P(None, "chan", "rows", None), P(None, "chan", None))
    return jax.shard_map(shards, mesh=mesh, in_specs=in_specs, out_specs=out_specs, check_vma=False)
```

```python
import functools

import jax
import jax.numpy as jnp
from jax import lax
from jax.experimental import pallas as pl
from jax.experimental.pallas import tpu as pltpu
from jax.sharding import PartitionSpec as P

CHANNELS = 192
EPSILON = 1e-06
MIB = 1024 * 1024


def round_up(value, unit):
    return -(-value // unit) * unit


def packing(taps_out, ins, count):
    blocks, rest = divmod(ins, 128)
    half = round_up(-(-taps_out // 2), 16) if rest else 0
    return blocks, rest, half, round_up(blocks * taps_out + half, 16 * count)


def vmem():
    return pl.BlockSpec(memory_space=pltpu.VMEM)


def copied():
    return pl.BlockSpec()


def smem():
    return pl.BlockSpec(memory_space=pltpu.SMEM)


def limit(taps_out, pixels):
    return pltpu.CompilerParams(vmem_limit_bytes=10 * MIB + 6 * taps_out * pixels)


def cost(rows, columns, depth):
    return pl.CostEstimate(
        flops=2 * rows * columns * depth,
        bytes_accessed=2 * (rows * depth + columns * depth),
        transcendentals=columns * depth,
    )


def gains(gain_ref, line, x_refs, start, group):
    line[...] = jnp.zeros_like(line)
    line[pl.ds(0, 1), pl.ds(0, gain_ref.shape[1])] = gain_ref[...]
    found = [jnp.transpose(jnp.broadcast_to(line[pl.ds(0, 1), :], (128, 128)))[:group]]
    for ref in x_refs[1:]:
        rows = ref[pl.ds(start, 16), :].astype(jnp.float32)
        gain = rows[0:1] + rows[1:2] + rows[2:3]
        found.append(jnp.transpose(jnp.broadcast_to(gain, (128, 128)))[:group])
    return found


def norm(x_refs, t, group):
    values = [ref[pl.ds(t * group, group), :].astype(jnp.float32) for ref in x_refs]
    squares = sum(jnp.sum(value * value, axis=0, keepdims=True) for value in values)
    scale = lax.rsqrt(squares / CHANNELS + EPSILON)
    return scale, [value * scale for value in values]


def prepare_kernel(adjoint_ref, x_ref, gain_ref, strips_ref, payload_ref, lines, gain_rows):
    channels, height, width = adjoint_ref.shape
    frames = x_ref.shape[0]
    group = strips_ref.shape[2]
    lines[...] = adjoint_ref[...].astype(jnp.float32).reshape(channels * height, width)
    nothing = jnp.zeros((group, width), jnp.bfloat16)
    strips_ref[0, 0] = nothing
    strips_ref[height - 1, 2] = nothing
    for r in range(height):
        row = lines[pl.ds(r, channels, stride=height), :]
        if group > channels:
            row = jnp.concatenate(
                [row, jnp.zeros((group - channels, width), jnp.float32)], axis=0
            )
        row = row.astype(jnp.bfloat16)
        for k in range(3):
            if 0 <= r + 1 - k < height:
                strips_ref[r + 1 - k, k] = row
    for t in range(frames):
        values = x_ref[t]
        if group > channels:
            values = jnp.concatenate(
                [
                    values.astype(jnp.float32),
                    jnp.zeros((group - channels, width), jnp.float32),
                ],
                axis=0,
            ).astype(jnp.bfloat16)
        payload_ref[pl.ds(t * group, group), :] = values
    gain = gain_ref[...]
    high = gain.astype(jnp.bfloat16).astype(jnp.float32)
    middle = (gain - high).astype(jnp.bfloat16).astype(jnp.float32)
    gain_rows[...] = jnp.zeros_like(gain_rows)
    gain_rows[pl.ds(0, 1), pl.ds(0, channels)] = high
    gain_rows[pl.ds(1, 1), pl.ds(0, channels)] = middle
    gain_rows[pl.ds(2, 1), pl.ds(0, channels)] = gain - high - middle
    payload_ref[pl.ds(frames * group, 16), :] = gain_rows[...].astype(jnp.bfloat16)


def build_windows(frames, group, slot_ref, adjoint_ref, windows, place):
    width = adjoint_ref.shape[-1]
    for slot in range(frames):
        place[slot_ref[slot]] = slot

    lane = lax.broadcasted_iota(jnp.int32, (group, width), 1)
    nothing = jnp.zeros((group, width), jnp.bfloat16)
    for a in range(2):
        for inner in range(9):
            for t in range(frames - 2 + a, frames):
                windows[pl.ds((a * 9 + inner) * group, group), pl.ds(t * width, width)] = nothing
    for frame in range(frames):
        slot = place[frame]
        for b in range(3):
            row = adjoint_ref[slot, 2 - b].astype(jnp.float32)
            after = jnp.where(lane == width - 1, 0.0, pltpu.roll(row, width - 1, 1))
            before = jnp.where(lane == 0, 0.0, pltpu.roll(row, 1, 1))
            for c, shifted in enumerate((after, row, before)):
                shifted = shifted.astype(jnp.bfloat16)
                for a in range(3):
                    t = frame + a - 2
                    if t >= 0:
                        windows[
                            pl.ds((a * 9 + b * 3 + c) * group, group), pl.ds(t * width, width)
                        ] = shifted


def grad_kernel(frames, group, factor, at_ref, slot_ref, gain_ref, adjoint_ref, *refs):
    groups = len(refs) - 7
    x_refs = refs[:groups]
    grad_ref, place, line, windows, hidden, packed, moved = refs[groups:]
    ins = groups * group
    width = adjoint_ref.shape[-1]
    build_windows(frames, group, slot_ref, adjoint_ref, windows, place)
    gain = gains(gain_ref, line, x_refs, frames * group, group)
    for t in range(frames):
        scale, scaled = norm(x_refs, t, group)
        for s in range(groups):
            normed = scaled[s] * gain[s]
            value = (normed * jax.nn.sigmoid(normed)).astype(jnp.bfloat16)
            start = pl.multiple_of((at_ref[0] ^ s) * group, 16)
            hidden[pl.ds(start, group), pl.ds(t * width, width)] = value

    taps_out = windows.shape[0]
    blocks, rest, half, rows = packing(taps_out, ins, 1)
    part = taps_out // 3
    base = blocks * taps_out
    leaving = []
    if packed.shape[0] > base + half:
        tail = packed.shape[0] - base - half
        packed[pl.ds(base + half, tail), :] = jnp.zeros((tail, 128), jnp.bfloat16)
    if rest:
        packed[pl.ds(base, half), :] = jnp.zeros((half, 128), jnp.bfloat16)
    for p in range(3):
        first = p * part
        grad = factor * lax.dot_general(
            windows[pl.ds(first, part), :], hidden[...], (((1,), (1,)), ((), ())),
            preferred_element_type=jnp.float32,
        )
        for block in range(blocks):
            span = pl.ds(block * taps_out + first, part)
            packed[span, :] = grad[:, block * 128 : block * 128 + 128].astype(jnp.bfloat16)
            leaving.append((span, len(leaving)))
            pltpu.make_async_copy(packed.at[span], grad_ref.at[span], moved.at[len(leaving) - 1]).start()
        if rest:
            for begin, end, low in ((0, half, 0), (half, taps_out, rest)):
                begin, end = max(begin, first), min(end, first + part)
                if begin < end:
                    shift = half if low else 0
                    packed[pl.ds(base + begin - shift, end - begin), pl.ds(low, rest)] = grad[
                        begin - first : end - first, blocks * 128 :
                    ].astype(jnp.bfloat16)
    span = pl.ds(base, packed.shape[0] - base)
    if packed.shape[0] > base:
        leaving.append((span, len(leaving)))
        pltpu.make_async_copy(packed.at[span], grad_ref.at[span], moved.at[len(leaving) - 1]).start()
    for span, k in leaving:
        pltpu.make_async_copy(packed.at[span], grad_ref.at[span], moved.at[k]).wait()


def part_kernel(frames, group, at_ref, slot_ref, gain_ref, adjoint_ref, weight_ref, *refs):
    groups = (len(refs) - 4) // 2
    x_refs = refs[:groups]
    part_refs = refs[groups : 2 * groups]
    place, line, windows, product = refs[2 * groups :]
    build_windows(frames, group, slot_ref, adjoint_ref, windows, place)
    width = part_refs[0].shape[-1]
    product[...] = lax.dot_general(
        weight_ref[...], windows[...], (((0,), (0,)), ((), ())), preferred_element_type=jnp.float32
    )
    gain = gains(gain_ref, line, x_refs, frames * group, group)
    shares = []
    for t in range(frames):
        scale, scaled = norm(x_refs, t, group)
        part_refs[0][pl.ds(frames * group + t, 1), :] = scale
        share = jnp.zeros((1, width), jnp.float32)
        for s in range(groups):
            normed = scaled[s] * gain[s]
            sigma = jax.nn.sigmoid(normed)
            slope = sigma * (1.0 + normed * (1.0 - sigma)) * gain[s]
            start = pl.multiple_of((at_ref[0] ^ s) * group, 16)
            term = product[pl.ds(start, group), pl.ds(t * width, width)] * slope * scale
            part_refs[s][pl.ds(t * group, group), :] = term.astype(part_refs[s].dtype)
            share = share + jnp.sum(term * scaled[s], axis=0, keepdims=True)
        shares.append(share)
    share = jnp.concatenate(shares, axis=0)
    part_refs[0][pl.ds(frames * group + frames, frames), :] = share
    high = share.astype(jnp.bfloat16).astype(jnp.float32)
    both = [high, share - high]
    unused = round_up(2 * frames, 16) - 2 * frames
    if unused:
        both.append(jnp.zeros((unused, width), jnp.float32))
    both = jnp.concatenate(both, axis=0).astype(jnp.bfloat16)
    for s in range(1, groups):
        part_refs[s][pl.ds(frames * group, both.shape[0]), :] = both


def finish_kernel(frames, group, packed_ref, x_ref, *refs):
    own_ref, others, (out_ref, grad_ref) = refs[0], refs[1:-2], refs[-2:]
    taps_out, ins = grad_ref.shape
    blocks, rest, half, rows = packing(taps_out, ins, 1)
    for block in range(blocks):
        grad_ref[:, pl.ds(block * 128, 128)] = packed_ref[
            pl.ds(block * taps_out, taps_out), :
        ].astype(jnp.float32)
    if rest:
        both = packed_ref[pl.ds(blocks * taps_out, half), :].astype(jnp.float32)
        grad_ref[pl.ds(0, half), pl.ds(blocks * 128, rest)] = both[:, :rest]
        grad_ref[pl.ds(half, taps_out - half), pl.ds(blocks * 128, rest)] = both[
            : taps_out - half, rest:
        ]

    share = own_ref[pl.ds(frames * group + frames, frames), :]
    for ref in others:
        both = ref[pl.ds(frames * group, round_up(2 * frames, 16)), :].astype(jnp.float32)
        share = share + both[:frames] + both[frames : 2 * frames]
    share = share / CHANNELS
    for t in range(frames):
        term = own_ref[pl.ds(t * group, group), :]
        for ref in others:
            term = term + ref[pl.ds(t * group, group), :].astype(jnp.float32)
        scale = own_ref[pl.ds(frames * group + t, 1), :]
        scaled = x_ref[pl.ds(t * group, group), :].astype(jnp.float32) * scale
        out_ref[t] = (term - scaled * share[t : t + 1]).astype(jnp.bfloat16)


def shards(frame_adjoint, frame_slot, inputs, gain, weight):
    count = lax.axis_size("rows")
    groups = lax.axis_size("chan")
    frames, channels, _, width = inputs.shape
    group = round_up(channels, 16)
    spare = group - channels
    ins = groups * group

    taps_out = 27 * group
    pixels = frames * width
    strips, payload = pl.pallas_call(
        prepare_kernel,
        out_shape=(
            jax.ShapeDtypeStruct((count, 3, group, width), jnp.bfloat16),
            jax.ShapeDtypeStruct((frames * group + 16, width), jnp.bfloat16),
        ),
        in_specs=[copied(), copied(), copied()],
        out_specs=(vmem(), vmem()),
        scratch_shapes=[
            pltpu.VMEM((channels * count, width), jnp.float32),
            pltpu.VMEM((16, width), jnp.float32),
        ],
        compiler_params=pltpu.CompilerParams(vmem_limit_bytes=60 * MIB),
        name="prepare_kernel",
    )(frame_adjoint[0], inputs[:, :, 0], gain.reshape(1, channels))
    partners = [[(z, z ^ s) for z in range(groups)] for s in range(groups)]
    own = jnp.pad(inputs[:, :, 0], ((0, 0), (0, spare), (0, 0))).reshape(frames * group, width)
    gain_line = gain.reshape(1, channels)
    everything = [own] + [
        lax.ppermute(payload, "chan", partners[s]) for s in range(1, groups)
    ]
    strips = lax.cond(
        lax.axis_index("rows") < count,
        lambda rows: lax.all_to_all(rows, "rows", split_axis=0, concat_axis=0, tiled=True),
        lambda rows: rows,
        strips,
    )
    at = lax.axis_index("chan").astype(jnp.int32).reshape(1)

    kernel = weight.reshape(27, channels, groups, channels)
    kernel = jnp.pad(kernel, ((0, 0), (0, spare), (0, 0), (0, spare)))
    kernel = kernel.reshape(27 * group, ins)

    packed_rows = packing(taps_out, ins, count)[3]
    factor = float(frames * count * width) ** (-0.5)
    packed = pl.pallas_call(
        functools.partial(grad_kernel, frames, group, factor),
        out_shape=jax.ShapeDtypeStruct((packed_rows, 128), jnp.bfloat16),
        in_specs=[smem(), smem()] + [copied()] * (groups + 2),
        out_specs=pl.BlockSpec(memory_space=pl.ANY),
        scratch_shapes=[
            pltpu.SMEM((frames,), jnp.int32),
            pltpu.VMEM((8, 128), jnp.float32),
            pltpu.VMEM((taps_out, pixels), jnp.bfloat16),
            pltpu.VMEM((ins, pixels), jnp.bfloat16),
            pltpu.VMEM((packed_rows, 128), jnp.bfloat16),
            pltpu.SemaphoreType.DMA((3 * (ins // 128) + 1,)),
        ],
        compiler_params=limit(taps_out, pixels),
        cost_estimate=cost(taps_out, ins, pixels),
        name="grad_kernel",
    )(at, frame_slot, gain_line, strips, *everything)

    pieces = lax.all_to_all(
        packed.reshape(count, packed_rows // count, 128),
        "rows", split_axis=0, concat_axis=0, tiled=True,
    )

    sent = frames * group + round_up(2 * frames, 16)
    parts = pl.pallas_call(
        functools.partial(part_kernel, frames, group),
        out_shape=tuple(
            [jax.ShapeDtypeStruct((frames * (group + 2), width), jnp.float32)]
            + [jax.ShapeDtypeStruct((sent, width), jnp.bfloat16)] * (groups - 1)
        ),
        in_specs=[smem(), smem()] + [copied()] * (groups + 3),
        out_specs=(vmem(),) * groups,
        scratch_shapes=[
            pltpu.SMEM((frames,), jnp.int32),
            pltpu.VMEM((8, 128), jnp.float32),
            pltpu.VMEM((taps_out, pixels), jnp.bfloat16),
            pltpu.VMEM((ins, pixels), jnp.float32),
        ],
        compiler_params=limit(taps_out, pixels),
        cost_estimate=cost(taps_out, ins, pixels),
        name="part_kernel",
    )(at, frame_slot, gain_line, strips, kernel, *everything)

    arrived = [lax.ppermute(parts[s], "chan", partners[s]) for s in range(1, groups)]
    summed = jnp.sum(pieces.astype(jnp.float32), axis=0).astype(jnp.bfloat16)
    whole = lax.all_gather(summed, "rows", axis=0, tiled=True)
    input_adjoint, grad = pl.pallas_call(
        functools.partial(finish_kernel, frames, group),
        out_shape=(
            jax.ShapeDtypeStruct((frames, group, width), jnp.bfloat16),
            jax.ShapeDtypeStruct((taps_out, ins), jnp.float32),
        ),
        in_specs=[copied()] * (groups + 2),
        out_specs=(vmem(), vmem()),
        compiler_params=limit(taps_out, pixels),
        name="finish_kernel",
    )(whole, own, parts[0], *arrived)
    grad = grad.reshape(27, group, groups, group)[:, :channels, :, :channels]
    return (
        input_adjoint[:, :channels, None, :],
        grad.reshape(27, channels, groups * channels),
    )


def solution(mesh):
    in_specs = (
        P("rows", "chan", None, None),
        P(),
        P(None, "chan", "rows", None),
        P("chan"),
        P(None, "chan", None),
    )
    out_specs = (P(None, "chan", "rows", None), P(None, "chan", None))
    return jax.shard_map(shards, mesh=mesh, in_specs=in_specs, out_specs=out_specs, check_vma=False)
```
